256 devices in a mesh: slab: 64 (over x, y, z_lo, core), pencil: 4 (over z_hi).
Axes of the slice: x: 4, y: 4, z: 8 (z_hi: 4, z_lo: 2; z = z_hi * 2 + z_lo), core: 2. Of those that a mesh axis runs over, the one named last changes fastest.
Arguments:
- volume: bfloat16 [4, 256, 64, 256], P(None, 'slab', 'pencil'), may hold values from -6 to 6
- weight_one: bfloat16 [32, 27, 4], replicated, may hold values from -0.625 to 0.625
- weight_two: bfloat16 [64, 27, 32], replicated, may hold values from -0.21875 to 0.21875
- cotangent: bfloat16 [64, 64, 16, 64], P(None, 'slab', 'pencil'), may hold values from -0.18164062 to 0.18164062
Outputs:
- pooled_two: bfloat16 [64, 64, 16, 64], P(None, 'slab', 'pencil')
- grad_one: float32 [32, 27, 4], replicated
- grad_two: float32 [64, 27, 32], P('pencil')
The draws below stay inside these ranges and needn't reach their ends.
All inputs are finite; a program needn't handle non-finite values.
Results may differ from the reference program's by a relative error of at most 0.019.
Values may be sent and summed in bfloat16 or wider, within the bound.
A program may use at most 64 MiB of HBM per device.

```python
import jax
import jax.numpy as jnp
from jax import lax

C0 = 4
C1 = 32
C2 = 64
ZW = 256
NX = 256
NY = 64


def block_levels(stream_key, shape, cuts, low, largest):
    def one(dim, shards_of):
        steps = jax.random.uniform(jax.random.fold_in(jax.random.fold_in(stream_key, 6), dim), (shards_of,), jnp.float32, low / len(cuts), largest / len(cuts))
        return jnp.repeat(jnp.exp(steps), shape[dim] // shards_of).reshape((-1,) + (1,) * (len(shape) - dim - 1))

    factor_of = one(*cuts[0])
    for cut in cuts[1:]:
        factor_of = factor_of * one(*cut)
    return factor_of


def bell_draw(rng, shape, scale, limit, split=(), kind=jnp.bfloat16):
    values = scale * jax.random.normal(rng, shape, jnp.float32)
    if split:
        values = values * block_levels(rng, shape, split, -0.22, 0.18)
    return jnp.clip(values, -limit, limit).astype(kind)


def setup_inputs(seed: int = 0) -> dict:
    arg_keys = jax.random.split(jax.random.key(seed), 5)
    return {
        "volume": bell_draw(arg_keys[0], (C0, NX, NY, ZW), 1.0, 6.0, ((1, 64), (2, 4))),
        "weight_one": bell_draw(arg_keys[1], (C1, 27, C0), (27 * C0) ** -0.5, 0.625),
        "weight_two": bell_draw(arg_keys[2], (C2, 27, C1), (27 * C1) ** -0.5, 0.21875),
        "cotangent": bell_draw(arg_keys[3], (C2, NX // 4, NY // 4, ZW // 4), (22.0 / (NX * NY * ZW // 8) ** 0.5), 0.18164062, ((1, 64), (2, 4))),
    }


def conv_full(field, weight):
    outs = weight.shape[0]
    chans = weight.shape[2]
    kernel = weight.reshape(outs, 3, 3, 3, chans).transpose(0, 4, 1, 2, 3)
    result = lax.conv_general_dilated(field[None], kernel, (1, 1, 1), ((1, 1), (1, 1), (1, 1)), dimension_numbers=('NCDHW', 'OIDHW', 'NCDHW'), precision=lax.Precision.HIGHEST)
    return result[0]

def act_fn(value):
    return 0.3 * value + 0.7 * jax.nn.softplus(value)

def slope_fn(value):
    return 0.3 + 0.7 * jax.nn.sigmoid(value)

def pool_fn(field):
    c, x, y, z = field.shape
    return field.reshape(c, x // 2, 2, y // 2, 2, z // 2, 2).mean(axis=(2, 4, 6))

def spread_fn(field):
    wide = jnp.repeat(jnp.repeat(jnp.repeat(field, 2, axis=1), 2, axis=2), 2, axis=3)
    return wide * 0.125

def reference(volume, weight_one, weight_two, cotangent):
    vol = volume.astype(jnp.float32)
    w_one = weight_one.astype(jnp.float32)
    w_two = weight_two.astype(jnp.float32)
    pre_one = conv_full(vol, w_one)
    pooled_one = pool_fn(act_fn(pre_one)).astype(jnp.bfloat16)
    pre_two, pull_two = jax.vjp(lambda w, v: conv_full(v, w), w_two, pooled_one.astype(jnp.float32))
    pooled_two = pool_fn(act_fn(pre_two)).astype(jnp.bfloat16)
    grad_pre_two = (slope_fn(pre_two) * spread_fn(cotangent.astype(jnp.float32))).astype(jnp.bfloat16)
    grad_two, grad_pooled = pull_two(grad_pre_two.astype(jnp.float32))
    grad_pre_one = (slope_fn(pre_one) * spread_fn(grad_pooled)).astype(jnp.bfloat16)
    _, pull_one = jax.vjp(lambda w: conv_full(vol, w), w_one)
    grad_one = pull_one(grad_pre_one.astype(jnp.float32))[0]
    return (pooled_two, grad_one, grad_two)
```

```python
import functools

import jax
import jax.numpy as jnp
from jax import lax
from jax.experimental import pallas as pl
from jax.experimental.pallas import tpu as pltpu
from jax.sharding import PartitionSpec as P

MESH = pl.DeviceIdType.MESH
F32 = jnp.float32
BF16 = jnp.bfloat16
SIDES = ((1, 0), (-1, 0), (0, 1), (0, -1), (1, 1), (1, -1), (-1, 1), (-1, -1))


def pick(rows, cols, hit):
    r = lax.broadcasted_iota(jnp.int32, (rows, cols), 0)
    c = lax.broadcasted_iota(jnp.int32, (rows, cols), 1)
    return jnp.where(hit(r, c), 1.0, 0.0).astype(BF16)


def dot(a, b):
    return jnp.dot(a, b, preferred_element_type=F32)


def dot_lanes(a, b):
    return lax.dot_general(a, b, (((1,), (1,)), ((), ())), preferred_element_type=F32)


def split(value, count):
    parts = []
    for _ in range(count):
        part = value.astype(BF16)
        parts.append(part)
        value = value - part.astype(F32)
    return parts


def dot_split(value, b, count=2):
    total = None
    for part in split(value, count):
        term = dot(part, b)
        total = term if total is None else total + term
    return total


def act_slope(pre):
    t = jnp.tanh(0.5 * pre)
    act = 0.3 * pre + 0.7 * (jnp.maximum(pre, 0.0) - jnp.log(0.5 + 0.5 * jnp.abs(t)))
    return act, 0.65 + 0.35 * t


def expand_map(xo, yo):
    def hit(r, j):
        a = (j >> 6) - xo
        b = ((j >> 4) & 3) - yo
        slot = j & 15
        ok = (a >= 0) & (a < 3) & (b >= 0) & (b < 3) & (slot < 12)
        return ok & (r == 36 * a + 12 * b + slot)

    return pick(128, 256, hit)


def kernel(
    stages,
    vol,
    w1f,
    w2a,
    w2b,
    cot,
    p2_out,
    g1_out,
    g2_out,
    V,
    PS,
    GS,
    SL,
    ypack,
    xrecv,
    yrecv,
    crecv,
    dw1,
    dw2,
    rs_send,
    rs_recv,
    ar1,
    ar2,
    halo_send,
    halo_recv,
    sem_rs,
    sem_ar1,
    sem_ar2,
):
    slab = lax.axis_index("slab")
    pencil = lax.axis_index("pencil")
    slabs = lax.axis_size("slab")
    pencils = lax.axis_size("pencil")

    def exists(dx, dy):
        x = slab + dx
        y = pencil + dy
        ok = None
        if dx:
            ok = (x >= 0) & (x < slabs)
        if dy:
            oky = (y >= 0) & (y < pencils)
            ok = oky if ok is None else ok & oky
        return ok

    def place(stage):
        axis, size, stride = stages[stage]
        if axis == "pencil":
            return size, pencil, lambda i: (slab, i)
        me = lax.rem(slab // stride, size)
        return size, me, lambda i: (slab + (i - me) * stride, pencil)

    xrecv[...] = jnp.zeros_like(xrecv)
    yrecv[...] = jnp.zeros_like(yrecv)
    crecv[...] = jnp.zeros_like(crecv)
    for field in (PS, GS):
        edge = field.shape[2:]
        for x in (0, 3):
            field[x] = jnp.zeros(field.shape[1:], BF16)
        for y in (0, 9):
            field[1:3, y] = jnp.zeros((2,) + edge, BF16)

    barrier = pltpu.get_barrier_semaphore()
    arrivals = 0
    for dx, dy in SIDES:
        ok = exists(dx, dy)
        arrivals = arrivals + ok.astype(jnp.int32)

        @pl.when(ok)
        def _():
            pl.semaphore_signal(
                barrier, inc=1, device_id=(slab + dx, pencil + dy), device_id_type=MESH
            )

    for stage in range(len(stages)):
        size, me, device = place(stage)
        arrivals = arrivals + (size - 1)
        for d in range(1, size):
            pl.semaphore_signal(
                barrier, inc=1, device_id=device(lax.rem(me + d, size)), device_id_type=MESH
            )

    edges = pick(32, 256, lambda r, c: c == ((r & 15) << 4) + 15 * (r >> 4))
    packed = dot(edges, vol[...].reshape(256, 256)).astype(BF16)
    ypack[0] = packed[:16]
    ypack[1] = packed[16:]
    pl.semaphore_wait(barrier, arrivals)

    def halo_copy(phase, k, refs):
        dx, dy = SIDES[k]
        src, dst = refs(dx, dy)
        return pltpu.make_async_remote_copy(
            src_ref=src,
            dst_ref=dst,
            send_sem=halo_send.at[phase, k],
            recv_sem=halo_recv.at[phase, k],
            device_id=(slab + dx, pencil + dy),
            device_id_type=MESH,
        )

    def halo_start(phase, refs):
        for k, (dx, dy) in enumerate(SIDES):

            @pl.when(exists(dx, dy))
            def _():
                halo_copy(phase, k, refs).start()

    def halo_wait(phase, refs):
        for k, (dx, dy) in enumerate(SIDES):

            @pl.when(exists(dx, dy))
            def _():
                halo_copy(phase, k, refs).wait_send()

            @pl.when(exists(-dx, -dy))
            def _():
                halo_copy(phase, k, refs).wait_recv()

    def volume_refs(dx, dy):
        if dy == 0:
            return vol.at[:, 3 if dx == 1 else 0], xrecv.at[0 if dx == 1 else 1]
        src = ypack.at[1 if dy == 1 else 0]
        side = 0 if dy == 1 else 1
        if dx == 0:
            return src, yrecv.at[side]
        return src, crecv.at[2 * (0 if dx == 1 else 1) + side]

    def field_refs(field, lo, hi, dx, dy):
        sx = {1: 2, -1: 1, 0: pl.ds(1, 2)}[dx]
        tx = {1: 0, -1: 3, 0: pl.ds(1, 2)}[dx]
        sy = {1: 8, -1: 1, 0: pl.ds(1, 8)}[dy]
        ty = {1: 0, -1: 9, 0: pl.ds(1, 8)}[dy]
        rows = pl.ds(lo, hi - lo)
        return field.at[sx, sy, rows], field.at[tx, ty, rows]

    halo_start(0, volume_refs)

    shift_1 = pick(256, 512, lambda r, c: r == jnp.where(c < 256, c - 1, c - 255))
    shift_2 = pick(128, 256, lambda r, c: r == jnp.where(c < 128, c - 1, c - 127))

    def shifted(block):
        sides = dot(block, shift_1).astype(BF16)
        return jnp.concatenate([sides[:, :256], block, sides[:, 256:]], axis=0)

    def order(r, c):
        slot = r & 15
        return (slot < 12) & (c == ((slot >> 2) << 6) + ((slot & 3) << 4) + (r >> 4))

    def order_edge(r, c):
        slot = r & 15
        return (slot < 12) & (c == ((slot >> 2) << 4) + ((slot & 3) << 2) + (r >> 4))

    to_rows = pick(256, 192, order)
    to_edge = pick(64, 48, order_edge)

    def fill(x, block):
        rows = dot(to_rows, shifted(block.reshape(64, 256))).astype(BF16)
        V[x, 1:17] = rows.reshape(16, 16, 256)

    def edge_rows(block):
        return dot(to_edge, shifted(block)).astype(BF16).reshape(4, 16, 256)

    for x in range(4):
        fill(x + 1, vol[:, x])

    w1e = jnp.concatenate(
        [dot(w1f[...], expand_map(xo, yo)).astype(BF16) for xo in range(2) for yo in range(2)],
        axis=0,
    )

    halo_wait(0, volume_refs)
    fill(0, xrecv[0])
    fill(5, xrecv[1])
    for side, y in ((0, 0), (1, 17)):
        V[1:5, y] = edge_rows(yrecv[side])
        V[0, y] = edge_rows(crecv[side])[3]
        V[5, y] = edge_rows(crecv[2 + side])[0]

    def pairs(r, c):
        return (r >> 1) == (c & 127) + (c >> 7) - 1

    pool_1 = pick(256, 384, pairs)

    def window(x1, y1):
        return V[pl.ds(2 * x1, 4), pl.ds(2 * y1, 4)].reshape(256, 256)

    def first_block(y1, carry):
        for x1 in range(2):
            act, slope = act_slope(dot(w1e, window(x1, y1)))
            SL[x1, y1] = slope
            cells = (act[:32] + act[32:64]) + (act[64:96] + act[96:])
            pooled = (0.125 * dot_split(cells, pool_1)).astype(BF16)
            for c in range(3):
                PS[x1 + 1, y1 + 1, 32 * c : 32 * c + 32] = pooled[:, 128 * c : 128 * c + 128]
        return carry

    lax.fori_loop(0, 8, first_block, 0)

    pooled_refs = functools.partial(field_refs, PS, 32, 64)
    halo_start(1, pooled_refs)

    def spread_edges(field, ch):
        def both(cells):
            count = cells.shape[0]
            sides = dot(cells.reshape(count * ch, 128), shift_2).astype(BF16)
            return sides.reshape(count, ch, 256)

        for x in (0, 3):
            sides = both(field[x, :, ch : 2 * ch])
            field[x, :, 0:ch] = sides[:, :, :128]
            field[x, :, 2 * ch :] = sides[:, :, 128:]
        for y in (0, 9):
            sides = both(field[1:3, y, ch : 2 * ch])
            field[1:3, y, 0:ch] = sides[:, :, :128]
            field[1:3, y, 2 * ch :] = sides[:, :, 128:]

    def taps(field, x, y2):
        depth = 3 * field.shape[2]
        one = field[x, pl.ds(2 * y2, 3)].reshape(depth, 128)
        two = field[x, pl.ds(2 * y2 + 1, 3)].reshape(depth, 128)
        return jnp.concatenate([one, two], axis=1)

    halo_wait(1, pooled_refs)
    spread_edges(PS, 32)

    pool_2 = pick(128, 64, lambda r, c: (r >> 1) == c)
    spread_2 = pick(64, 128, lambda r, c: r == (c >> 1))

    def second_block(y2, carry):
        seeds = 0.125 * dot(cot[y2], spread_2)
        seeds = jnp.concatenate([seeds, seeds], axis=1)
        total = None
        for x1 in range(2):
            pre = None
            for a in range(3):
                term = dot(w2a[a], taps(PS, x1 + a, y2))
                pre = term if pre is None else pre + term
            act, slope = act_slope(pre)
            total = act if total is None else total + act
            grad = (slope * seeds).astype(BF16)
            for yo in range(2):
                cells = grad[:, 128 * yo : 128 * yo + 128]
                sides = dot(cells, shift_2).astype(BF16)
                GS[x1 + 1, 2 * y2 + 1 + yo, 64:128] = cells
                GS[x1 + 1, 2 * y2 + 1 + yo, 0:64] = sides[:, :128]
                GS[x1 + 1, 2 * y2 + 1 + yo, 128:192] = sides[:, 128:]
        total = total[:, :128] + total[:, 128:]
        p2_out[y2] = (0.125 * dot_split(total, pool_2)).astype(BF16)
        return carry

    lax.fori_loop(0, 4, second_block, 0)

    grad_refs = functools.partial(field_refs, GS, 64, 128)
    halo_start(2, grad_refs)

    dw2[...] = jnp.zeros_like(dw2)
    groups = dw2.shape[0]
    share = 64 // groups

    def second_grad(y2, carry):
        for a in range(3):
            term = None
            for x1 in range(2):
                cells = jnp.concatenate(
                    [GS[x1 + 1, 2 * y2 + 1, 64:128], GS[x1 + 1, 2 * y2 + 2, 64:128]], axis=1
                )
                part = dot_lanes(cells, taps(PS, x1 + a, y2))
                term = part if term is None else term + part
            for g in range(groups):
                dw2[g, a] += term[share * g : share * g + share]
        return carry

    lax.fori_loop(0, 4, second_grad, 0)
    rs_send[...] = dw2[...].astype(BF16)

    def stage_copy(stage, src, dst_of, sems, d, incoming):
        size, me, device = place(stage)
        peer = lax.rem(me + d, size)
        slot = peer if incoming else me
        return pltpu.make_async_remote_copy(
            src_ref=src(peer, me),
            dst_ref=dst_of(slot),
            send_sem=sems.at[0, d],
            recv_sem=sems.at[1, slot],
            device_id=device(peer),
            device_id_type=MESH,
        )

    def stage_start(stage, src, dst_of, sems):
        for d in range(1, stages[stage][1]):
            stage_copy(stage, src, dst_of, sems, d, False).start()

    def stage_wait(stage, src, dst_of, sems):
        for d in range(1, stages[stage][1]):
            stage_copy(stage, src, dst_of, sems, d, False).wait_send()
            stage_copy(stage, src, dst_of, sems, d, True).wait_recv()

    def scatter(step):
        step(0, lambda peer, me: rs_send.at[peer], lambda slot: rs_recv.at[slot], sem_rs)

    def gather(step, stage, buffer, sems):
        step(
            stage,
            lambda peer, me: buffer.at[stage, me],
            lambda slot: buffer.at[stage, slot],
            sems.at[stage],
        )

    def total_of(buffer, stage):
        total = buffer[stage, 0]
        for i in range(1, stages[stage][1]):
            total = total + buffer[stage, i]
        return total

    scatter(stage_start)

    halo_wait(2, grad_refs)
    spread_edges(GS, 64)
    spread_1 = pick(128, 256, lambda r, c: r == (c >> 1))
    dw1[...] = jnp.zeros_like(dw1)

    def first_grad(y2, carry):
        for x1 in range(2):
            back = None
            for a in range(3):
                term = dot(w2b[a], taps(GS, x1 + a, y2))
                back = term if back is None else back + term
            for yo in range(2):
                y1 = 2 * y2 + yo
                seed = 0.125 * dot_split(back[:, 128 * yo : 128 * yo + 128], spread_1)
                seed = jnp.concatenate([seed] * 4, axis=0)
                grad = (SL[x1, y1] * seed).astype(BF16)
                dw1[...] += dot_lanes(grad, window(x1, y1))
        return carry

    lax.fori_loop(0, 4, first_grad, 0)

    folded = None
    for i in range(4):
        to_taps = expand_map(i // 2, i % 2)
        for part in split(dw1[32 * i : 32 * i + 32], 3):
            term = dot_lanes(part, to_taps)
            folded = term if folded is None else folded + term

    _, mine, _ = place(0)
    ar1[0, mine] = folded
    gather(stage_start, 0, ar1, sem_ar1)
    scatter(stage_wait)
    total = dw2[mine]
    for d in range(1, groups):
        total = total + rs_recv[lax.rem(mine + d, groups)].astype(F32)
    for stage in range(1, len(stages)):
        _, mine, _ = place(stage)
        ar2[stage, mine] = total
        gather(stage_start, stage, ar2, sem_ar2)
        gather(stage_wait, stage - 1, ar1, sem_ar1)
        ar1[stage, mine] = total_of(ar1, stage - 1)
        gather(stage_start, stage, ar1, sem_ar1)
        gather(stage_wait, stage, ar2, sem_ar2)
        total = total_of(ar2, stage)
    g2_out[...] = total
    last = len(stages) - 1
    gather(stage_wait, last, ar1, sem_ar1)
    g1_out[...] = total_of(ar1, last)


def stages_of(mesh):
    stages = [("pencil", mesh.shape["pencil"], 1)]
    stride = 1
    while stride < mesh.shape["slab"]:
        stages.append(("slab", 4, stride))
        stride *= 4
    return stages


def solution(mesh):
    stages = stages_of(mesh)
    pencils = mesh.shape["pencil"]
    share = 64 // pencils
    steps = len(stages)
    most = max(size for _, size, _ in stages)

    def per_device(volume, weight_one, weight_two, cotangent):
        w1f = jnp.pad(weight_one.reshape(32, 108), ((0, 0), (0, 20)))
        w2a = weight_two.reshape(64, 3, 288).transpose(1, 0, 2)
        w2b = jnp.flip(weight_two, axis=1).transpose(2, 1, 0).reshape(32, 3, 576)
        w2b = w2b.transpose(1, 0, 2)
        cot = cotangent.reshape(64, 4, 64).transpose(1, 0, 2)
        vmem = pl.BlockSpec(memory_space=pltpu.VMEM)
        pooled, grad_one, grad_two = pl.pallas_call(
            functools.partial(kernel, stages),
            out_shape=(
                jax.ShapeDtypeStruct((4, 64, 64), BF16),
                jax.ShapeDtypeStruct((32, 128), F32),
                jax.ShapeDtypeStruct((3, share, 288), F32),
            ),
            in_specs=[vmem] * 5,
            out_specs=(vmem,) * 3,
            scratch_shapes=[
                pltpu.VMEM((6, 18, 16, 256), BF16),
                pltpu.VMEM((4, 10, 96, 128), BF16),
                pltpu.VMEM((4, 10, 192, 128), BF16),
                pltpu.VMEM((2, 8, 128, 256), F32),
                pltpu.VMEM((2, 16, 256), BF16),
                pltpu.VMEM((2, 4, 16, 256), BF16),
                pltpu.VMEM((2, 16, 256), BF16),
                pltpu.VMEM((4, 16, 256), BF16),
                pltpu.VMEM((128, 256), F32),
                pltpu.VMEM((pencils, 3, share, 288), F32),
                pltpu.VMEM((pencils, 3, share, 288), BF16),
                pltpu.VMEM((pencils, 3, share, 288), BF16),
                pltpu.VMEM((steps, most, 32, 128), F32),
                pltpu.VMEM((steps, most, 3, share, 288), F32),
                pltpu.SemaphoreType.DMA((3, 8)),
                pltpu.SemaphoreType.DMA((3, 8)),
                pltpu.SemaphoreType.DMA((2, most)),
                pltpu.SemaphoreType.DMA((steps, 2, most)),
                pltpu.SemaphoreType.DMA((steps, 2, most)),
            ],
            compiler_params=pltpu.CompilerParams(
                collective_id=0, has_side_effects=True, vmem_limit_bytes=40 * 2**20
            ),
        )(volume, w1f, w2a, w2b, cot)
        pooled_two = pooled.transpose(1, 0, 2).reshape(64, 1, 4, 64)
        grad_one = grad_one[:, :108].reshape(32, 27, 4)
        grad_two = grad_two.transpose(1, 0, 2).reshape(share, 27, 32)
        return (pooled_two, grad_one, grad_two)

    in_specs = (P(None, "slab", "pencil", None), P(), P(), P(None, "slab", "pencil", None))
    out_specs = (P(None, "slab", "pencil", None), P(), P("pencil", None, None))
    return jax.shard_map(
        per_device, mesh=mesh, in_specs=in_specs, out_specs=out_specs, check_vma=False
    )
```

```python
import functools

import jax
import jax.numpy as jnp
from jax import lax
from jax.experimental import pallas as pl
from jax.experimental.pallas import tpu as pltpu
from jax.sharding import PartitionSpec as P

MESH = pl.DeviceIdType.MESH
LOW = 4
F32 = jnp.float32
BF16 = jnp.bfloat16
SIDES = ((1, 0), (-1, 0), (0, 1), (0, -1), (1, 1), (1, -1), (-1, 1), (-1, -1))


def pick(rows, cols, hit):
    r = lax.broadcasted_iota(jnp.int32, (rows, cols), 0)
    c = lax.broadcasted_iota(jnp.int32, (rows, cols), 1)
    return jnp.where(hit(r, c), 1.0, 0.0).astype(BF16)


def dot(a, b):
    return jnp.dot(a, b, preferred_element_type=F32)


def dot_lanes(a, b):
    return lax.dot_general(a, b, (((1,), (1,)), ((), ())), preferred_element_type=F32)


def split(value, count):
    parts = []
    for _ in range(count):
        part = value.astype(BF16)
        parts.append(part)
        value = value - part.astype(F32)
    return parts


def dot_split(value, b, count=2):
    total = None
    for part in split(value, count):
        term = dot(part, b)
        total = term if total is None else total + term
    return total


def act_slope(pre):
    t = jnp.tanh(0.5 * pre)
    act = 0.3 * pre + 0.7 * (jnp.maximum(pre, 0.0) - jnp.log(0.5 + 0.5 * jnp.abs(t)))
    return act, 0.65 + 0.35 * t


def expand_map(xo, yo):
    def hit(r, j):
        a = (j >> 6) - xo
        b = ((j >> 4) & 3) - yo
        slot = j & 15
        ok = (a >= 0) & (a < 3) & (b >= 0) & (b < 3) & (slot < 12)
        return ok & (r == 36 * a + 12 * b + slot)

    return pick(128, 256, hit)


def kernel(
    vol,
    w1f,
    w2a,
    w2b,
    cot,
    p2_out,
    g1_out,
    g2_out,
    V,
    PS,
    GS,
    SL,
    ypack,
    xrecv,
    yrecv,
    crecv,
    dw1,
    dw2,
    part2,
    sum_a,
    sum_b,
    sum_c,
    sum_1,
    halo_send,
    halo_recv,
    sem_a,
    sem_b,
    sem_c,
    sem_1,
):
    slab = lax.axis_index("slab")
    pencil = lax.axis_index("pencil")
    slabs = lax.axis_size("slab")
    pencils = lax.axis_size("pencil")

    def exists(dx, dy):
        x = slab + dx
        y = pencil + dy
        ok = None
        if dx:
            ok = (x >= 0) & (x < slabs)
        if dy:
            oky = (y >= 0) & (y < pencils)
            ok = oky if ok is None else ok & oky
        return ok

    low = lax.rem(slab, LOW)
    group_z = (LOW * pencils, low * pencils + pencil, lambda i: (slab - low + i // pencils, lax.rem(i, pencils)))
    group_xy = (slabs // LOW, slab // LOW, lambda i: (i * LOW + low, pencil))
    group_low = (LOW, low, lambda i: (slab - low + i, pencil))

    xrecv[...] = jnp.zeros_like(xrecv)
    yrecv[...] = jnp.zeros_like(yrecv)
    crecv[...] = jnp.zeros_like(crecv)
    for field in (PS, GS):
        edge = field.shape[2:]
        for x in (0, 3):
            field[x] = jnp.zeros(field.shape[1:], BF16)
        for y in (0, 9):
            field[1:3, y] = jnp.zeros((2,) + edge, BF16)

    barrier = pltpu.get_barrier_semaphore()
    arrivals = 0
    for dx, dy in SIDES:
        ok = exists(dx, dy)
        arrivals = arrivals + ok.astype(jnp.int32)

        @pl.when(ok)
        def _():
            pl.semaphore_signal(
                barrier, inc=1, device_id=(slab + dx, pencil + dy), device_id_type=MESH
            )

    for size, me, device in (group_z, group_xy):
        arrivals = arrivals + (size - 1)
        for d in range(1, size):
            pl.semaphore_signal(
                barrier, inc=1, device_id=device(lax.rem(me + d, size)), device_id_type=MESH
            )

    edges = pick(32, 256, lambda r, c: c == ((r & 15) << 4) + 15 * (r >> 4))
    packed = dot(edges, vol[...].reshape(256, 256)).astype(BF16)
    ypack[0] = packed[:16]
    ypack[1] = packed[16:]

    def halo_copy(phase, k, refs):
        dx, dy = SIDES[k]
        src, dst = refs(dx, dy)
        return pltpu.make_async_remote_copy(
            src_ref=src,
            dst_ref=dst,
            send_sem=halo_send.at[phase, k],
            recv_sem=halo_recv.at[phase, k],
            device_id=(slab + dx, pencil + dy),
            device_id_type=MESH,
        )

    def halo_start(phase, refs):
        for k, (dx, dy) in enumerate(SIDES):

            @pl.when(exists(dx, dy))
            def _():
                halo_copy(phase, k, refs).start()

    def halo_wait(phase, refs):
        for k, (dx, dy) in enumerate(SIDES):

            @pl.when(exists(dx, dy))
            def _():
                halo_copy(phase, k, refs).wait_send()

            @pl.when(exists(-dx, -dy))
            def _():
                halo_copy(phase, k, refs).wait_recv()

    def volume_refs(dx, dy):
        if dy == 0:
            return vol.at[:, 3 if dx == 1 else 0], xrecv.at[0 if dx == 1 else 1]
        src = ypack.at[1 if dy == 1 else 0]
        side = 0 if dy == 1 else 1
        if dx == 0:
            return src, yrecv.at[side]
        return src, crecv.at[2 * (0 if dx == 1 else 1) + side]

    def field_refs(field, lo, hi, dx, dy):
        sx = {1: 2, -1: 1, 0: pl.ds(1, 2)}[dx]
        tx = {1: 0, -1: 3, 0: pl.ds(1, 2)}[dx]
        sy = {1: 8, -1: 1, 0: pl.ds(1, 8)}[dy]
        ty = {1: 0, -1: 9, 0: pl.ds(1, 8)}[dy]
        rows = pl.ds(lo, hi - lo)
        return field.at[sx, sy, rows], field.at[tx, ty, rows]

    shift_1 = pick(256, 512, lambda r, c: r == jnp.where(c < 256, c - 1, c - 255))
    shift_2 = pick(128, 256, lambda r, c: r == jnp.where(c < 128, c - 1, c - 127))

    def shifted(block):
        sides = dot(block, shift_1).astype(BF16)
        return jnp.concatenate([sides[:, :256], block, sides[:, 256:]], axis=0)

    def order(r, c):
        slot = r & 15
        return (slot < 12) & (c == ((slot >> 2) << 6) + ((slot & 3) << 4) + (r >> 4))

    def order_edge(r, c):
        slot = r & 15
        return (slot < 12) & (c == ((slot >> 2) << 4) + ((slot & 3) << 2) + (r >> 4))

    to_rows = pick(256, 192, order)
    to_edge = pick(64, 48, order_edge)

    def fill(x, block):
        rows = dot(to_rows, shifted(block.reshape(64, 256))).astype(BF16)
        V[x, 1:17] = rows.reshape(16, 16, 256)

    def edge_rows(block):
        return dot(to_edge, shifted(block)).astype(BF16).reshape(4, 16, 256)

    for x in range(4):
        fill(x + 1, vol[:, x])

    w1e = jnp.concatenate(
        [dot(w1f[...], expand_map(xo, yo)).astype(BF16) for xo in range(2) for yo in range(2)],
        axis=0,
    )

    pl.semaphore_wait(barrier, arrivals)
    halo_start(0, volume_refs)
    halo_wait(0, volume_refs)
    fill(0, xrecv[0])
    fill(5, xrecv[1])
    for side, y in ((0, 0), (1, 17)):
        V[1:5, y] = edge_rows(yrecv[side])
        V[0, y] = edge_rows(crecv[side])[3]
        V[5, y] = edge_rows(crecv[2 + side])[0]

    def pairs(r, c):
        return (r >> 1) == (c & 127) + (c >> 7) - 1

    pool_1 = pick(256, 384, pairs)

    def window(x1, y1):
        return V[pl.ds(2 * x1, 4), pl.ds(2 * y1, 4)].reshape(256, 256)

    def first_block(y1, carry):
        for x1 in range(2):
            act, slope = act_slope(dot(w1e, window(x1, y1)))
            SL[x1, y1] = slope
            cells = (act[:32] + act[32:64]) + (act[64:96] + act[96:])
            pooled = (0.125 * dot_split(cells, pool_1)).astype(BF16)
            for c in range(3):
                PS[x1 + 1, y1 + 1, 32 * c : 32 * c + 32] = pooled[:, 128 * c : 128 * c + 128]
        return carry

    lax.fori_loop(0, 8, first_block, 0)

    pooled_refs = functools.partial(field_refs, PS, 32, 64)
    halo_start(1, pooled_refs)

    def spread_edges(field, ch):
        def both(cells):
            count = cells.shape[0]
            sides = dot(cells.reshape(count * ch, 128), shift_2).astype(BF16)
            return sides.reshape(count, ch, 256)

        for x in (0, 3):
            sides = both(field[x, :, ch : 2 * ch])
            field[x, :, 0:ch] = sides[:, :, :128]
            field[x, :, 2 * ch :] = sides[:, :, 128:]
        for y in (0, 9):
            sides = both(field[1:3, y, ch : 2 * ch])
            field[1:3, y, 0:ch] = sides[:, :, :128]
            field[1:3, y, 2 * ch :] = sides[:, :, 128:]

    def taps(field, x, y2):
        depth = 3 * field.shape[2]
        one = field[x, pl.ds(2 * y2, 3)].reshape(depth, 128)
        two = field[x, pl.ds(2 * y2 + 1, 3)].reshape(depth, 128)
        return jnp.concatenate([one, two], axis=1)

    halo_wait(1, pooled_refs)
    spread_edges(PS, 32)

    pool_2 = pick(128, 64, lambda r, c: (r >> 1) == c)
    spread_2 = pick(64, 128, lambda r, c: r == (c >> 1))

    def second_block(y2, carry):
        seeds = 0.125 * dot(cot[y2], spread_2)
        seeds = jnp.concatenate([seeds, seeds], axis=1)
        total = None
        for x1 in range(2):
            pre = None
            for a in range(3):
                term = dot(w2a[a], taps(PS, x1 + a, y2))
                pre = term if pre is None else pre + term
            act, slope = act_slope(pre)
            total = act if total is None else total + act
            grad = (slope * seeds).astype(BF16)
            for yo in range(2):
                cells = grad[:, 128 * yo : 128 * yo + 128]
                sides = dot(cells, shift_2).astype(BF16)
                GS[x1 + 1, 2 * y2 + 1 + yo, 64:128] = cells
                GS[x1 + 1, 2 * y2 + 1 + yo, 0:64] = sides[:, :128]
                GS[x1 + 1, 2 * y2 + 1 + yo, 128:192] = sides[:, 128:]
        total = total[:, :128] + total[:, 128:]
        p2_out[y2] = (0.125 * dot_split(total, pool_2)).astype(BF16)
        return carry

    lax.fori_loop(0, 4, second_block, 0)

    grad_refs = functools.partial(field_refs, GS, 64, 128)
    halo_start(2, grad_refs)

    dw2[...] = jnp.zeros_like(dw2)
    groups = dw2.shape[0]
    share = 64 // groups

    def second_grad(y2, carry):
        for a in range(3):
            term = None
            for x1 in range(2):
                cells = jnp.concatenate(
                    [GS[x1 + 1, 2 * y2 + 1, 64:128], GS[x1 + 1, 2 * y2 + 2, 64:128]], axis=1
                )
                part = dot_lanes(cells, taps(PS, x1 + a, y2))
                term = part if term is None else term + part
            for g in range(groups):
                dw2[g, a] += term[share * g : share * g + share]
        return carry

    lax.fori_loop(0, 4, second_grad, 0)
    part2[...] = dw2[...].astype(BF16)

    def group_copies(group, src_of, dst_of, sems, sends=None, gets=None):
        size, me, device = group

        def copy(d, slot):
            peer = lax.rem(me + d, size)
            return pltpu.make_async_remote_copy(
                src_ref=src_of(peer),
                dst_ref=dst_of(peer if slot is None else slot),
                send_sem=sems.at[0, d],
                recv_sem=sems.at[1, peer if slot is None else slot],
                device_id=device(peer),
                device_id_type=MESH,
            )

        def each(allowed, act):
            for d in range(1, size):
                if allowed is None:
                    act(d)
                else:
                    pl.when(allowed(lax.rem(me + d, size)))(functools.partial(act, d))

        def start():
            each(sends, lambda d: copy(d, me).start())

        def wait():
            each(sends, lambda d: copy(d, me).wait_send())
            each(gets, lambda d: copy(d, None).wait_recv())

        return start, wait

    owner = low < 3
    mine = jnp.minimum(low, 2)
    start_a, wait_a = group_copies(
        group_z,
        lambda i: part2.at[lax.rem(i, pencils), jnp.minimum(i // pencils, 2)],
        lambda slot: sum_a.at[slot],
        sem_a,
        sends=lambda i: i // pencils < 3,
        gets=lambda i: owner,
    )
    start_b, wait_b = group_copies(
        group_xy,
        lambda i: sum_b.at[group_xy[1]],
        lambda slot: sum_b.at[slot],
        sem_b,
        sends=lambda i: owner,
        gets=lambda i: owner,
    )
    start_c, wait_c = group_copies(
        group_low,
        lambda i: sum_c.at[low],
        lambda slot: sum_c.at[slot],
        sem_c,
        sends=lambda i: owner,
        gets=lambda i: i < 3,
    )
    sums_1 = [
        group_copies(
            group,
            lambda i, k=k, me=group[1]: sum_1.at[k, me],
            lambda slot, k=k: sum_1.at[k, slot],
            sem_1.at[k],
        )
        for k, group in enumerate((group_z, group_xy))
    ]

    def total_of(slots, size):
        total = slots[0].astype(F32)
        for i in range(1, size):
            total = total + slots[i].astype(F32)
        return total

    start_a()

    halo_wait(2, grad_refs)
    spread_edges(GS, 64)
    spread_1 = pick(128, 256, lambda r, c: r == (c >> 1))
    dw1[...] = jnp.zeros_like(dw1)

    def first_grad(y2, carry):
        for x1 in range(2):
            back = None
            for a in range(3):
                term = dot(w2b[a], taps(GS, x1 + a, y2))
                back = term if back is None else back + term
            for yo in range(2):
                y1 = 2 * y2 + yo
                seed = 0.125 * dot_split(back[:, 128 * yo : 128 * yo + 128], spread_1)
                seed = jnp.concatenate([seed] * 4, axis=0)
                grad = (SL[x1, y1] * seed).astype(BF16)
                dw1[...] += dot_lanes(grad, window(x1, y1))
        return carry

    lax.fori_loop(0, 2, first_grad, 0)
    wait_a()

    @pl.when(owner)
    def _():
        sum_a[group_z[1]] = part2[pencil, mine]
        sum_b[group_xy[1]] = total_of(sum_a, group_z[0]).astype(BF16)

    start_b()
    lax.fori_loop(2, 4, first_grad, 0)

    folded = None
    for i in range(4):
        to_taps = expand_map(i // 2, i % 2)
        for part in split(dw1[32 * i : 32 * i + 32], 3):
            term = dot_lanes(part, to_taps)
            folded = term if folded is None else folded + term

    sum_1[0, group_z[1]] = folded.astype(BF16)
    sums_1[0][0]()
    wait_b()

    @pl.when(owner)
    def _():
        sum_c[low] = total_of(sum_b, group_xy[0])

    start_c()
    sums_1[0][1]()
    sum_1[1, group_xy[1]] = total_of(sum_1.at[0], group_z[0]).astype(BF16)
    sums_1[1][0]()
    wait_c()
    for a in range(3):
        g2_out[a] = sum_c[a]
    sums_1[1][1]()
    g1_out[...] = total_of(sum_1.at[1], group_xy[0])


def solution(mesh):
    pencils = mesh.shape["pencil"]
    share = 64 // pencils
    size_z = LOW * pencils
    size_xy = mesh.shape["slab"] // LOW
    most = max(size_z, size_xy)

    def per_device(volume, weight_one, weight_two, cotangent):
        w1f = jnp.pad(weight_one.reshape(32, 108), ((0, 0), (0, 20)))
        w2a = weight_two.reshape(64, 3, 288).transpose(1, 0, 2)
        w2b = jnp.flip(weight_two, axis=1).transpose(2, 1, 0).reshape(32, 3, 576)
        w2b = w2b.transpose(1, 0, 2)
        cot = cotangent.reshape(64, 4, 64).transpose(1, 0, 2)
        vmem = pl.BlockSpec(memory_space=pltpu.VMEM)
        pooled, grad_one, grad_two = pl.pallas_call(
            kernel,
            out_shape=(
                jax.ShapeDtypeStruct((4, 64, 64), BF16),
                jax.ShapeDtypeStruct((32, 128), F32),
                jax.ShapeDtypeStruct((3, share, 288), F32),
            ),
            in_specs=[vmem] * 5,
            out_specs=(vmem,) * 3,
            scratch_shapes=[
                pltpu.VMEM((6, 18, 16, 256), BF16),
                pltpu.VMEM((4, 10, 96, 128), BF16),
                pltpu.VMEM((4, 10, 192, 128), BF16),
                pltpu.VMEM((2, 8, 128, 256), F32),
                pltpu.VMEM((2, 16, 256), BF16),
                pltpu.VMEM((2, 4, 16, 256), BF16),
                pltpu.VMEM((2, 16, 256), BF16),
                pltpu.VMEM((4, 16, 256), BF16),
                pltpu.VMEM((128, 256), F32),
                pltpu.VMEM((pencils, 3, share, 288), F32),
                pltpu.VMEM((pencils, 3, share, 288), BF16),
                pltpu.VMEM((size_z, share, 288), BF16),
                pltpu.VMEM((size_xy, share, 288), BF16),
                pltpu.VMEM((LOW, share, 288), F32),
                pltpu.VMEM((2, most, 32, 128), BF16),
                pltpu.SemaphoreType.DMA((3, 8)),
                pltpu.SemaphoreType.DMA((3, 8)),
                pltpu.SemaphoreType.DMA((2, size_z)),
                pltpu.SemaphoreType.DMA((2, size_xy)),
                pltpu.SemaphoreType.DMA((2, LOW)),
                pltpu.SemaphoreType.DMA((2, 2, most)),
            ],
            compiler_params=pltpu.CompilerParams(
                collective_id=0, has_side_effects=True, vmem_limit_bytes=40 * 2**20
            ),
        )(volume, w1f, w2a, w2b, cot)
        pooled_two = pooled.transpose(1, 0, 2).reshape(64, 1, 4, 64)
        grad_one = grad_one[:, :108].reshape(32, 27, 4)
        grad_two = grad_two.transpose(1, 0, 2).reshape(share, 27, 32)
        return (pooled_two, grad_one, grad_two)

    in_specs = (P(None, "slab", "pencil", None), P(), P(), P(None, "slab", "pencil", None))
    out_specs = (P(None, "slab", "pencil", None), P(), P("pencil", None, None))
    return jax.shard_map(
        per_device, mesh=mesh, in_specs=in_specs, out_specs=out_specs, check_vma=False
    )
```

```python
import functools

import jax
import jax.numpy as jnp
from jax import lax
from jax.experimental import pallas as pl
from jax.experimental.pallas import tpu as pltpu
from jax.sharding import PartitionSpec as P

MESH = pl.DeviceIdType.MESH
LOW = 4
F32 = jnp.float32
BF16 = jnp.bfloat16
SIDES = ((1, 1), (1, -1), (-1, 1), (-1, -1), (1, 0), (-1, 0), (0, 1), (0, -1))


def pick(rows, cols, hit):
    r = lax.broadcasted_iota(jnp.int32, (rows, cols), 0)
    c = lax.broadcasted_iota(jnp.int32, (rows, cols), 1)
    return jnp.where(hit(r, c), 1.0, 0.0).astype(BF16)


def dot(a, b):
    return jnp.dot(a, b, preferred_element_type=F32)


def dot_lanes(a, b):
    return lax.dot_general(a, b, (((1,), (1,)), ((), ())), preferred_element_type=F32)


def split(value, count):
    parts = []
    for _ in range(count):
        part = value.astype(BF16)
        parts.append(part)
        value = value - part.astype(F32)
    return jnp.concatenate(parts, axis=0)


def joined(value, count):
    rows = value.shape[0] // count
    total = value[:rows]
    for i in range(1, count):
        total = total + value[rows * i : rows * i + rows]
    return total


def act_slope(pre):
    t = jnp.tanh(0.5 * pre)
    act = 0.3 * pre + 0.7 * (jnp.maximum(pre, 0.0) - jnp.log(0.5 + 0.5 * jnp.abs(t)))
    return act, 0.65 + 0.35 * t


def expand_map(yo):
    def hit(r, j):
        b = ((j >> 4) & 3) - yo
        slot = j & 15
        return (b >= 0) & (b < 3) & (slot < 12) & (r == 36 * (j >> 6) + 12 * b + slot)

    return pick(128, 192, hit)


def kernel(
    vol_hbm,
    w2_hbm,
    w1f,
    cot,
    p2_out,
    g1_out,
    g2_out,
    vol,
    w2r,
    V,
    PS,
    GS,
    SL,
    CELLS,
    TOT,
    SEED,
    G2,
    BACK,
    W2A,
    W2B,
    MAPS,
    pool_1,
    shift_2,
    spread_1,
    ypack,
    xrecv,
    yrecv,
    crecv,
    dw1,
    dw2,
    part2,
    sum_a,
    sum_b,
    sum_c,
    sum_1,
    sem_in,
    halo_send,
    halo_recv,
    sem_a,
    sem_b,
    sem_c,
    sem_1,
):
    slab = lax.axis_index("slab")
    pencil = lax.axis_index("pencil")
    slabs = lax.axis_size("slab")
    pencils = lax.axis_size("pencil")

    load_vol = pltpu.make_async_copy(vol_hbm, vol, sem_in.at[0])
    load_w2 = pltpu.make_async_copy(w2_hbm, w2r, sem_in.at[1])
    load_vol.start()
    load_w2.start()

    def exists(dx, dy):
        x = slab + dx
        y = pencil + dy
        ok = None
        if dx:
            ok = (x >= 0) & (x < slabs)
        if dy:
            oky = (y >= 0) & (y < pencils)
            ok = oky if ok is None else ok & oky
        return ok

    low = lax.rem(slab, LOW)
    group_z = (
        LOW * pencils,
        low * pencils + pencil,
        lambda i: (slab - low + i // pencils, lax.rem(i, pencils)),
    )
    group_xy = (slabs // LOW, slab // LOW, lambda i: (i * LOW + low, pencil))
    group_low = (LOW, low, lambda i: (slab - low + i, pencil))

    barrier = pltpu.get_barrier_semaphore()
    arrivals = 0
    for dx, dy in SIDES:
        ok = exists(dx, dy)
        arrivals = arrivals + ok.astype(jnp.int32)

        @pl.when(ok)
        def _():
            pl.semaphore_signal(
                barrier, inc=1, device_id=(slab + dx, pencil + dy), device_id_type=MESH
            )

    for size, me, device in (group_z, group_xy):
        arrivals = arrivals + (size - 1)
        for d in range(1, size):
            pl.semaphore_signal(
                barrier, inc=1, device_id=device(lax.rem(me + d, size)), device_id_type=MESH
            )

    def volume_refs(dx, dy):
        if dy == 0:
            return vol.at[:, 3 if dx == 1 else 0], xrecv.at[0 if dx == 1 else 1]
        src = ypack.at[1 if dy == 1 else 0]
        side = 0 if dy == 1 else 1
        if dx == 0:
            return src, yrecv.at[side]
        return src, crecv.at[2 * (0 if dx == 1 else 1) + side]

    def field_refs(field, lo, hi, dx, dy):
        sx = {1: 2, -1: 1, 0: pl.ds(1, 2)}[dx]
        tx = {1: 0, -1: 3, 0: pl.ds(1, 2)}[dx]
        sy = {1: 8, -1: 1, 0: pl.ds(1, 8)}[dy]
        ty = {1: 0, -1: 9, 0: pl.ds(1, 8)}[dy]
        rows = pl.ds(lo, hi - lo)
        return field.at[sx, sy, rows], field.at[tx, ty, rows]

    pooled_refs = functools.partial(field_refs, PS, 32, 64)
    grad_refs = functools.partial(field_refs, GS, 64, 128)

    for dx, dy in SIDES:

        @pl.when(jnp.logical_not(exists(-dx, -dy)))
        def _():
            for refs in (volume_refs, pooled_refs, grad_refs):
                target = refs(dx, dy)[1]
                target[...] = jnp.zeros(target.shape, BF16)

    def halo_copy(phase, k, refs):
        dx, dy = SIDES[k]
        src, dst = refs(dx, dy)
        return pltpu.make_async_remote_copy(
            src_ref=src,
            dst_ref=dst,
            send_sem=halo_send.at[phase, k],
            recv_sem=halo_recv.at[phase, k],
            device_id=(slab + dx, pencil + dy),
            device_id_type=MESH,
        )

    def halo_start(phase, refs):
        for k, (dx, dy) in enumerate(SIDES):

            @pl.when(exists(dx, dy))
            def _():
                halo_copy(phase, k, refs).start()

    def halo_wait(phase, refs):
        for k, (dx, dy) in enumerate(SIDES):

            @pl.when(exists(dx, dy))
            def _():
                halo_copy(phase, k, refs).wait_send()

            @pl.when(exists(-dx, -dy))
            def _():
                halo_copy(phase, k, refs).wait_recv()

    load_vol.wait()
    edges = pick(32, 256, lambda r, c: c == ((r & 15) << 4) + 15 * (r >> 4))
    packed = dot(edges, vol[...].reshape(256, 256)).astype(BF16)
    ypack[0] = packed[:16]
    ypack[1] = packed[16:]

    shift_1 = pick(256, 512, lambda r, c: r == jnp.where(c < 256, c - 1, c - 255))

    def shifted(block):
        sides = dot(block, shift_1).astype(BF16)
        return sides[:, :256], block, sides[:, 256:]

    def order(r, c):
        slot = r & 15
        return (slot < 12) & (c == ((slot >> 2) << 6) + ((slot & 3) << 4) + (r >> 4))

    def order_edge(r, c):
        slot = r & 15
        return (slot < 12) & (c == ((slot >> 2) << 4) + ((slot & 3) << 2) + (r >> 4))

    to_rows = pick(256, 192, order)
    to_edge = pick(64, 48, order_edge)

    def rows_of(parts, lo, hi):
        return jnp.concatenate([part[lo:hi] for part in parts], axis=0)

    local = shifted(jnp.concatenate([vol[:, x].reshape(64, 256) for x in range(4)], axis=0))
    for x in range(4):
        rows = dot(to_rows, rows_of(local, 64 * x, 64 * x + 64)).astype(BF16)
        V[x + 1, 1:17] = rows.reshape(16, 16, 256)

    for yo in range(2):
        MAPS[yo] = expand_map(yo)
    w1p = jnp.concatenate([dot(w1f[...], MAPS[yo]).astype(BF16) for yo in range(2)], axis=0)

    pl.semaphore_wait(barrier, arrivals)
    halo_start(0, volume_refs)

    def window(x, y1):
        return V[pl.ds(x, 3), pl.ds(2 * y1, 4)].reshape(192, 256)

    def first_cells(x, y1):
        act, slope = act_slope(dot(w1p, window(x, y1)))
        SL[x, y1] = slope
        return act[:32] + act[32:]

    def inner(i, carry):
        for x in (1, 2):
            for j in range(2):
                CELLS[x - 1, 1 + 2 * i + j] = first_cells(x, 1 + 2 * i + j)
        return carry

    lax.fori_loop(0, 3, inner, 0)

    def pairs(r, c):
        return (r >> 1) == (c & 127) + (c >> 7) - 1

    pool_1[...] = pick(256, 384, pairs)
    shift_2[...] = pick(128, 256, lambda r, c: r == jnp.where(c < 128, c - 1, c - 127))
    spread_1[...] = pick(128, 256, lambda r, c: r == (c >> 1))

    halo_wait(0, volume_refs)
    arrived = shifted(
        jnp.concatenate(
            [xrecv[s].reshape(64, 256) for s in range(2)]
            + [yrecv[s] for s in range(2)]
            + [crecv[s] for s in range(4)],
            axis=0,
        )
    )
    for side, x in ((0, 0), (1, 5)):
        rows = dot(to_rows, rows_of(arrived, 64 * side, 64 * side + 64)).astype(BF16)
        V[x, 1:17] = rows.reshape(16, 16, 256)
    for side, y in ((0, 0), (1, 17)):
        at = 128 + 16 * side
        V[1:5, y] = dot(to_edge, rows_of(arrived, at, at + 16)).astype(BF16).reshape(4, 16, 256)
        at = 160 + 16 * side
        V[0, y] = dot(to_edge[48:], rows_of(arrived, at, at + 16)).astype(BF16)
        at = 192 + 16 * side
        V[5, y] = dot(to_edge[:16], rows_of(arrived, at, at + 16)).astype(BF16)

    for x in (1, 2):
        for y1 in (0, 7):
            CELLS[x - 1, y1] = first_cells(x, y1)

    def outer(i, carry):
        for x in (0, 3):
            for j in range(2):
                CELLS[x // 2, 2 * i + j] += first_cells(x, 2 * i + j)
        return carry

    lax.fori_loop(0, 4, outer, 0)

    for x1 in range(2):
        parts = split(CELLS[x1].reshape(256, 256), 2)
        pooled = (0.125 * joined(dot(parts, pool_1[...]), 2)).astype(BF16)
        for c in range(3):
            PS[x1 + 1, 1:9, 32 * c : 32 * c + 32] = pooled[:, 128 * c : 128 * c + 128].reshape(
                8, 32, 128
            )

    halo_start(1, pooled_refs)

    load_w2.wait()
    eye = pick(64, 64, lambda r, c: r == c)
    for a in range(3):
        taps_a = w2r[9 * a : 9 * a + 9].reshape(288, 64)
        W2A[64 * (2 - a) : 64 * (2 - a) + 64] = dot_lanes(eye, taps_a).astype(BF16)
        W2B[32 * (2 - a) : 32 * (2 - a) + 32] = jnp.concatenate(
            [w2r[26 - 9 * a - j] for j in range(9)], axis=1
        )
    spread_2 = pick(64, 128, lambda r, c: r == (c >> 1))
    for y2 in range(4):
        SEED[y2] = 0.125 * dot(cot[y2], spread_2)

    def spread_sides(field, ch, xs, ys):
        cells = field[xs, ys, ch : 2 * ch]
        shape = cells.shape
        sides = dot(cells.reshape(-1, 128), shift_2[...]).astype(BF16)
        field[xs, ys, 0:ch] = sides[:, :128].reshape(shape)
        field[xs, ys, 2 * ch :] = sides[:, 128:].reshape(shape)

    def spread_edges(field, ch):
        for x in (0, 3):
            spread_sides(field, ch, x, slice(0, 10))
        for y in (0, 9):
            spread_sides(field, ch, slice(1, 3), y)

    def taps(field, x, y2):
        depth = 3 * field.shape[2]
        one = field[x, pl.ds(2 * y2, 3)].reshape(depth, 128)
        two = field[x, pl.ds(2 * y2 + 1, 3)].reshape(depth, 128)
        return jnp.concatenate([one, two], axis=1)

    def both_rows(field, weights, ch, y2):
        whole = dot(weights[ch : 3 * ch], taps(field, 1, y2))
        whole = whole + dot(weights[0 : 2 * ch], taps(field, 2, y2))
        first = dot(weights[2 * ch : 3 * ch], taps(field, 0, y2))
        last = dot(weights[0:ch], taps(field, 3, y2))
        return whole + jnp.concatenate([first, last], axis=0)

    halo_wait(1, pooled_refs)
    spread_edges(PS, 32)

    def second_block(i, carry):
        for j in range(2):
            y2 = 2 * i + j
            act, slope = act_slope(both_rows(PS, W2A, 64, y2))
            total = act[:64] + act[64:]
            TOT[y2] = total[:, :128] + total[:, 128:]
            seed = jnp.concatenate([SEED[y2]] * 2, axis=0)
            grad = (slope * jnp.concatenate([seed, seed], axis=1)).astype(BF16)
            G2[y2] = grad
            for x1 in range(2):
                for yo in range(2):
                    cells = grad[64 * x1 : 64 * x1 + 64, 128 * yo : 128 * yo + 128]
                    GS[x1 + 1, 2 * y2 + 1 + yo, 64:128] = cells
        return carry

    lax.fori_loop(0, 2, second_block, 0)
    halo_start(2, grad_refs)

    groups = dw2.shape[0]
    share = 64 // groups
    dw2[...] = jnp.zeros_like(dw2)

    def second_grad(y2, carry):
        terms = [None] * 3
        for x in range(4):
            lo, hi = (0 if x < 3 else 64), (128 if x > 0 else 64)
            part = dot_lanes(G2[y2, lo:hi], taps(PS, x, y2))
            for x1 in range(2):
                if 0 <= x - x1 < 3:
                    piece = part[64 * x1 - lo : 64 * x1 - lo + 64]
                    old = terms[x - x1]
                    terms[x - x1] = piece if old is None else old + piece
        for a in range(3):
            for g in range(groups):
                dw2[g, a] += terms[a][share * g : share * g + share]
        return carry

    lax.fori_loop(0, 4, second_grad, 0)
    part2[...] = dw2[...].astype(BF16)

    def group_copies(group, src_of, dst_of, sems, sends=None, gets=None):
        size, me, device = group

        def copy(d, slot):
            peer = lax.rem(me + d, size)
            return pltpu.make_async_remote_copy(
                src_ref=src_of(peer),
                dst_ref=dst_of(peer if slot is None else slot),
                send_sem=sems.at[0, d],
                recv_sem=sems.at[1, peer if slot is None else slot],
                device_id=device(peer),
                device_id_type=MESH,
            )

        def each(allowed, act):
            for d in range(1, size):
                pl.when(allowed(lax.rem(me + d, size)))(functools.partial(act, d))

        def start():
            each(sends, lambda d: copy(d, me).start())

        def wait():
            each(sends, lambda d: copy(d, me).wait_send())
            each(gets, lambda d: copy(d, None).wait_recv())

        return start, wait

    def group_gather(group, slots, sems):
        size, me, device = group

        def start():
            for d in range(1, size):
                pltpu.make_async_remote_copy(
                    src_ref=slots.at[me],
                    dst_ref=slots.at[me],
                    send_sem=sems.at[0],
                    recv_sem=sems.at[1],
                    device_id=device(lax.rem(me + d, size)),
                    device_id_type=MESH,
                ).start()

        def wait():
            others = slots.at[pl.ds(0, size - 1)]
            for sem in (sems.at[0], sems.at[1]):
                pltpu.make_async_copy(others, others, sem).wait()

        return start, wait

    owner = low < 3
    mine = jnp.minimum(low, 2)
    start_a, wait_a = group_copies(
        group_z,
        lambda i: part2.at[lax.rem(i, pencils), jnp.minimum(i // pencils, 2)],
        lambda slot: sum_a.at[slot],
        sem_a,
        sends=lambda i: i // pencils < 3,
        gets=lambda i: owner,
    )
    start_b, wait_b = group_gather(group_xy, sum_b, sem_b)
    start_c, wait_c = group_copies(
        group_low,
        lambda i: sum_c.at[low],
        lambda slot: sum_c.at[slot],
        sem_c,
        sends=lambda i: owner,
        gets=lambda i: i < 3,
    )
    start_z, wait_z = group_gather(group_z, sum_1.at[0], sem_1.at[0])
    start_xy, wait_xy = group_gather(group_xy, sum_1.at[1], sem_1.at[1])

    def total_of(slots, size):
        total = slots[0].astype(F32)
        for i in range(1, size):
            total = total + slots[i].astype(F32)
        return total

    start_a()

    for x in (1, 2):
        spread_sides(GS, 64, x, slice(1, 9))
    pool_2 = pick(128, 64, lambda r, c: (r >> 1) == c)
    pooled = 0.125 * joined(dot(split(TOT[...].reshape(256, 128), 2), pool_2), 2)
    p2_out[...] = pooled.astype(BF16).reshape(4, 64, 64)

    halo_wait(2, grad_refs)
    spread_edges(GS, 64)

    def first_back(i, carry):
        for j in range(2):
            y2 = 2 * i + j
            back = both_rows(GS, W2B, 32, y2)
            for x1 in range(2):
                for yo in range(2):
                    cells = back[32 * x1 : 32 * x1 + 32, 128 * yo : 128 * yo + 128]
                    BACK[x1, 2 * y2 + yo] = cells
        return carry

    lax.fori_loop(0, 2, first_back, 0)
    for x1 in range(2):
        parts = split(BACK[x1].reshape(256, 128), 2)
        CELLS[x1] = (0.125 * joined(dot(parts, spread_1[...]), 2)).reshape(8, 32, 256)

    dw1[...] = jnp.zeros_like(dw1)

    def first_grad(y1, carry):
        total = None
        for x in range(4):
            seed = jnp.concatenate([CELLS[x // 2, y1]] * 2, axis=0)
            term = dot_lanes((SL[x, y1] * seed).astype(BF16), window(x, y1))
            total = term if total is None else total + term
        dw1[...] += total
        return carry

    lax.fori_loop(0, 8, first_grad, 0)

    folded = None
    for yo in range(2):
        term = joined(dot_lanes(split(dw1[32 * yo : 32 * yo + 32], 3), MAPS[yo]), 3)
        folded = term if folded is None else folded + term

    sum_1[0, group_z[1]] = folded.astype(BF16)
    start_z()
    wait_a()

    @pl.when(owner)
    def _():
        sum_a[group_z[1]] = part2[pencil, mine]
        sum_b[group_xy[1]] = total_of(sum_a, group_z[0]).astype(BF16)
        start_b()

    wait_z()
    sum_1[1, group_xy[1]] = total_of(sum_1.at[0], group_z[0]).astype(BF16)
    start_xy()

    @pl.when(owner)
    def _():
        wait_b()
        sum_c[low] = total_of(sum_b, group_xy[0])

    start_c()
    wait_c()
    for a in range(3):
        g2_out[a] = sum_c[a]
    wait_xy()
    g1_out[...] = total_of(sum_1.at[1], group_xy[0])


def solution(mesh):
    pencils = mesh.shape["pencil"]
    share = 64 // pencils
    size_z = LOW * pencils
    size_xy = mesh.shape["slab"] // LOW
    most = max(size_z, size_xy)

    def per_device(volume, weight_one, weight_two, cotangent):
        w1f = jnp.pad(weight_one.reshape(32, 108), ((0, 0), (0, 20)))
        w2 = weight_two.transpose(1, 2, 0)
        cot = cotangent.reshape(64, 4, 64).transpose(1, 0, 2)
        vmem = pl.BlockSpec(memory_space=pltpu.VMEM)
        hbm = pl.BlockSpec(memory_space=pltpu.HBM)
        pooled, grad_one, grad_two = pl.pallas_call(
            kernel,
            out_shape=(
                jax.ShapeDtypeStruct((4, 64, 64), BF16),
                jax.ShapeDtypeStruct((32, 128), F32),
                jax.ShapeDtypeStruct((3, share, 288), F32),
            ),
            in_specs=[hbm, hbm, vmem, vmem],
            out_specs=(vmem,) * 3,
            scratch_shapes=[
                pltpu.VMEM((4, 4, 16, 256), BF16),
                pltpu.VMEM((27, 32, 64), BF16),
                pltpu.VMEM((6, 18, 16, 256), BF16),
                pltpu.VMEM((4, 10, 96, 128), BF16),
                pltpu.VMEM((4, 10, 192, 128), BF16),
                pltpu.VMEM((4, 8, 64, 256), F32),
                pltpu.VMEM((2, 8, 32, 256), F32),
                pltpu.VMEM((4, 64, 128), F32),
                pltpu.VMEM((4, 64, 128), F32),
                pltpu.VMEM((4, 128, 256), BF16),
                pltpu.VMEM((2, 8, 32, 128), F32),
                pltpu.VMEM((192, 288), BF16),
                pltpu.VMEM((96, 576), BF16),
                pltpu.VMEM((2, 128, 192), BF16),
                pltpu.VMEM((256, 384), BF16),
                pltpu.VMEM((128, 256), BF16),
                pltpu.VMEM((128, 256), BF16),
                pltpu.VMEM((2, 16, 256), BF16),
                pltpu.VMEM((2, 4, 16, 256), BF16),
                pltpu.VMEM((2, 16, 256), BF16),
                pltpu.VMEM((4, 16, 256), BF16),
                pltpu.VMEM((64, 192), F32),
                pltpu.VMEM((pencils, 3, share, 288), F32),
                pltpu.VMEM((pencils, 3, share, 288), BF16),
                pltpu.VMEM((size_z, share, 288), BF16),
                pltpu.VMEM((size_xy, share, 288), BF16),
                pltpu.VMEM((LOW, share, 288), F32),
                pltpu.VMEM((2, most, 32, 128), BF16),
                pltpu.SemaphoreType.DMA((2,)),
                pltpu.SemaphoreType.DMA((3, 8)),
                pltpu.SemaphoreType.DMA((3, 8)),
                pltpu.SemaphoreType.DMA((2, size_z)),
                pltpu.SemaphoreType.DMA((2,)),
                pltpu.SemaphoreType.DMA((2, LOW)),
                pltpu.SemaphoreType.DMA((2, 2)),
            ],
            compiler_params=pltpu.CompilerParams(
                collective_id=0, has_side_effects=True, vmem_limit_bytes=40 * 2**20
            ),
        )(volume, w2, w1f, cot)
        pooled_two = pooled.transpose(1, 0, 2).reshape(64, 1, 4, 64)
        grad_one = grad_one[:, :108].reshape(32, 27, 4)
        grad_two = grad_two.transpose(1, 0, 2).reshape(share, 27, 32)
        return (pooled_two, grad_one, grad_two)

    in_specs = (P(None, "slab", "pencil", None), P(), P(), P(None, "slab", "pencil", None))
    out_specs = (P(None, "slab", "pencil", None), P(), P("pencil", None, None))
    return jax.shard_map(
        per_device, mesh=mesh, in_specs=in_specs, out_specs=out_specs, check_vma=False
    )
```

```python
import functools

import jax
import jax.numpy as jnp
from jax import lax
from jax.experimental import pallas as pl
from jax.experimental.pallas import tpu as pltpu
from jax.sharding import PartitionSpec as P

MESH = pl.DeviceIdType.MESH
LOW = 4
F32 = jnp.float32
BF16 = jnp.bfloat16
SIDES = ((1, 1), (1, -1), (-1, 1), (-1, -1), (1, 0), (-1, 0), (0, 1), (0, -1))


def pick(rows, cols, hit):
    r = lax.broadcasted_iota(jnp.int32, (rows, cols), 0)
    c = lax.broadcasted_iota(jnp.int32, (rows, cols), 1)
    return jnp.where(hit(r, c), 1.0, 0.0).astype(BF16)


def dot(a, b):
    return jnp.dot(a, b, preferred_element_type=F32)


def dot_lanes(a, b):
    return lax.dot_general(a, b, (((1,), (1,)), ((), ())), preferred_element_type=F32)


def split(value, count):
    parts = []
    for _ in range(count):
        part = value.astype(BF16)
        parts.append(part)
        value = value - part.astype(F32)
    return jnp.concatenate(parts, axis=0)


def joined(value, count):
    rows = value.shape[0] // count
    total = value[:rows]
    for i in range(1, count):
        total = total + value[rows * i : rows * i + rows]
    return total


def act_slope(pre):
    t = jnp.tanh(0.5 * pre)
    act = 0.3 * pre + 0.7 * (jnp.maximum(pre, 0.0) - jnp.log(0.5 + 0.5 * jnp.abs(t)))
    return act, 0.65 + 0.35 * t


def expand_map(yo):
    def hit(r, j):
        b = ((j >> 4) & 3) - yo
        slot = j & 15
        row = 72 * (j >> 6) + 24 * b + 8 * (slot >> 2) + (slot & 3)
        return (b >= 0) & (b < 3) & (slot < 12) & (r == row)

    return pick(216, 192, hit)


def eight_rows(value):
    value = value.astype(F32)
    value = jnp.concatenate([value, value], axis=1)
    return value.reshape(-1, value.shape[2]).astype(BF16)


def kernel(
    vol_hbm,
    w1_hbm,
    w2_hbm,
    cot_hbm,
    p2_out,
    g1_out,
    g2_out,
    vol,
    w1r,
    w2r,
    cot,
    V,
    PS,
    GS,
    SL,
    CELLS,
    TOT,
    SEED,
    G2,
    BACK,
    W2A,
    W2B,
    MAPS,
    pool_1,
    shift_2,
    spread_1,
    ypack,
    xrecv,
    yrecv,
    crecv,
    dw1,
    dw2,
    part2,
    sum_a,
    sum_b,
    sum_c,
    sum_1,
    sem_in,
    halo_send,
    halo_recv,
    sem_a,
    sem_b,
    sem_c,
    sem_1,
):
    slab = lax.axis_index("slab")
    pencil = lax.axis_index("pencil")
    slabs = lax.axis_size("slab")
    pencils = lax.axis_size("pencil")

    load_vol = pltpu.make_async_copy(vol_hbm, vol, sem_in.at[0])
    load_w1 = pltpu.make_async_copy(w1_hbm, w1r, sem_in.at[1])
    load_w2 = pltpu.make_async_copy(w2_hbm, w2r, sem_in.at[2])
    load_cot = pltpu.make_async_copy(cot_hbm, cot, sem_in.at[3])
    for load in (load_vol, load_w1, load_w2, load_cot):
        load.start()

    def exists(dx, dy):
        x = slab + dx
        y = pencil + dy
        ok = None
        if dx:
            ok = (x >= 0) & (x < slabs)
        if dy:
            oky = (y >= 0) & (y < pencils)
            ok = oky if ok is None else ok & oky
        return ok

    low = lax.rem(slab, LOW)
    group_z = (
        LOW * pencils,
        low * pencils + pencil,
        lambda i: (slab - low + i // pencils, lax.rem(i, pencils)),
    )
    group_xy = (slabs // LOW, slab // LOW, lambda i: (i * LOW + low, pencil))
    group_low = (LOW, low, lambda i: (slab - low + i, pencil))

    barrier = pltpu.get_barrier_semaphore()
    arrivals = 0
    for dx, dy in SIDES:
        ok = exists(dx, dy)
        arrivals = arrivals + ok.astype(jnp.int32)

        @pl.when(ok)
        def _():
            pl.semaphore_signal(
                barrier, inc=1, device_id=(slab + dx, pencil + dy), device_id_type=MESH
            )

    for size, me, device in (group_z, group_xy):
        arrivals = arrivals + (size - 1)
        for d in range(1, size):
            pl.semaphore_signal(
                barrier, inc=1, device_id=device(lax.rem(me + d, size)), device_id_type=MESH
            )

    def volume_refs(dx, dy):
        if dy == 0:
            return vol.at[:, 3 if dx == 1 else 0], xrecv.at[0 if dx == 1 else 1]
        src = ypack.at[1 if dy == 1 else 0]
        side = 0 if dy == 1 else 1
        if dx == 0:
            return src, yrecv.at[side]
        return src, crecv.at[2 * (0 if dx == 1 else 1) + side]

    def field_refs(field, lo, hi, dx, dy):
        sx = {1: 2, -1: 1, 0: pl.ds(1, 2)}[dx]
        tx = {1: 0, -1: 3, 0: pl.ds(1, 2)}[dx]
        sy = {1: 8, -1: 1, 0: pl.ds(1, 8)}[dy]
        ty = {1: 0, -1: 9, 0: pl.ds(1, 8)}[dy]
        rows = pl.ds(lo, hi - lo)
        return field.at[sx, sy, rows], field.at[tx, ty, rows]

    pooled_refs = functools.partial(field_refs, PS, 32, 64)
    grad_refs = functools.partial(field_refs, GS, 64, 128)

    for dx, dy in SIDES:

        @pl.when(jnp.logical_not(exists(-dx, -dy)))
        def _():
            for refs in (volume_refs, pooled_refs, grad_refs):
                target = refs(dx, dy)[1]
                target[...] = jnp.zeros(target.shape, BF16)

    def halo_copy(phase, k, refs):
        dx, dy = SIDES[k]
        src, dst = refs(dx, dy)
        return pltpu.make_async_remote_copy(
            src_ref=src,
            dst_ref=dst,
            send_sem=halo_send.at[phase, k],
            recv_sem=halo_recv.at[phase, k],
            device_id=(slab + dx, pencil + dy),
            device_id_type=MESH,
        )

    def halo_start(phase, refs):
        for k, (dx, dy) in enumerate(SIDES):

            @pl.when(exists(dx, dy))
            def _():
                halo_copy(phase, k, refs).start()

    def halo_wait(phase, refs):
        for k, (dx, dy) in enumerate(SIDES):

            @pl.when(exists(dx, dy))
            def _():
                halo_copy(phase, k, refs).wait_send()

            @pl.when(exists(-dx, -dy))
            def _():
                halo_copy(phase, k, refs).wait_recv()

    load_vol.wait()
    edges = pick(32, 256, lambda r, c: c == ((r & 15) << 4) + 15 * (r >> 4))
    packed = dot(edges, vol[...].reshape(256, 256)).astype(BF16)
    ypack[0] = packed[:16]
    ypack[1] = packed[16:]

    shift_1 = pick(256, 512, lambda r, c: r == jnp.where(c < 256, c - 1, c - 255))

    def shifted(block):
        sides = dot(block, shift_1).astype(BF16)
        return sides[:, :256], block, sides[:, 256:]

    def order(r, c):
        slot = r & 15
        return (slot < 12) & (c == ((slot >> 2) << 6) + ((slot & 3) << 4) + (r >> 4))

    def order_edge(r, c):
        slot = r & 15
        return (slot < 12) & (c == ((slot >> 2) << 4) + ((slot & 3) << 2) + (r >> 4))

    to_rows = pick(256, 192, order)
    to_edge = pick(64, 48, order_edge)

    def rows_of(parts, lo, hi):
        return jnp.concatenate([part[lo:hi] for part in parts], axis=0)

    local = shifted(jnp.concatenate([vol[:, x].reshape(64, 256) for x in range(4)], axis=0))
    for x in range(4):
        rows = dot(to_rows, rows_of(local, 64 * x, 64 * x + 64)).astype(BF16)
        V[x + 1, 1:17] = rows.reshape(16, 16, 256)

    for yo in range(2):
        MAPS[yo] = expand_map(yo)
    load_w1.wait()
    eye = pick(32, 32, lambda r, c: r == c)
    w1f = dot_lanes(eye, eight_rows(w1r[...])).astype(BF16)
    w1p = jnp.concatenate([dot(w1f, MAPS[yo]).astype(BF16) for yo in range(2)], axis=0)

    pl.semaphore_wait(barrier, arrivals)
    halo_start(0, volume_refs)

    def window(x, y1):
        return V[pl.ds(x, 3), pl.ds(2 * y1, 4)].reshape(192, 256)

    def first_cells(x, y1):
        act, slope = act_slope(dot(w1p, window(x, y1)))
        SL[x, y1] = slope
        return act[:32] + act[32:]

    def inner(i, carry):
        for x in (1, 2):
            for j in range(2):
                CELLS[x - 1, 1 + 2 * i + j] = first_cells(x, 1 + 2 * i + j)
        return carry

    lax.fori_loop(0, 3, inner, 0)

    def pairs(r, c):
        return (r >> 1) == (c & 127) + (c >> 7) - 1

    pool_1[...] = pick(256, 384, pairs)
    shift_2[...] = pick(128, 256, lambda r, c: r == jnp.where(c < 128, c - 1, c - 127))
    spread_1[...] = pick(128, 256, lambda r, c: r == (c >> 1))

    halo_wait(0, volume_refs)
    arrived = shifted(
        jnp.concatenate(
            [xrecv[s].reshape(64, 256) for s in range(2)]
            + [yrecv[s] for s in range(2)]
            + [crecv[s] for s in range(4)],
            axis=0,
        )
    )
    for side, x in ((0, 0), (1, 5)):
        rows = dot(to_rows, rows_of(arrived, 64 * side, 64 * side + 64)).astype(BF16)
        V[x, 1:17] = rows.reshape(16, 16, 256)
    for side, y in ((0, 0), (1, 17)):
        at = 128 + 16 * side
        V[1:5, y] = dot(to_edge, rows_of(arrived, at, at + 16)).astype(BF16).reshape(4, 16, 256)
        at = 160 + 16 * side
        V[0, y] = dot(to_edge[48:], rows_of(arrived, at, at + 16)).astype(BF16)
        at = 192 + 16 * side
        V[5, y] = dot(to_edge[:16], rows_of(arrived, at, at + 16)).astype(BF16)

    for x in (1, 2):
        for y1 in (0, 7):
            CELLS[x - 1, y1] = first_cells(x, y1)

    def outer(i, carry):
        for x in (0, 3):
            for j in range(2):
                CELLS[x // 2, 2 * i + j] += first_cells(x, 2 * i + j)
        return carry

    lax.fori_loop(0, 4, outer, 0)

    for x1 in range(2):
        parts = split(CELLS[x1].reshape(256, 256), 2)
        pooled = (0.125 * joined(dot(parts, pool_1[...]), 2)).astype(BF16)
        for c in range(3):
            PS[x1 + 1, 1:9, 32 * c : 32 * c + 32] = pooled[:, 128 * c : 128 * c + 128].reshape(
                8, 32, 128
            )

    halo_start(1, pooled_refs)

    load_w2.wait()
    eye = pick(64, 64, lambda r, c: r == c)
    for a in range(3):
        taps_a = w2r[9 * a : 9 * a + 9].reshape(288, 64)
        W2A[64 * (2 - a) : 64 * (2 - a) + 64] = dot_lanes(eye, taps_a).astype(BF16)
        W2B[32 * (2 - a) : 32 * (2 - a) + 32] = jnp.concatenate(
            [w2r[26 - 9 * a - j] for j in range(9)], axis=1
        )
    spread_2 = pick(64, 128, lambda r, c: r == (c >> 1))
    load_cot.wait()
    to_y2 = pick(256, 512, lambda r, c: c == ((r & 63) << 3) + (r >> 6))
    seeds = dot(to_y2, eight_rows(cot[...])).astype(BF16)
    SEED[...] = (0.125 * dot(seeds, spread_2)).reshape(4, 64, 128)

    def spread_sides(field, ch, xs, ys):
        cells = field[xs, ys, ch : 2 * ch]
        shape = cells.shape
        sides = dot(cells.reshape(-1, 128), shift_2[...]).astype(BF16)
        field[xs, ys, 0:ch] = sides[:, :128].reshape(shape)
        field[xs, ys, 2 * ch :] = sides[:, 128:].reshape(shape)

    def spread_edges(field, ch):
        for x in (0, 3):
            spread_sides(field, ch, x, slice(0, 10))
        for y in (0, 9):
            spread_sides(field, ch, slice(1, 3), y)

    def taps(field, x, y2):
        depth = 3 * field.shape[2]
        one = field[x, pl.ds(2 * y2, 3)].reshape(depth, 128)
        two = field[x, pl.ds(2 * y2 + 1, 3)].reshape(depth, 128)
        return jnp.concatenate([one, two], axis=1)

    def both_rows(field, weights, ch, y2):
        whole = dot(weights[ch : 3 * ch], taps(field, 1, y2))
        whole = whole + dot(weights[0 : 2 * ch], taps(field, 2, y2))
        first = dot(weights[2 * ch : 3 * ch], taps(field, 0, y2))
        last = dot(weights[0:ch], taps(field, 3, y2))
        return whole + jnp.concatenate([first, last], axis=0)

    halo_wait(1, pooled_refs)
    spread_edges(PS, 32)

    def second_block(i, carry):
        for j in range(2):
            y2 = 2 * i + j
            act, slope = act_slope(both_rows(PS, W2A, 64, y2))
            total = act[:64] + act[64:]
            TOT[y2] = total[:, :128] + total[:, 128:]
            seed = jnp.concatenate([SEED[y2]] * 2, axis=0)
            grad = (slope * jnp.concatenate([seed, seed], axis=1)).astype(BF16)
            G2[y2] = grad
            for x1 in range(2):
                for yo in range(2):
                    cells = grad[64 * x1 : 64 * x1 + 64, 128 * yo : 128 * yo + 128]
                    GS[x1 + 1, 2 * y2 + 1 + yo, 64:128] = cells
        return carry

    lax.fori_loop(0, 2, second_block, 0)
    halo_start(2, grad_refs)

    groups = dw2.shape[0]
    share = 64 // groups
    dw2[...] = jnp.zeros_like(dw2)

    def second_grad(y2, carry):
        terms = [None] * 3
        for x in range(4):
            lo, hi = (0 if x < 3 else 64), (128 if x > 0 else 64)
            part = dot_lanes(G2[y2, lo:hi], taps(PS, x, y2))
            for x1 in range(2):
                if 0 <= x - x1 < 3:
                    piece = part[64 * x1 - lo : 64 * x1 - lo + 64]
                    old = terms[x - x1]
                    terms[x - x1] = piece if old is None else old + piece
        for a in range(3):
            for g in range(groups):
                dw2[g, a] += terms[a][share * g : share * g + share]
        return carry

    lax.fori_loop(0, 4, second_grad, 0)
    part2[...] = dw2[...].astype(BF16)

    def group_copies(group, src_of, dst_of, sems, sends=None, gets=None):
        size, me, device = group

        def copy(d, slot):
            peer = lax.rem(me + d, size)
            return pltpu.make_async_remote_copy(
                src_ref=src_of(peer),
                dst_ref=dst_of(peer if slot is None else slot),
                send_sem=sems.at[0, d],
                recv_sem=sems.at[1, peer if slot is None else slot],
                device_id=device(peer),
                device_id_type=MESH,
            )

        def each(allowed, act):
            for d in range(1, size):
                pl.when(allowed(lax.rem(me + d, size)))(functools.partial(act, d))

        def start():
            each(sends, lambda d: copy(d, me).start())

        def wait():
            each(sends, lambda d: copy(d, me).wait_send())
            each(gets, lambda d: copy(d, None).wait_recv())

        return start, wait

    def group_gather(group, slots, sems):
        size, me, device = group

        def start():
            for d in range(1, size):
                pltpu.make_async_remote_copy(
                    src_ref=slots.at[me],
                    dst_ref=slots.at[me],
                    send_sem=sems.at[0],
                    recv_sem=sems.at[1],
                    device_id=device(lax.rem(me + d, size)),
                    device_id_type=MESH,
                ).start()

        def wait():
            others = slots.at[pl.ds(0, size - 1)]
            for sem in (sems.at[0], sems.at[1]):
                pltpu.make_async_copy(others, others, sem).wait()

        return start, wait

    owner = low < 3
    mine = jnp.minimum(low, 2)
    start_a, wait_a = group_copies(
        group_z,
        lambda i: part2.at[lax.rem(i, pencils), jnp.minimum(i // pencils, 2)],
        lambda slot: sum_a.at[slot],
        sem_a,
        sends=lambda i: i // pencils < 3,
        gets=lambda i: owner,
    )
    start_b, wait_b = group_gather(group_xy, sum_b, sem_b)
    start_c, wait_c = group_copies(
        group_low,
        lambda i: sum_c.at[low],
        lambda slot: sum_c.at[slot],
        sem_c,
        sends=lambda i: owner,
        gets=lambda i: i < 3,
    )
    start_z, wait_z = group_gather(group_z, sum_1.at[0], sem_1.at[0])
    start_xy, wait_xy = group_gather(group_xy, sum_1.at[1], sem_1.at[1])

    def total_of(slots, size):
        total = slots[0].astype(F32)
        for i in range(1, size):
            total = total + slots[i].astype(F32)
        return total

    start_a()

    for x in (1, 2):
        spread_sides(GS, 64, x, slice(1, 9))
    pool_2 = pick(128, 64, lambda r, c: (r >> 1) == c)
    pooled = 0.125 * joined(dot(split(TOT[...].reshape(256, 128), 2), pool_2), 2)
    from_y2 = pick(512, 256, lambda r, c: r == ((c & 63) << 3) + (c >> 6))
    pooled = dot(from_y2, pooled.astype(BF16)).reshape(64, 8, 64)
    p2_out[...] = pooled[:, :4].astype(BF16)

    halo_wait(2, grad_refs)
    spread_edges(GS, 64)

    def first_back(i, carry):
        for j in range(2):
            y2 = 2 * i + j
            back = both_rows(GS, W2B, 32, y2)
            for x1 in range(2):
                for yo in range(2):
                    cells = back[32 * x1 : 32 * x1 + 32, 128 * yo : 128 * yo + 128]
                    BACK[x1, 2 * y2 + yo] = cells
        return carry

    lax.fori_loop(0, 2, first_back, 0)
    for x1 in range(2):
        parts = split(BACK[x1].reshape(256, 128), 2)
        CELLS[x1] = (0.125 * joined(dot(parts, spread_1[...]), 2)).reshape(8, 32, 256)

    dw1[...] = jnp.zeros_like(dw1)

    def first_grad(y1, carry):
        total = None
        for x in range(4):
            seed = jnp.concatenate([CELLS[x // 2, y1]] * 2, axis=0)
            term = dot_lanes((SL[x, y1] * seed).astype(BF16), window(x, y1))
            total = term if total is None else total + term
        dw1[...] += total
        return carry

    lax.fori_loop(0, 8, first_grad, 0)

    folded = None
    for yo in range(2):
        term = joined(dot_lanes(split(dw1[32 * yo : 32 * yo + 32], 3), MAPS[yo]), 3)
        folded = term if folded is None else folded + term

    sum_1[0, group_z[1]] = folded.astype(BF16)
    start_z()
    wait_a()

    @pl.when(owner)
    def _():
        sum_a[group_z[1]] = part2[pencil, mine]
        sum_b[group_xy[1]] = total_of(sum_a, group_z[0]).astype(BF16)
        start_b()

    wait_z()
    sum_1[1, group_xy[1]] = total_of(sum_1.at[0], group_z[0]).astype(BF16)
    start_xy()

    @pl.when(owner)
    def _():
        wait_b()
        sum_c[low] = total_of(sum_b, group_xy[0])

    start_c()
    wait_c()
    for a in range(3):
        for j in range(9):
            g2_out[9 * a + j] = sum_c[a, :, 32 * j : 32 * j + 32]
    wait_xy()
    total = total_of(sum_1.at[1], group_xy[0]).T
    for tap in range(27):
        g1_out[tap] = total[8 * tap : 8 * tap + 4]


def write_out(*refs):
    count = len(refs) // 2
    sems = refs[-1]
    copies = [pltpu.make_async_copy(refs[i], refs[count + i], sems.at[i]) for i in range(count)]
    for copy in copies:
        copy.start()
    for copy in copies:
        copy.wait()


def solution(mesh):
    pencils = mesh.shape["pencil"]
    share = 64 // pencils
    size_z = LOW * pencils
    size_xy = mesh.shape["slab"] // LOW
    most = max(size_z, size_xy)

    def per_device(volume, weight_one, weight_two, cotangent):
        w1 = weight_one.transpose(1, 2, 0)
        w2 = weight_two.transpose(1, 2, 0)
        cot = cotangent.reshape(64, 4, 64)
        vmem = pl.BlockSpec(memory_space=pltpu.VMEM)
        hbm = pl.BlockSpec(memory_space=pltpu.HBM)
        shapes = (
            pltpu.VMEM((64, 4, 64), BF16),
            pltpu.VMEM((27, 4, 32), F32),
            pltpu.VMEM((27, share, 32), F32),
        )
        results = pl.pallas_call(
            kernel,
            out_shape=shapes,
            in_specs=[hbm] * 4,
            out_specs=(vmem,) * 3,
            scratch_shapes=[
                pltpu.VMEM((4, 4, 16, 256), BF16),
                pltpu.VMEM((27, 4, 32), BF16),
                pltpu.VMEM((27, 32, 64), BF16),
                pltpu.VMEM((64, 4, 64), BF16),
                pltpu.VMEM((6, 18, 16, 256), BF16),
                pltpu.VMEM((4, 10, 96, 128), BF16),
                pltpu.VMEM((4, 10, 192, 128), BF16),
                pltpu.VMEM((4, 8, 64, 256), F32),
                pltpu.VMEM((2, 8, 32, 256), F32),
                pltpu.VMEM((4, 64, 128), F32),
                pltpu.VMEM((4, 64, 128), F32),
                pltpu.VMEM((4, 128, 256), BF16),
                pltpu.VMEM((2, 8, 32, 128), F32),
                pltpu.VMEM((192, 288), BF16),
                pltpu.VMEM((96, 576), BF16),
                pltpu.VMEM((2, 216, 192), BF16),
                pltpu.VMEM((256, 384), BF16),
                pltpu.VMEM((128, 256), BF16),
                pltpu.VMEM((128, 256), BF16),
                pltpu.VMEM((2, 16, 256), BF16),
                pltpu.VMEM((2, 4, 16, 256), BF16),
                pltpu.VMEM((2, 16, 256), BF16),
                pltpu.VMEM((4, 16, 256), BF16),
                pltpu.VMEM((64, 192), F32),
                pltpu.VMEM((pencils, 3, share, 288), F32),
                pltpu.VMEM((pencils, 3, share, 288), BF16),
                pltpu.VMEM((size_z, share, 288), BF16),
                pltpu.VMEM((size_xy, share, 288), BF16),
                pltpu.VMEM((LOW, share, 288), F32),
                pltpu.VMEM((2, most, 32, 216), BF16),
                pltpu.SemaphoreType.DMA((4,)),
                pltpu.SemaphoreType.DMA((3, 8)),
                pltpu.SemaphoreType.DMA((3, 8)),
                pltpu.SemaphoreType.DMA((2, size_z)),
                pltpu.SemaphoreType.DMA((2,)),
                pltpu.SemaphoreType.DMA((2, LOW)),
                pltpu.SemaphoreType.DMA((2, 2)),
            ],
            compiler_params=pltpu.CompilerParams(
                collective_id=0, has_side_effects=True, vmem_limit_bytes=56 * 2**20
            ),
        )(volume, w1, w2, cot)
        pooled, grad_one, grad_two = pl.pallas_call(
            write_out,
            out_shape=tuple(jax.ShapeDtypeStruct(s.shape, s.dtype) for s in shapes),
            in_specs=[vmem] * 3,
            out_specs=(hbm,) * 3,
            scratch_shapes=[pltpu.SemaphoreType.DMA((3,))],
        )(*results)
        return (
            pooled.reshape(64, 1, 4, 64),
            grad_one.transpose(2, 0, 1),
            grad_two.transpose(1, 0, 2),
        )

    in_specs = (P(None, "slab", "pencil", None), P(), P(), P(None, "slab", "pencil", None))
    out_specs = (P(None, "slab", "pencil", None), P(), P("pencil", None, None))
    return jax.shard_map(
        per_device, mesh=mesh, in_specs=in_specs, out_specs=out_specs, check_vma=False
    )
```

```python
import functools

import jax
import jax.numpy as jnp
from jax import lax
from jax.experimental import pallas as pl
from jax.experimental.pallas import tpu as pltpu
from jax.sharding import PartitionSpec as P

MESH = pl.DeviceIdType.MESH
LOW = 4
F32 = jnp.float32
BF16 = jnp.bfloat16
SIDES = ((1, 1), (1, -1), (-1, 1), (-1, -1), (1, 0), (-1, 0), (0, 1), (0, -1))


def pick(rows, cols, hit):
    r = lax.broadcasted_iota(jnp.int32, (rows, cols), 0)
    c = lax.broadcasted_iota(jnp.int32, (rows, cols), 1)
    return jnp.where(hit(r, c), 1.0, 0.0).astype(BF16)


def dot(a, b):
    return jnp.dot(a, b, preferred_element_type=F32)


def dot_lanes(a, b):
    return lax.dot_general(a, b, (((1,), (1,)), ((), ())), preferred_element_type=F32)


def split(value, count):
    parts = []
    for _ in range(count):
        part = value.astype(BF16)
        parts.append(part)
        value = value - part.astype(F32)
    return jnp.concatenate(parts, axis=0)


def joined(value, count):
    rows = value.shape[0] // count
    total = value[:rows]
    for i in range(1, count):
        total = total + value[rows * i : rows * i + rows]
    return total


def act_slope(pre):
    t = jnp.tanh(0.5 * pre)
    act = 0.3 * pre + 0.7 * (jnp.maximum(pre, 0.0) - jnp.log(0.5 + 0.5 * jnp.abs(t)))
    return act, 0.65 + 0.35 * t


def expand_map(yo, rows, slots):
    def hit(r, j):
        b = ((j >> 4) & 3) - yo
        slot = j & 15
        row = slots * (9 * (j >> 6) + 3 * b + (slot >> 2)) + (slot & 3)
        return (b >= 0) & (b < 3) & (slot < 12) & (r == row)

    return pick(rows, 192, hit)


def eight_rows(value):
    value = value.astype(F32)
    value = jnp.concatenate([value, value], axis=1)
    return value.reshape(-1, value.shape[2]).astype(BF16)


def kernel(
    vol_hbm,
    w1_hbm,
    w2_hbm,
    cot_hbm,
    p2_out,
    g1_out,
    g2_out,
    vol,
    w1r,
    w2r,
    cot,
    V,
    PS,
    GS,
    SL,
    CELLS,
    TOT,
    SEED,
    G2,
    BACK,
    OUTER,
    face_x,
    face_y,
    corner,
    W2A,
    W2B,
    MAPS,
    pool_1,
    shift_2,
    spread_1,
    ypack,
    xrecv,
    yrecv,
    crecv,
    dw1,
    dw2,
    part2,
    sum_a,
    sum_b,
    sum_c,
    sum_1,
    sem_in,
    halo_send,
    halo_recv,
    sem_a,
    sem_b,
    sem_c,
    sem_1,
):
    slab = lax.axis_index("slab")
    pencil = lax.axis_index("pencil")
    slabs = lax.axis_size("slab")
    pencils = lax.axis_size("pencil")

    load_vol = pltpu.make_async_copy(vol_hbm, vol, sem_in.at[0])
    load_w1 = pltpu.make_async_copy(w1_hbm, w1r, sem_in.at[1])
    load_w2 = pltpu.make_async_copy(w2_hbm, w2r, sem_in.at[2])
    load_cot = pltpu.make_async_copy(cot_hbm, cot, sem_in.at[3])
    for load in (load_vol, load_w1, load_w2, load_cot):
        load.start()

    def exists(dx, dy):
        x = slab + dx
        y = pencil + dy
        ok = None
        if dx:
            ok = (x >= 0) & (x < slabs)
        if dy:
            oky = (y >= 0) & (y < pencils)
            ok = oky if ok is None else ok & oky
        return ok

    low = lax.rem(slab, LOW)
    group_z = (
        LOW * pencils,
        low * pencils + pencil,
        lambda i: (slab - low + i // pencils, lax.rem(i, pencils)),
    )
    group_xy = (slabs // LOW, slab // LOW, lambda i: (i * LOW + low, pencil))
    group_low = (LOW, low, lambda i: (slab - low + i, pencil))

    barrier = pltpu.get_barrier_semaphore()
    arrivals = 0
    for dx, dy in SIDES:
        ok = exists(dx, dy)
        arrivals = arrivals + ok.astype(jnp.int32)

        @pl.when(ok)
        def _():
            pl.semaphore_signal(
                barrier, inc=1, device_id=(slab + dx, pencil + dy), device_id_type=MESH
            )

    for size, me, device in (group_z, group_xy):
        arrivals = arrivals + (size - 1)
        for d in range(1, size):
            pl.semaphore_signal(
                barrier, inc=1, device_id=device(lax.rem(me + d, size)), device_id_type=MESH
            )

    def volume_refs(dx, dy):
        if dy == 0:
            return vol.at[:, 3 if dx == 1 else 0], xrecv.at[0 if dx == 1 else 1]
        src = ypack.at[1 if dy == 1 else 0]
        side = 0 if dy == 1 else 1
        if dx == 0:
            return src, yrecv.at[side]
        return src, crecv.at[2 * (0 if dx == 1 else 1) + side]

    def pooled_refs(dx, dy):
        sx = {1: 2, -1: 1, 0: pl.ds(1, 2)}[dx]
        tx = {1: 0, -1: 3, 0: pl.ds(1, 2)}[dx]
        sy = {1: 8, -1: 1, 0: pl.ds(1, 8)}[dy]
        ty = {1: 0, -1: 9, 0: pl.ds(1, 8)}[dy]
        rows = pl.ds(32, 32)
        return PS.at[sx, sy, rows], PS.at[tx, ty, rows]

    def grad_refs(dx, dy):
        src = OUTER.at[
            {1: 3, -1: 0, 0: pl.ds(1, 2)}[dx], {1: 9, -1: 0, 0: pl.ds(1, 8)}[dy]
        ]
        side_x = 0 if dx == 1 else 1
        side_y = 0 if dy == 1 else 1
        if dy == 0:
            return src, face_x.at[side_x]
        if dx == 0:
            return src, face_y.at[side_y]
        return src, corner.at[2 * side_x + side_y]

    for dx, dy in SIDES:

        @pl.when(jnp.logical_not(exists(-dx, -dy)))
        def _():
            for refs in (volume_refs, pooled_refs, grad_refs):
                target = refs(dx, dy)[1]
                target[...] = jnp.zeros(target.shape, BF16)

    def halo_copy(phase, k, refs):
        dx, dy = SIDES[k]
        src, dst = refs(dx, dy)
        return pltpu.make_async_remote_copy(
            src_ref=src,
            dst_ref=dst,
            send_sem=halo_send.at[phase, k],
            recv_sem=halo_recv.at[phase, k],
            device_id=(slab + dx, pencil + dy),
            device_id_type=MESH,
        )

    def halo_start(phase, refs):
        for k, (dx, dy) in enumerate(SIDES):

            @pl.when(exists(dx, dy))
            def _():
                halo_copy(phase, k, refs).start()

    def halo_wait(phase, refs):
        for k, (dx, dy) in enumerate(SIDES):

            @pl.when(exists(dx, dy))
            def _():
                halo_copy(phase, k, refs).wait_send()

            @pl.when(exists(-dx, -dy))
            def _():
                halo_copy(phase, k, refs).wait_recv()

    for y in (0, 1, 10, 11):
        GS[:, y] = jnp.zeros((2, 192, 128), BF16)

    load_vol.wait()
    edges = pick(32, 256, lambda r, c: c == ((r & 15) << 4) + 15 * (r >> 4))
    packed = dot(edges, vol[...].reshape(256, 256)).astype(BF16)
    ypack[0] = packed[:16]
    ypack[1] = packed[16:]

    shift_1 = pick(256, 512, lambda r, c: r == jnp.where(c < 256, c - 1, c - 255))

    def shifted(block):
        sides = dot(block, shift_1).astype(BF16)
        return sides[:, :256], block, sides[:, 256:]

    def order(r, c):
        slot = r & 15
        return (slot < 12) & (c == ((slot >> 2) << 6) + ((slot & 3) << 4) + (r >> 4))

    def order_edge(r, c):
        slot = r & 15
        return (slot < 12) & (c == ((slot >> 2) << 4) + ((slot & 3) << 2) + (r >> 4))

    to_rows = pick(256, 192, order)
    to_edge = pick(64, 48, order_edge)

    def rows_of(parts, lo, hi):
        return jnp.concatenate([part[lo:hi] for part in parts], axis=0)

    local = shifted(jnp.concatenate([vol[:, x].reshape(64, 256) for x in range(4)], axis=0))
    for x in range(4):
        rows = dot(to_rows, rows_of(local, 64 * x, 64 * x + 64)).astype(BF16)
        V[x + 1, 1:17] = rows.reshape(16, 16, 256)

    load_w1.wait()
    eye = pick(32, 32, lambda r, c: r == c)
    w1f = dot_lanes(eye, eight_rows(w1r[...])).astype(BF16)
    w1p = jnp.concatenate(
        [dot(w1f, expand_map(yo, 216, 8)).astype(BF16) for yo in range(2)], axis=0
    )

    pl.semaphore_wait(barrier, arrivals)
    halo_start(0, volume_refs)

    def window(x, y1):
        return V[pl.ds(x, 3), pl.ds(2 * y1, 4)].reshape(192, 256)

    def first_cells(x, y1):
        act, slope = act_slope(dot(w1p, window(x, y1)))
        SL[x, y1] = slope
        return act[:32] + act[32:]

    def inner(i, carry):
        for x in (1, 2):
            for j in range(2):
                CELLS[x - 1, 1 + 2 * i + j] = first_cells(x, 1 + 2 * i + j)
        return carry

    lax.fori_loop(0, 3, inner, 0)

    def pairs(r, c):
        return (r >> 1) == (c & 127) + (c >> 7) - 1

    pool_1[...] = pick(256, 384, pairs)
    shift_2[...] = pick(128, 256, lambda r, c: r == jnp.where(c < 128, c - 1, c - 127))
    spread_1[...] = pick(128, 256, lambda r, c: r == (c >> 1))

    halo_wait(0, volume_refs)
    arrived = shifted(
        jnp.concatenate(
            [xrecv[s].reshape(64, 256) for s in range(2)]
            + [yrecv[s] for s in range(2)]
            + [crecv[s] for s in range(4)],
            axis=0,
        )
    )
    for side, x in ((0, 0), (1, 5)):
        rows = dot(to_rows, rows_of(arrived, 64 * side, 64 * side + 64)).astype(BF16)
        V[x, 1:17] = rows.reshape(16, 16, 256)
    for side, y in ((0, 0), (1, 17)):
        at = 128 + 16 * side
        V[1:5, y] = dot(to_edge, rows_of(arrived, at, at + 16)).astype(BF16).reshape(4, 16, 256)
        at = 160 + 16 * side
        V[0, y] = dot(to_edge[48:], rows_of(arrived, at, at + 16)).astype(BF16)
        at = 192 + 16 * side
        V[5, y] = dot(to_edge[:16], rows_of(arrived, at, at + 16)).astype(BF16)

    for x in (1, 2):
        for y1 in (0, 7):
            CELLS[x - 1, y1] = first_cells(x, y1)

    def outer(i, carry):
        for x in (0, 3):
            for j in range(2):
                CELLS[x // 2, 2 * i + j] += first_cells(x, 2 * i + j)
        return carry

    lax.fori_loop(0, 4, outer, 0)

    for x1 in range(2):
        parts = split(CELLS[x1].reshape(256, 256), 2)
        pooled = (0.125 * joined(dot(parts, pool_1[...]), 2)).astype(BF16)
        for c in range(3):
            PS[x1 + 1, 1:9, 32 * c : 32 * c + 32] = pooled[:, 128 * c : 128 * c + 128].reshape(
                8, 32, 128
            )

    halo_start(1, pooled_refs)

    load_w2.wait()
    for yo in range(2):
        MAPS[yo] = expand_map(yo, 128, 4)
    eye = pick(64, 64, lambda r, c: r == c)
    for a in range(3):
        taps_a = w2r[9 * a : 9 * a + 9].reshape(288, 64)
        W2A[64 * (2 - a) : 64 * (2 - a) + 64] = dot_lanes(eye, taps_a).astype(BF16)
        W2B[32 * (2 - a) : 32 * (2 - a) + 32] = jnp.concatenate(
            [w2r[26 - 9 * a - j] for j in range(9)], axis=1
        )
    spread_2 = pick(64, 128, lambda r, c: r == (c >> 1))
    load_cot.wait()
    to_y2 = pick(256, 512, lambda r, c: c == ((r & 63) << 3) + (r >> 6))
    seeds = dot(to_y2, eight_rows(cot[...])).astype(BF16)
    SEED[...] = (0.125 * dot(seeds, spread_2)).reshape(4, 64, 128)

    def spread_edges(xs, ys):
        cells = PS[xs, ys, 32:64]
        shape = cells.shape
        sides = dot(cells.reshape(-1, 128), shift_2[...]).astype(BF16)
        PS[xs, ys, 0:32] = sides[:, :128].reshape(shape)
        PS[xs, ys, 64:96] = sides[:, 128:].reshape(shape)

    def taps(field, x, y2):
        depth = 3 * field.shape[2]
        one = field[x, pl.ds(2 * y2, 3)].reshape(depth, 128)
        two = field[x, pl.ds(2 * y2 + 1, 3)].reshape(depth, 128)
        return jnp.concatenate([one, two], axis=1)

    def second_conv(y2):
        whole = dot(W2A[64:192], taps(PS, 1, y2)) + dot(W2A[0:128], taps(PS, 2, y2))
        first = dot(W2A[128:192], taps(PS, 0, y2))
        last = dot(W2A[0:64], taps(PS, 3, y2))
        return whole + jnp.concatenate([first, last], axis=0)

    halo_wait(1, pooled_refs)
    for x in (0, 3):
        spread_edges(x, slice(0, 10))
    for y in (0, 9):
        spread_edges(slice(1, 3), y)

    def second_block(i, carry):
        for j in range(2):
            y2 = 2 * i + j
            act, slope = act_slope(second_conv(y2))
            total = act[:64] + act[64:]
            TOT[y2] = total[:, :128] + total[:, 128:]
            seed = jnp.concatenate([SEED[y2]] * 2, axis=0)
            grad = (slope * jnp.concatenate([seed, seed], axis=1)).astype(BF16)
            G2[y2] = grad
            for yo in range(2):
                cells = grad[:, 128 * yo : 128 * yo + 128]
                for x1 in range(2):
                    GS[x1, 2 * y2 + yo + 2, 64:128] = cells[64 * x1 : 64 * x1 + 64]
        return carry

    lax.fori_loop(0, 2, second_block, 0)
    for x1 in range(2):
        sides = dot(GS[x1, 2:10, 64:128].reshape(512, 128), shift_2[...]).astype(BF16)
        GS[x1, 2:10, 0:64] = sides[:, :128].reshape(8, 64, 128)
        GS[x1, 2:10, 128:192] = sides[:, 128:].reshape(8, 64, 128)

    for p in range(5):
        one = dot(W2B[...], taps(GS, 0, p))
        two = dot(W2B[...], taps(GS, 1, p))
        rows = (one[:32], one[32:64] + two[:32], one[64:] + two[32:64], two[64:])
        for yo in range(2):
            y = 2 * p + yo
            for x in range(4):
                cells = rows[x][:, 128 * yo : 128 * yo + 128]
                if 0 < x < 3 and 0 < y < 9:
                    BACK[x - 1, y - 1] = cells
                else:
                    OUTER[x, y] = cells.astype(BF16)
    halo_start(2, grad_refs)

    groups = dw2.shape[0]
    share = 64 // groups
    dw2[...] = jnp.zeros_like(dw2)

    def second_grad(y2, carry):
        terms = [None] * 3
        for x in range(4):
            lo, hi = (0 if x < 3 else 64), (128 if x > 0 else 64)
            part = dot_lanes(G2[y2, lo:hi], taps(PS, x, y2))
            for x1 in range(2):
                if 0 <= x - x1 < 3:
                    piece = part[64 * x1 - lo : 64 * x1 - lo + 64]
                    old = terms[x - x1]
                    terms[x - x1] = piece if old is None else old + piece
        for a in range(3):
            for g in range(groups):
                dw2[g, a] += terms[a][share * g : share * g + share]
        return carry

    lax.fori_loop(0, 4, second_grad, 0)
    part2[...] = dw2[...].astype(BF16)

    def group_copies(group, src_of, dst_of, sems, sends=None, gets=None):
        size, me, device = group

        def copy(d, slot):
            peer = lax.rem(me + d, size)
            return pltpu.make_async_remote_copy(
                src_ref=src_of(peer),
                dst_ref=dst_of(peer if slot is None else slot),
                send_sem=sems.at[0, d],
                recv_sem=sems.at[1, peer if slot is None else slot],
                device_id=device(peer),
                device_id_type=MESH,
            )

        def each(allowed, act):
            for d in range(1, size):
                pl.when(allowed(lax.rem(me + d, size)))(functools.partial(act, d))

        def start():
            each(sends, lambda d: copy(d, me).start())

        def wait():
            each(sends, lambda d: copy(d, me).wait_send())
            each(gets, lambda d: copy(d, None).wait_recv())

        return start, wait

    def group_gather(group, slots, sems):
        size, me, device = group

        def start():
            for d in range(1, size):
                pltpu.make_async_remote_copy(
                    src_ref=slots.at[me],
                    dst_ref=slots.at[me],
                    send_sem=sems.at[0],
                    recv_sem=sems.at[1],
                    device_id=device(lax.rem(me + d, size)),
                    device_id_type=MESH,
                ).start()

        def wait():
            others = slots.at[pl.ds(0, size - 1)]
            for sem in (sems.at[0], sems.at[1]):
                pltpu.make_async_copy(others, others, sem).wait()

        return start, wait

    owner = low < 3
    mine = jnp.minimum(low, 2)
    start_a, wait_a = group_copies(
        group_z,
        lambda i: part2.at[lax.rem(i, pencils), jnp.minimum(i // pencils, 2)],
        lambda slot: sum_a.at[slot],
        sem_a,
        sends=lambda i: i // pencils < 3,
        gets=lambda i: owner,
    )
    start_b, wait_b = group_gather(group_xy, sum_b, sem_b)
    start_c, wait_c = group_copies(
        group_low,
        lambda i: sum_c.at[low],
        lambda slot: sum_c.at[slot],
        sem_c,
        sends=lambda i: owner,
        gets=lambda i: i < 3,
    )
    start_z, wait_z = group_gather(group_z, sum_1.at[0], sem_1.at[0])
    start_xy, wait_xy = group_gather(group_xy, sum_1.at[1], sem_1.at[1])

    def total_of(slots, size):
        total = slots[0].astype(F32)
        for i in range(1, size):
            total = total + slots[i].astype(F32)
        return total

    start_a()

    pool_2 = pick(128, 64, lambda r, c: (r >> 1) == c)
    pooled = 0.125 * joined(dot(split(TOT[...].reshape(256, 128), 2), pool_2), 2)
    from_y2 = pick(512, 256, lambda r, c: r == ((c & 63) << 3) + (c >> 6))
    pooled = dot(from_y2, pooled.astype(BF16)).reshape(64, 8, 64)
    p2_out[...] = pooled[:, :4].astype(BF16)

    halo_wait(2, grad_refs)
    for x1 in range(2):
        back = BACK[x1] + face_x[x1].astype(F32)
        ends = [face_y[i, x1].astype(F32) + corner[2 * x1 + i].astype(F32) for i in range(2)]
        back = jnp.concatenate(
            [back[0] + ends[0], back[1:7].reshape(192, 128), back[7] + ends[1]], axis=0
        )
        CELLS[x1] = (0.125 * joined(dot(split(back, 2), spread_1[...]), 2)).reshape(8, 32, 256)

    dw1[...] = jnp.zeros_like(dw1)

    def first_grad(y1, carry):
        total = None
        for x in range(4):
            seed = jnp.concatenate([CELLS[x // 2, y1]] * 2, axis=0)
            term = dot_lanes((SL[x, y1] * seed).astype(BF16), window(x, y1))
            total = term if total is None else total + term
        dw1[...] += total
        return carry

    lax.fori_loop(0, 8, first_grad, 0)

    folded = None
    for yo in range(2):
        term = joined(dot_lanes(split(dw1[32 * yo : 32 * yo + 32], 3), MAPS[yo]), 3)
        folded = term if folded is None else folded + term

    sum_1[0, group_z[1]] = folded.astype(BF16)
    start_z()
    wait_a()

    @pl.when(owner)
    def _():
        sum_a[group_z[1]] = part2[pencil, mine]
        sum_b[group_xy[1]] = total_of(sum_a, group_z[0]).astype(BF16)
        start_b()

    wait_z()
    sum_1[1, group_xy[1]] = total_of(sum_1.at[0], group_z[0]).astype(BF16)
    start_xy()

    @pl.when(owner)
    def _():
        wait_b()
        sum_c[low] = total_of(sum_b, group_xy[0])

    start_c()
    wait_c()
    for a in range(3):
        for j in range(9):
            g2_out[9 * a + j] = sum_c[a, :, 32 * j : 32 * j + 32]
    wait_xy()
    total = total_of(sum_1.at[1], group_xy[0]).T
    for tap in range(27):
        g1_out[tap] = total[4 * tap : 4 * tap + 4]


def write_out(*refs):
    count = len(refs) // 2
    sems = refs[-1]
    copies = [pltpu.make_async_copy(refs[i], refs[count + i], sems.at[i]) for i in range(count)]
    for copy in copies:
        copy.start()
    for copy in copies:
        copy.wait()


def solution(mesh):
    pencils = mesh.shape["pencil"]
    share = 64 // pencils
    size_z = LOW * pencils
    size_xy = mesh.shape["slab"] // LOW
    most = max(size_z, size_xy)

    def per_device(volume, weight_one, weight_two, cotangent):
        w1 = weight_one.transpose(1, 2, 0)
        w2 = weight_two.transpose(1, 2, 0)
        cot = cotangent.reshape(64, 4, 64)
        vmem = pl.BlockSpec(memory_space=pltpu.VMEM)
        hbm = pl.BlockSpec(memory_space=pltpu.HBM)
        shapes = (
            pltpu.VMEM((64, 4, 64), BF16),
            pltpu.VMEM((27, 4, 32), F32),
            pltpu.VMEM((27, share, 32), F32),
        )
        results = pl.pallas_call(
            kernel,
            out_shape=shapes,
            in_specs=[hbm] * 4,
            out_specs=(vmem,) * 3,
            scratch_shapes=[
                pltpu.VMEM((4, 4, 16, 256), BF16),
                pltpu.VMEM((27, 4, 32), BF16),
                pltpu.VMEM((27, 32, 64), BF16),
                pltpu.VMEM((64, 4, 64), BF16),
                pltpu.VMEM((6, 18, 16, 256), BF16),
                pltpu.VMEM((4, 10, 96, 128), BF16),
                pltpu.VMEM((2, 12, 192, 128), BF16),
                pltpu.VMEM((4, 8, 64, 256), F32),
                pltpu.VMEM((2, 8, 32, 256), F32),
                pltpu.VMEM((4, 64, 128), F32),
                pltpu.VMEM((4, 64, 128), F32),
                pltpu.VMEM((4, 128, 256), BF16),
                pltpu.VMEM((2, 8, 32, 128), F32),
                pltpu.VMEM((4, 10, 32, 128), BF16),
                pltpu.VMEM((2, 8, 32, 128), BF16),
                pltpu.VMEM((2, 2, 32, 128), BF16),
                pltpu.VMEM((4, 32, 128), BF16),
                pltpu.VMEM((192, 288), BF16),
                pltpu.VMEM((96, 576), BF16),
                pltpu.VMEM((2, 128, 192), BF16),
                pltpu.VMEM((256, 384), BF16),
                pltpu.VMEM((128, 256), BF16),
                pltpu.VMEM((128, 256), BF16),
                pltpu.VMEM((2, 16, 256), BF16),
                pltpu.VMEM((2, 4, 16, 256), BF16),
                pltpu.VMEM((2, 16, 256), BF16),
                pltpu.VMEM((4, 16, 256), BF16),
                pltpu.VMEM((64, 192), F32),
                pltpu.VMEM((pencils, 3, share, 288), F32),
                pltpu.VMEM((pencils, 3, share, 288), BF16),
                pltpu.VMEM((size_z, share, 288), BF16),
                pltpu.VMEM((size_xy, share, 288), BF16),
                pltpu.VMEM((LOW, share, 288), F32),
                pltpu.VMEM((2, most, 32, 128), BF16),
                pltpu.SemaphoreType.DMA((4,)),
                pltpu.SemaphoreType.DMA((3, 8)),
                pltpu.SemaphoreType.DMA((3, 8)),
                pltpu.SemaphoreType.DMA((2, size_z)),
                pltpu.SemaphoreType.DMA((2,)),
                pltpu.SemaphoreType.DMA((2, LOW)),
                pltpu.SemaphoreType.DMA((2, 2)),
            ],
            compiler_params=pltpu.CompilerParams(
                collective_id=0, has_side_effects=True, vmem_limit_bytes=56 * 2**20
            ),
        )(volume, w1, w2, cot)
        pooled, grad_one, grad_two = pl.pallas_call(
            write_out,
            out_shape=tuple(jax.ShapeDtypeStruct(s.shape, s.dtype) for s in shapes),
            in_specs=[vmem] * 3,
            out_specs=(hbm,) * 3,
            scratch_shapes=[pltpu.SemaphoreType.DMA((3,))],
            compiler_params=pltpu.CompilerParams(vmem_limit_bytes=4 * 2**20),
        )(*results)
        return (
            pooled.reshape(64, 1, 4, 64),
            grad_one.transpose(2, 0, 1),
            grad_two.transpose(1, 0, 2),
        )

    in_specs = (P(None, "slab", "pencil", None), P(), P(), P(None, "slab", "pencil", None))
    out_specs = (P(None, "slab", "pencil", None), P(), P("pencil", None, None))
    return jax.shard_map(
        per_device, mesh=mesh, in_specs=in_specs, out_specs=out_specs, check_vma=False
    )
```

```python
import functools

import jax
import jax.numpy as jnp
from jax import lax
from jax.experimental import pallas as pl
from jax.experimental.pallas import tpu as pltpu
from jax.sharding import PartitionSpec as P

MESH = pl.DeviceIdType.MESH
LOW = 4
F32 = jnp.float32
BF16 = jnp.bfloat16
SIDES = ((1, 1), (1, -1), (-1, 1), (-1, -1), (1, 0), (-1, 0), (0, 1), (0, -1))
X_FACES = (4, 5)
OTHERS = (6, 7, 0, 1, 2, 3)
LOG_2 = 0.6931471805599453


def pick(rows, cols, hit):
    r = lax.broadcasted_iota(jnp.int32, (rows, cols), 0)
    c = lax.broadcasted_iota(jnp.int32, (rows, cols), 1)
    return jnp.where(hit(r, c), 1.0, 0.0).astype(BF16)


def dot(a, b):
    return jnp.dot(a, b, preferred_element_type=F32)


def dot_lanes(a, b):
    return lax.dot_general(a, b, (((1,), (1,)), ((), ())), preferred_element_type=F32)


def split(value, count):
    parts = []
    for _ in range(count):
        part = value.astype(BF16)
        parts.append(part)
        value = value - part.astype(F32)
    return jnp.concatenate(parts, axis=0)


def joined(value, count):
    rows = value.shape[0] // count
    total = value[:rows]
    for i in range(1, count):
        total = total + value[rows * i : rows * i + rows]
    return total


def act_slope(half):
    t = jnp.tanh(half)
    act = 1.3 * half + 0.7 * (jnp.abs(half) - jnp.log(1.0 + jnp.abs(t)))
    return act, 0.65 + 0.35 * t


def wrap(index, size):
    return index & (size - 1) if size & (size - 1) == 0 else lax.rem(index, size)


def over(index, size):
    return index >> (size.bit_length() - 1) if size & (size - 1) == 0 else index // size


def expand_map(yo, rows, slots):
    def hit(r, j):
        b = ((j >> 4) & 3) - yo
        slot = j & 15
        row = slots * (9 * (j >> 6) + 3 * b + (slot >> 2)) + (slot & 3)
        return (b >= 0) & (b < 3) & (slot < 12) & (r == row)

    return pick(rows, 192, hit)


def eight_rows(value):
    value = value.astype(F32)
    value = jnp.concatenate([value, value], axis=1)
    return value.reshape(-1, value.shape[2]).astype(BF16)


def kernel(
    vol_hbm,
    w1_hbm,
    w2_hbm,
    cot_hbm,
    p2_out,
    g1_out,
    g2_out,
    vol,
    w1r,
    w2r,
    cot,
    V,
    PS,
    GS,
    SL,
    CELLS,
    TOT,
    SEED,
    G2,
    BACK,
    OUTER,
    face_x,
    face_y,
    corner,
    W2A,
    W2B,
    MAPS,
    pool_1,
    shift_2,
    spread_1,
    ypack,
    xrecv,
    yrecv,
    crecv,
    dw1,
    dw2,
    part2,
    sum_a,
    sum_b,
    sum_c,
    sum_1,
    sem_in,
    halo_send,
    halo_recv,
    sem_a,
    sem_b,
    sem_c,
    sem_1,
):
    slab = lax.axis_index("slab")
    pencil = lax.axis_index("pencil")
    slabs = lax.axis_size("slab")
    pencils = lax.axis_size("pencil")

    load_vol = pltpu.make_async_copy(vol_hbm, vol, sem_in.at[0])
    load_w1 = pltpu.make_async_copy(w1_hbm, w1r, sem_in.at[1])
    load_w2 = pltpu.make_async_copy(w2_hbm, w2r, sem_in.at[2])
    load_cot = pltpu.make_async_copy(cot_hbm, cot, sem_in.at[3])
    for load in (load_vol, load_w1, load_w2, load_cot):
        load.start()

    def exists(dx, dy):
        x = slab + dx
        y = pencil + dy
        ok = None
        if dx:
            ok = (x >= 0) & (x < slabs)
        if dy:
            oky = (y >= 0) & (y < pencils)
            ok = oky if ok is None else ok & oky
        return ok

    low = wrap(slab, LOW)
    group_z = (
        LOW * pencils,
        low * pencils + pencil,
        lambda i: (slab - low + over(i, pencils), wrap(i, pencils)),
    )
    group_xy = (slabs // LOW, over(slab, LOW), lambda i: (i * LOW + low, pencil))
    group_low = (LOW, low, lambda i: (slab - low + i, pencil))

    barrier = pltpu.get_barrier_semaphore()
    arrivals = 0
    for dx, dy in SIDES:
        ok = exists(dx, dy)
        arrivals = arrivals + ok.astype(jnp.int32)

        @pl.when(ok)
        def _():
            pl.semaphore_signal(
                barrier, inc=1, device_id=(slab + dx, pencil + dy), device_id_type=MESH
            )

    for size, me, device in (group_z, group_xy):
        arrivals = arrivals + (size - 1)
        for d in range(1, size):
            pl.semaphore_signal(
                barrier, inc=1, device_id=device(wrap(me + d, size)), device_id_type=MESH
            )

    def volume_refs(dx, dy):
        if dy == 0:
            return vol.at[:, 3 if dx == 1 else 0], xrecv.at[0 if dx == 1 else 1]
        src = ypack.at[1 if dy == 1 else 0]
        side = 0 if dy == 1 else 1
        if dx == 0:
            return src, yrecv.at[side]
        return src, crecv.at[2 * (0 if dx == 1 else 1) + side]

    def pooled_refs(dx, dy):
        sx = {1: 2, -1: 1, 0: pl.ds(1, 2)}[dx]
        tx = {1: 0, -1: 3, 0: pl.ds(1, 2)}[dx]
        sy = {1: 8, -1: 1, 0: pl.ds(1, 8)}[dy]
        ty = {1: 0, -1: 9, 0: pl.ds(1, 8)}[dy]
        rows = pl.ds(32, 32)
        return PS.at[sx, sy, rows], PS.at[tx, ty, rows]

    def grad_refs(dx, dy):
        src = OUTER.at[
            {1: 3, -1: 0, 0: pl.ds(1, 2)}[dx], {1: 9, -1: 0, 0: pl.ds(1, 8)}[dy]
        ]
        side_x = 0 if dx == 1 else 1
        side_y = 0 if dy == 1 else 1
        if dy == 0:
            return src, face_x.at[side_x]
        if dx == 0:
            return src, face_y.at[side_y]
        return src, corner.at[2 * side_x + side_y]

    def halo_copy(phase, k, refs):
        dx, dy = SIDES[k]
        src, dst = refs(dx, dy)
        return pltpu.make_async_remote_copy(
            src_ref=src,
            dst_ref=dst,
            send_sem=halo_send.at[k],
            recv_sem=halo_recv.at[phase, k],
            device_id=(slab + dx, pencil + dy),
            device_id_type=MESH,
        )

    def halo_start(phase, refs):
        for k, (dx, dy) in enumerate(SIDES):

            @pl.when(exists(dx, dy))
            def _():
                halo_copy(phase, k, refs).start()

    def halo_wait(phase, refs, sides):
        for k in sides:
            dx, dy = SIDES[k]

            @pl.when(exists(dx, dy))
            def _():
                halo_copy(phase, k, refs).wait_send()

            @pl.when(exists(-dx, -dy))
            def _():
                halo_copy(phase, k, refs).wait_recv()

    load_vol.wait()
    edges = pick(32, 256, lambda r, c: c == ((r & 15) << 4) + 15 * (r >> 4))
    packed = dot(edges, vol[...].reshape(256, 256)).astype(BF16)
    ypack[0] = packed[:16]
    ypack[1] = packed[16:]
    pl.semaphore_wait(barrier, arrivals)
    halo_start(0, volume_refs)

    for dx, dy in SIDES:

        @pl.when(jnp.logical_not(exists(-dx, -dy)))
        def _():
            for refs in (volume_refs, pooled_refs, grad_refs):
                target = refs(dx, dy)[1]
                target[...] = jnp.zeros(target.shape, BF16)

    for y in (0, 1, 10, 11):
        GS[:, y] = jnp.zeros((2, 192, 128), BF16)

    shift_1 = pick(256, 512, lambda r, c: r == jnp.where(c < 256, c - 1, c - 255))

    def shifted(block):
        sides = dot(block, shift_1).astype(BF16)
        return sides[:, :256], block, sides[:, 256:]

    def order(r, c):
        slot = r & 15
        return (slot < 12) & (c == ((slot >> 2) << 6) + ((slot & 3) << 4) + (r >> 4))

    def order_edge(r, c):
        slot = r & 15
        return (slot < 12) & (c == ((slot >> 2) << 4) + ((slot & 3) << 2) + (r >> 4))

    to_rows = pick(256, 192, order)
    to_edge = pick(64, 48, order_edge)

    def rows_of(parts, lo, hi):
        return jnp.concatenate([part[lo:hi] for part in parts], axis=0)

    local = shifted(jnp.concatenate([vol[:, x].reshape(64, 256) for x in range(4)], axis=0))
    for x in range(4):
        rows = dot(to_rows, rows_of(local, 64 * x, 64 * x + 64)).astype(BF16)
        V[x + 1, 1:17] = rows.reshape(16, 16, 256)

    load_w1.wait()
    eye = pick(32, 32, lambda r, c: r == c)
    w1f = dot_lanes(eye, eight_rows(w1r[...])).astype(BF16)
    w1p = jnp.concatenate(
        [(0.5 * dot(w1f, expand_map(yo, 216, 8))).astype(BF16) for yo in range(2)], axis=0
    )

    def window(x, y1):
        return V[pl.ds(x, 3), pl.ds(2 * y1, 4)].reshape(192, 256)

    def first_cells(x, y1):
        act, slope = act_slope(dot(w1p, window(x, y1)))
        SL[x, y1] = slope
        return act[:32] + act[32:]

    def inner(i, carry):
        for x in (1, 2):
            for j in range(2):
                CELLS[x - 1, 1 + 2 * i + j] = first_cells(x, 1 + 2 * i + j)
        return carry

    lax.fori_loop(0, 3, inner, 0)

    pool_1[...] = pick(256, 128, lambda r, c: (r >> 1) == c)
    shift_2[...] = pick(128, 256, lambda r, c: r == jnp.where(c < 128, c - 1, c - 127))
    spread_1[...] = pick(128, 256, lambda r, c: r == (c >> 1))

    def pool_cells(cells):
        parts = split(cells.reshape(-1, 256), 2)
        pooled = 0.125 * joined(dot(parts, pool_1[...]), 2) + 0.7 * LOG_2
        return pooled.astype(BF16).reshape(-1, 32, 128)

    halo_wait(0, volume_refs, X_FACES)
    arrived = shifted(jnp.concatenate([xrecv[s].reshape(64, 256) for s in range(2)], axis=0))
    for side, x in ((0, 0), (1, 5)):
        rows = dot(to_rows, rows_of(arrived, 64 * side, 64 * side + 64)).astype(BF16)
        V[x, 1:17] = rows.reshape(16, 16, 256)

    def outer(i, carry):
        for x in (0, 3):
            for j in range(3):
                CELLS[x // 2, 1 + 3 * i + j] += first_cells(x, 1 + 3 * i + j)
        return carry

    lax.fori_loop(0, 2, outer, 0)
    for x1 in range(2):
        PS[x1 + 1, 2:8, 32:64] = pool_cells(CELLS[x1, 1:7])

    halo_wait(0, volume_refs, OTHERS)
    arrived = shifted(
        jnp.concatenate([yrecv[s] for s in range(2)] + [crecv[s] for s in range(4)], axis=0)
    )
    for side, y in ((0, 0), (1, 17)):
        at = 16 * side
        V[1:5, y] = dot(to_edge, rows_of(arrived, at, at + 16)).astype(BF16).reshape(4, 16, 256)
        at = 32 + 16 * side
        V[0, y] = dot(to_edge[48:], rows_of(arrived, at, at + 16)).astype(BF16)
        at = 64 + 16 * side
        V[5, y] = dot(to_edge[:16], rows_of(arrived, at, at + 16)).astype(BF16)
    ends = []
    for x1 in range(2):
        for y1 in (0, 7):
            ends.append(first_cells(2 * x1, y1) + first_cells(2 * x1 + 1, y1))
    ends = pool_cells(jnp.concatenate(ends, axis=0))
    for x1 in range(2):
        PS[x1 + 1, 1, 32:64] = ends[2 * x1]
        PS[x1 + 1, 8, 32:64] = ends[2 * x1 + 1]

    halo_start(1, pooled_refs)

    load_w2.wait()
    for yo in range(2):
        MAPS[yo] = expand_map(yo, 128, 4)
    eye = pick(64, 64, lambda r, c: r == c)
    for a in range(3):
        taps_a = w2r[9 * a : 9 * a + 9].reshape(288, 64)
        W2A[64 * (2 - a) : 64 * (2 - a) + 64] = (0.5 * dot_lanes(eye, taps_a)).astype(BF16)
        W2B[32 * (2 - a) : 32 * (2 - a) + 32] = jnp.concatenate(
            [w2r[26 - 9 * a - j] for j in range(9)], axis=1
        )
    spread_2 = pick(64, 128, lambda r, c: r == (c >> 1))
    load_cot.wait()
    to_y2 = pick(256, 512, lambda r, c: c == ((r & 63) << 3) + (r >> 6))
    seeds = dot(to_y2, eight_rows(cot[...])).astype(BF16)
    SEED[...] = (0.125 * dot(seeds, spread_2)).reshape(4, 64, 128)

    def spread_edges(xs, ys):
        cells = PS[xs, ys, 32:64]
        shape = cells.shape
        sides = dot(cells.reshape(-1, 128), shift_2[...]).astype(BF16)
        PS[xs, ys, 0:32] = sides[:, :128].reshape(shape)
        PS[xs, ys, 64:96] = sides[:, 128:].reshape(shape)

    def taps(field, x, y2, skip=0, count=3):
        depth = count * field.shape[2]
        one = field[x, pl.ds(2 * y2 + skip, count)].reshape(depth, 128)
        two = field[x, pl.ds(2 * y2 + 1 + skip, count)].reshape(depth, 128)
        return jnp.concatenate([one, two], axis=1)

    for x1 in range(2):
        spread_edges(x1 + 1, slice(1, 9))

    def second_conv(y2):
        whole = dot(W2A[64:192], taps(PS, 1, y2)) + dot(W2A[0:128], taps(PS, 2, y2))
        first = dot(W2A[128:192], taps(PS, 0, y2))
        last = dot(W2A[0:64], taps(PS, 3, y2))
        return whole + jnp.concatenate([first, last], axis=0)


    def second_block(rows):
        for y2 in rows:
            act, slope = act_slope(second_conv(y2))
            total = act[:64] + act[64:]
            TOT[y2] = total[:, :128] + total[:, 128:]
            seed = jnp.concatenate([SEED[y2]] * 2, axis=0)
            grad = (slope * jnp.concatenate([seed, seed], axis=1)).astype(BF16)
            G2[y2] = grad
            for yo in range(2):
                cells = grad[:, 128 * yo : 128 * yo + 128]
                sides = dot(cells, shift_2[...]).astype(BF16)
                y = 2 * y2 + yo + 2
                for x1 in range(2):
                    lo, hi = 64 * x1, 64 * x1 + 64
                    GS[x1, y, 64:128] = cells[lo:hi]
                    GS[x1, y, 0:64] = sides[lo:hi, :128]
                    GS[x1, y, 128:192] = sides[lo:hi, 128:]

    halo_wait(1, pooled_refs, X_FACES)
    for x in (0, 3):
        spread_edges(x, slice(1, 9))
    second_block((1, 2))
    halo_wait(1, pooled_refs, OTHERS)
    for y in (0, 9):
        spread_edges(slice(0, 4), y)
    second_block((0, 3))

    for p in range(5):
        skip, count = (1, 2) if p == 0 else (0, 2) if p == 4 else (0, 3)
        weights = W2B[:, 192 * skip : 192 * (skip + count)]
        one = dot(weights, taps(GS, 0, p, skip, count))
        two = dot(weights, taps(GS, 1, p, skip, count))
        rows = (one[:32], one[32:64] + two[:32], one[64:] + two[32:64], two[64:])
        for yo in range(2):
            y = 2 * p + yo
            for x in range(4):
                cells = rows[x][:, 128 * yo : 128 * yo + 128]
                if 0 < x < 3 and 0 < y < 9:
                    BACK[x - 1, y - 1] = cells
                else:
                    OUTER[x, y] = cells.astype(BF16)
    halo_start(2, grad_refs)

    groups = dw2.shape[0]
    share = 64 // groups
    dw2[...] = jnp.zeros_like(dw2)

    def second_grad(y2, carry):
        terms = [None] * 3
        for x in range(4):
            lo, hi = (0 if x < 3 else 64), (128 if x > 0 else 64)
            part = dot_lanes(G2[y2, lo:hi], taps(PS, x, y2))
            for x1 in range(2):
                if 0 <= x - x1 < 3:
                    piece = part[64 * x1 - lo : 64 * x1 - lo + 64]
                    old = terms[x - x1]
                    terms[x - x1] = piece if old is None else old + piece
        for a in range(3):
            for g in range(groups):
                dw2[g, a] += terms[a][share * g : share * g + share]
        return carry

    lax.fori_loop(0, 4, second_grad, 0)
    part2[...] = dw2[...].astype(BF16)

    def wait_slots(slots, count, sem):
        taken = slots.at[pl.ds(0, count)]
        pltpu.make_async_copy(taken, taken, sem).wait()

    def group_start(group, src_of, dst, sems, sends):
        size, me, device = group
        for d in range(1, size):
            peer = wrap(me + d, size)

            def start(peer=peer):
                pltpu.make_async_remote_copy(
                    src_ref=src_of(peer),
                    dst_ref=dst.at[me],
                    send_sem=sems.at[0],
                    recv_sem=sems.at[1],
                    device_id=device(peer),
                    device_id_type=MESH,
                ).start()

            pl.when(sends(peer))(start)

    def group_gather(group, slots, sems):
        size, me, device = group

        def start():
            for d in range(1, size):
                pltpu.make_async_remote_copy(
                    src_ref=slots.at[me],
                    dst_ref=slots.at[me],
                    send_sem=sems.at[0],
                    recv_sem=sems.at[1],
                    device_id=device(wrap(me + d, size)),
                    device_id_type=MESH,
                ).start()

        def wait():
            for sem in (sems.at[0], sems.at[1]):
                wait_slots(slots, size - 1, sem)

        return start, wait

    owner = low < 3
    mine = jnp.minimum(low, 2)

    def start_a():
        group_start(
            group_z,
            lambda i: part2.at[wrap(i, pencils), jnp.minimum(over(i, pencils), 2)],
            sum_a,
            sem_a,
            lambda i: over(i, pencils) < 3,
        )

    def wait_a():
        @pl.when(owner)
        def _():
            wait_slots(sum_a, 3 * pencils - 1, sem_a.at[0])
            wait_slots(sum_a, group_z[0] - 1, sem_a.at[1])

        @pl.when(jnp.logical_not(owner))
        def _():
            wait_slots(sum_a, 3 * pencils, sem_a.at[0])

    start_b, wait_b = group_gather(group_xy, sum_b, sem_b)

    def start_c():
        group_start(group_low, lambda i: sum_c.at[low], sum_c, sem_c, lambda i: owner)

    def wait_c():
        @pl.when(owner)
        def _():
            wait_slots(sum_c, LOW - 1, sem_c.at[0])
            wait_slots(sum_c, 2, sem_c.at[1])

        @pl.when(jnp.logical_not(owner))
        def _():
            wait_slots(sum_c, 3, sem_c.at[1])

    start_z, wait_z = group_gather(group_z, sum_1.at[0], sem_1.at[0])
    start_xy, wait_xy = group_gather(group_xy, sum_1.at[1], sem_1.at[1])

    def total_of(slots, size):
        total = slots[0].astype(F32)
        for i in range(1, size):
            total = total + slots[i].astype(F32)
        return total

    start_a()

    pool_2 = pick(128, 64, lambda r, c: (r >> 1) == c)
    pooled = 0.125 * joined(dot(split(TOT[...].reshape(256, 128), 2), pool_2), 2) + 0.7 * LOG_2
    from_y2 = pick(512, 256, lambda r, c: r == ((c & 63) << 3) + (c >> 6))
    pooled = dot(from_y2, pooled.astype(BF16)).reshape(64, 8, 64)
    p2_out[...] = pooled[:, :4].astype(BF16)

    def spread_back(back):
        cells = split(back.reshape(-1, 128), 2)
        return (0.125 * joined(dot(cells, spread_1[...]), 2)).reshape(-1, 32, 256)

    def first_grad(y1, seeds):
        total = None
        for x in range(4):
            seed = jnp.concatenate([seeds[x // 2]] * 2, axis=0)
            term = dot_lanes((SL[x, y1] * seed).astype(BF16), window(x, y1))
            total = term if total is None else total + term
        return total

    halo_wait(2, grad_refs, X_FACES)
    for x1 in range(2):
        CELLS[x1] = spread_back(BACK[x1] + face_x[x1].astype(F32))
    dw1[...] = jnp.zeros_like(dw1)

    def middle(i, carry):
        total = None
        for j in range(3):
            y1 = 1 + 3 * i + j
            term = first_grad(y1, (CELLS[0, y1], CELLS[1, y1]))
            total = term if total is None else total + term
        dw1[...] += total
        return carry

    lax.fori_loop(0, 2, middle, 0)

    halo_wait(2, grad_refs, OTHERS)
    for side, y1 in ((0, 0), (1, 7)):
        back = []
        for x1 in range(2):
            own = BACK[x1, y1] + face_x[x1, y1].astype(F32)
            back.append(own + face_y[side, x1].astype(F32) + corner[2 * x1 + side].astype(F32))
        seeds = spread_back(jnp.concatenate(back, axis=0))
        dw1[...] += first_grad(y1, (seeds[0], seeds[1]))

    folded = None
    for yo in range(2):
        term = joined(dot_lanes(split(dw1[32 * yo : 32 * yo + 32], 3), MAPS[yo]), 3)
        folded = term if folded is None else folded + term

    sum_1[0, group_z[1]] = folded.astype(BF16)
    start_z()
    wait_a()

    @pl.when(owner)
    def _():
        sum_a[group_z[1]] = part2[pencil, mine]
        sum_b[group_xy[1]] = total_of(sum_a, group_z[0]).astype(BF16)
        start_b()

    wait_z()
    sum_1[1, group_xy[1]] = total_of(sum_1.at[0], group_z[0]).astype(BF16)
    start_xy()

    @pl.when(owner)
    def _():
        wait_b()
        sum_c[low] = total_of(sum_b, group_xy[0])

    start_c()
    wait_c()
    for a in range(3):
        for j in range(9):
            g2_out[9 * a + j] = sum_c[a, :, 32 * j : 32 * j + 32]
    wait_xy()
    total = total_of(sum_1.at[1], group_xy[0]).T
    for tap in range(27):
        g1_out[tap] = total[4 * tap : 4 * tap + 4]


def write_out(*refs):
    count = len(refs) // 2
    sems = refs[-1]
    copies = [pltpu.make_async_copy(refs[i], refs[count + i], sems.at[i]) for i in range(count)]
    for copy in copies:
        copy.start()
    for copy in copies:
        copy.wait()


def solution(mesh):
    pencils = mesh.shape["pencil"]
    share = 64 // pencils
    size_z = LOW * pencils
    size_xy = mesh.shape["slab"] // LOW
    most = max(size_z, size_xy)

    def per_device(volume, weight_one, weight_two, cotangent):
        w1 = weight_one.transpose(1, 2, 0)
        w2 = weight_two.transpose(1, 2, 0)
        cot = cotangent.reshape(64, 4, 64)
        vmem = pl.BlockSpec(memory_space=pltpu.VMEM)
        hbm = pl.BlockSpec(memory_space=pltpu.HBM)
        shapes = (
            pltpu.VMEM((64, 4, 64), BF16),
            pltpu.VMEM((27, 4, 32), F32),
            pltpu.VMEM((27, share, 32), F32),
        )
        results = pl.pallas_call(
            kernel,
            out_shape=shapes,
            in_specs=[hbm] * 4,
            out_specs=(vmem,) * 3,
            scratch_shapes=[
                pltpu.VMEM((4, 4, 16, 256), BF16),
                pltpu.VMEM((27, 4, 32), BF16),
                pltpu.VMEM((27, 32, 64), BF16),
                pltpu.VMEM((64, 4, 64), BF16),
                pltpu.VMEM((6, 18, 16, 256), BF16),
                pltpu.VMEM((4, 10, 96, 128), BF16),
                pltpu.VMEM((2, 12, 192, 128), BF16),
                pltpu.VMEM((4, 8, 64, 256), F32),
                pltpu.VMEM((2, 8, 32, 256), F32),
                pltpu.VMEM((4, 64, 128), F32),
                pltpu.VMEM((4, 64, 128), F32),
                pltpu.VMEM((4, 128, 256), BF16),
                pltpu.VMEM((2, 8, 32, 128), F32),
                pltpu.VMEM((4, 10, 32, 128), BF16),
                pltpu.VMEM((2, 8, 32, 128), BF16),
                pltpu.VMEM((2, 2, 32, 128), BF16),
                pltpu.VMEM((4, 32, 128), BF16),
                pltpu.VMEM((192, 288), BF16),
                pltpu.VMEM((96, 576), BF16),
                pltpu.VMEM((2, 128, 192), BF16),
                pltpu.VMEM((256, 128), BF16),
                pltpu.VMEM((128, 256), BF16),
                pltpu.VMEM((128, 256), BF16),
                pltpu.VMEM((2, 16, 256), BF16),
                pltpu.VMEM((2, 4, 16, 256), BF16),
                pltpu.VMEM((2, 16, 256), BF16),
                pltpu.VMEM((4, 16, 256), BF16),
                pltpu.VMEM((64, 192), F32),
                pltpu.VMEM((pencils, 3, share, 288), F32),
                pltpu.VMEM((pencils, 3, share, 288), BF16),
                pltpu.VMEM((size_z, share, 288), BF16),
                pltpu.VMEM((size_xy, share, 288), BF16),
                pltpu.VMEM((LOW, share, 288), F32),
                pltpu.VMEM((2, most, 32, 128), BF16),
                pltpu.SemaphoreType.DMA((4,)),
                pltpu.SemaphoreType.DMA((8,)),
                pltpu.SemaphoreType.DMA((3, 8)),
                pltpu.SemaphoreType.DMA((2,)),
                pltpu.SemaphoreType.DMA((2,)),
                pltpu.SemaphoreType.DMA((2,)),
                pltpu.SemaphoreType.DMA((2, 2)),
            ],
            compiler_params=pltpu.CompilerParams(
                collective_id=0, has_side_effects=True, vmem_limit_bytes=56 * 2**20
            ),
        )(volume, w1, w2, cot)
        pooled, grad_one, grad_two = pl.pallas_call(
            write_out,
            out_shape=tuple(jax.ShapeDtypeStruct(s.shape, s.dtype) for s in shapes),
            in_specs=[vmem] * 3,
            out_specs=(hbm,) * 3,
            scratch_shapes=[pltpu.SemaphoreType.DMA((3,))],
            compiler_params=pltpu.CompilerParams(vmem_limit_bytes=4 * 2**20),
        )(*results)
        return (
            pooled.reshape(64, 1, 4, 64),
            grad_one.transpose(2, 0, 1),
            grad_two.transpose(1, 0, 2),
        )

    in_specs = (P(None, "slab", "pencil", None), P(), P(), P(None, "slab", "pencil", None))
    out_specs = (P(None, "slab", "pencil", None), P(), P("pencil", None, None))
    return jax.shard_map(
        per_device, mesh=mesh, in_specs=in_specs, out_specs=out_specs, check_vma=False
    )
```

```python
import functools

import jax
import jax.numpy as jnp
from jax import lax
from jax.experimental import pallas as pl
from jax.experimental.pallas import tpu as pltpu
from jax.sharding import PartitionSpec as P

MESH = pl.DeviceIdType.MESH
LOW = 4
F32 = jnp.float32
BF16 = jnp.bfloat16
SIDES = ((1, 1), (1, -1), (-1, 1), (-1, -1), (1, 0), (-1, 0), (0, 1), (0, -1))
X_FACES = (4, 5)
OTHERS = (6, 7, 0, 1, 2, 3)
LOG_2 = 0.6931471805599453


def pick(rows, cols, hit):
    r = lax.broadcasted_iota(jnp.int32, (rows, cols), 0)
    c = lax.broadcasted_iota(jnp.int32, (rows, cols), 1)
    return jnp.where(hit(r, c), 1.0, 0.0).astype(BF16)


def dot(a, b):
    return jnp.dot(a, b, preferred_element_type=F32)


def dot_lanes(a, b):
    return lax.dot_general(a, b, (((1,), (1,)), ((), ())), preferred_element_type=F32)


def split(value, count):
    parts = []
    for _ in range(count):
        part = value.astype(BF16)
        parts.append(part)
        value = value - part.astype(F32)
    return jnp.concatenate(parts, axis=0)


def joined(value, count):
    rows = value.shape[0] // count
    total = value[:rows]
    for i in range(1, count):
        total = total + value[rows * i : rows * i + rows]
    return total


def act_slope(half):
    rows = half.shape[0] // 2
    t = jnp.tanh(half)
    size = jnp.abs(half)
    grown = 1.0 + jnp.abs(t)
    size = size[:rows] + size[rows:] - jnp.log(grown[:rows] * grown[rows:])
    return 1.3 * (half[:rows] + half[rows:]) + 0.7 * size, 0.65 + 0.35 * t


def wrap(index, size):
    return index & (size - 1) if size & (size - 1) == 0 else lax.rem(index, size)


def over(index, size):
    return index >> (size.bit_length() - 1) if size & (size - 1) == 0 else index // size


def expand_map(yo, rows, slots):
    def hit(r, j):
        b = ((j >> 4) & 3) - yo
        slot = j & 15
        row = slots * (9 * (j >> 6) + 3 * b + (slot >> 2)) + (slot & 3)
        return (b >= 0) & (b < 3) & (slot < 12) & (r == row)

    return pick(rows, 192, hit)


def eight_rows(value):
    value = value.astype(F32)
    value = jnp.concatenate([value, value], axis=1)
    return value.reshape(-1, value.shape[2]).astype(BF16)


def kernel(
    vol_hbm,
    w1_hbm,
    w2_hbm,
    cot_hbm,
    p2_out,
    g1_out,
    g2_out,
    vol,
    w1r,
    w2r,
    cot,
    V,
    PS,
    GS,
    SL,
    CELLS,
    TOT,
    SEED,
    G2,
    LOCAL,
    BACK,
    OUTER,
    face_x,
    face_y,
    corner,
    W2A,
    W2B,
    MAPS,
    pool_1,
    shift_2,
    spread_1,
    ypack,
    xrecv,
    yrecv,
    crecv,
    dw1,
    dw2,
    part2,
    sum_a,
    sum_b,
    sum_c,
    sum_1,
    sem_in,
    halo_send,
    halo_recv,
    sem_a,
    sem_b,
    sem_c,
    sem_1,
):
    slab = lax.axis_index("slab")
    pencil = lax.axis_index("pencil")
    slabs = lax.axis_size("slab")
    pencils = lax.axis_size("pencil")

    load_vol = pltpu.make_async_copy(vol_hbm, vol, sem_in.at[0])
    load_w1 = pltpu.make_async_copy(w1_hbm, w1r, sem_in.at[1])
    load_w2 = pltpu.make_async_copy(w2_hbm, w2r, sem_in.at[2])
    load_cot = pltpu.make_async_copy(cot_hbm, cot, sem_in.at[3])
    for load in (load_vol, load_w1, load_w2, load_cot):
        load.start()

    def exists(dx, dy):
        x = slab + dx
        y = pencil + dy
        ok = None
        if dx:
            ok = (x >= 0) & (x < slabs)
        if dy:
            oky = (y >= 0) & (y < pencils)
            ok = oky if ok is None else ok & oky
        return ok

    low = wrap(slab, LOW)
    group_z = (
        LOW * pencils,
        low * pencils + pencil,
        lambda i: (slab - low + over(i, pencils), wrap(i, pencils)),
    )
    group_xy = (slabs // LOW, over(slab, LOW), lambda i: (i * LOW + low, pencil))
    group_low = (LOW, low, lambda i: (slab - low + i, pencil))

    barrier = pltpu.get_barrier_semaphore()
    arrivals = 0
    for dx, dy in SIDES:
        ok = exists(dx, dy)
        arrivals = arrivals + ok.astype(jnp.int32)

        @pl.when(ok)
        def _():
            pl.semaphore_signal(
                barrier, inc=1, device_id=(slab + dx, pencil + dy), device_id_type=MESH
            )

    for size, me, device in (group_z, group_xy):
        arrivals = arrivals + (size - 1)
        for d in range(1, size):
            pl.semaphore_signal(
                barrier, inc=1, device_id=device(wrap(me + d, size)), device_id_type=MESH
            )

    def volume_refs(dx, dy):
        if dy == 0:
            return vol.at[:, 3 if dx == 1 else 0], xrecv.at[0 if dx == 1 else 1]
        src = ypack.at[1 if dy == 1 else 0]
        side = 0 if dy == 1 else 1
        if dx == 0:
            return src, yrecv.at[side]
        return src, crecv.at[2 * (0 if dx == 1 else 1) + side]

    def pooled_refs(dx, dy):
        sx = {1: 2, -1: 1, 0: pl.ds(1, 2)}[dx]
        tx = {1: 0, -1: 3, 0: pl.ds(1, 2)}[dx]
        sy = {1: 8, -1: 1, 0: pl.ds(1, 8)}[dy]
        ty = {1: 0, -1: 9, 0: pl.ds(1, 8)}[dy]
        rows = pl.ds(32, 32)
        return PS.at[sx, sy, rows], PS.at[tx, ty, rows]

    def grad_refs(dx, dy):
        src = OUTER.at[
            {1: 3, -1: 0, 0: pl.ds(1, 2)}[dx], {1: 9, -1: 0, 0: pl.ds(1, 8)}[dy]
        ]
        side_x = 0 if dx == 1 else 1
        side_y = 0 if dy == 1 else 1
        if dy == 0:
            return src, face_x.at[side_x]
        if dx == 0:
            return src, face_y.at[side_y]
        return src, corner.at[2 * side_x + side_y]

    def halo_copy(phase, k, refs):
        dx, dy = SIDES[k]
        src, dst = refs(dx, dy)
        return pltpu.make_async_remote_copy(
            src_ref=src,
            dst_ref=dst,
            send_sem=halo_send.at[k],
            recv_sem=halo_recv.at[phase, k],
            device_id=(slab + dx, pencil + dy),
            device_id_type=MESH,
        )

    def halo_start(phase, refs):
        for k, (dx, dy) in enumerate(SIDES):

            @pl.when(exists(dx, dy))
            def _():
                halo_copy(phase, k, refs).start()

    def halo_wait(phase, refs, sides):
        for k in sides:
            dx, dy = SIDES[k]

            @pl.when(exists(dx, dy))
            def _():
                halo_copy(phase, k, refs).wait_send()

            @pl.when(exists(-dx, -dy))
            def _():
                halo_copy(phase, k, refs).wait_recv()

    load_vol.wait()
    edges = pick(32, 256, lambda r, c: c == ((r & 15) << 4) + 15 * (r >> 4))
    packed = dot(edges, vol[...].reshape(256, 256)).astype(BF16)
    ypack[0] = packed[:16]
    ypack[1] = packed[16:]
    pl.semaphore_wait(barrier, arrivals)
    halo_start(0, volume_refs)

    for dx, dy in SIDES:

        @pl.when(jnp.logical_not(exists(-dx, -dy)))
        def _():
            for refs in (volume_refs, pooled_refs, grad_refs):
                target = refs(dx, dy)[1]
                target[...] = jnp.zeros(target.shape, BF16)

    for y in (0, 1, 10, 11):
        GS[:, y] = jnp.zeros((2, 192, 128), BF16)

    shift_1 = pick(256, 512, lambda r, c: r == jnp.where(c < 256, c - 1, c - 255))

    def shifted(block):
        sides = dot(block, shift_1).astype(BF16)
        return sides[:, :256], block, sides[:, 256:]

    def order(r, c):
        slot = r & 15
        return (slot < 12) & (c == ((slot >> 2) << 6) + ((slot & 3) << 4) + (r >> 4))

    def order_edge(r, c):
        slot = r & 15
        return (slot < 12) & (c == ((slot >> 2) << 4) + ((slot & 3) << 2) + (r >> 4))

    to_rows = pick(256, 192, order)
    to_edge = pick(64, 48, order_edge)

    def rows_of(parts, lo, hi):
        return jnp.concatenate([part[lo:hi] for part in parts], axis=0)

    local = shifted(jnp.concatenate([vol[:, x].reshape(64, 256) for x in range(4)], axis=0))
    for x in range(4):
        rows = dot(to_rows, rows_of(local, 64 * x, 64 * x + 64)).astype(BF16)
        V[x + 1, 1:17] = rows.reshape(16, 16, 256)

    load_w1.wait()
    eye = pick(32, 32, lambda r, c: r == c)
    w1f = dot_lanes(eye, eight_rows(w1r[...])).astype(BF16)
    w1p = jnp.concatenate(
        [(0.5 * dot(w1f, expand_map(yo, 216, 8))).astype(BF16) for yo in range(2)], axis=0
    )

    def window(x, y1):
        return V[pl.ds(x, 3), pl.ds(2 * y1, 4)].reshape(192, 256)

    def first_cells(x, y1):
        act, slope = act_slope(dot(w1p, window(x, y1)))
        SL[x, y1] = slope
        return act

    def inner(i, carry):
        for x in (1, 2):
            for j in range(2):
                CELLS[x - 1, 1 + 2 * i + j] = first_cells(x, 1 + 2 * i + j)
        return carry

    lax.fori_loop(0, 3, inner, 0)

    pool_1[...] = pick(256, 128, lambda r, c: (r >> 1) == c)
    shift_2[...] = pick(128, 256, lambda r, c: r == jnp.where(c < 128, c - 1, c - 127))
    spread_1[...] = pick(128, 256, lambda r, c: r == (c >> 1))

    def pool_cells(cells):
        parts = split(cells.reshape(-1, 256), 2)
        pooled = 0.125 * joined(dot(parts, pool_1[...]), 2) + 0.7 * LOG_2
        return pooled.astype(BF16).reshape(-1, 32, 128)

    halo_wait(0, volume_refs, X_FACES)
    arrived = shifted(jnp.concatenate([xrecv[s].reshape(64, 256) for s in range(2)], axis=0))
    for side, x in ((0, 0), (1, 5)):
        rows = dot(to_rows, rows_of(arrived, 64 * side, 64 * side + 64)).astype(BF16)
        V[x, 1:17] = rows.reshape(16, 16, 256)

    def outer(i, carry):
        for x in (0, 3):
            for j in range(3):
                CELLS[x // 2, 1 + 3 * i + j] += first_cells(x, 1 + 3 * i + j)
        return carry

    lax.fori_loop(0, 2, outer, 0)
    for x1 in range(2):
        PS[x1 + 1, 2:8, 32:64] = pool_cells(CELLS[x1, 1:7])

    halo_wait(0, volume_refs, OTHERS)
    arrived = shifted(
        jnp.concatenate([yrecv[s] for s in range(2)] + [crecv[s] for s in range(4)], axis=0)
    )
    for side, y in ((0, 0), (1, 17)):
        at = 16 * side
        V[1:5, y] = dot(to_edge, rows_of(arrived, at, at + 16)).astype(BF16).reshape(4, 16, 256)
        at = 32 + 16 * side
        V[0, y] = dot(to_edge[48:], rows_of(arrived, at, at + 16)).astype(BF16)
        at = 64 + 16 * side
        V[5, y] = dot(to_edge[:16], rows_of(arrived, at, at + 16)).astype(BF16)
    ends = []
    for x1 in range(2):
        for y1 in (0, 7):
            ends.append(first_cells(2 * x1, y1) + first_cells(2 * x1 + 1, y1))
    ends = pool_cells(jnp.concatenate(ends, axis=0))
    for x1 in range(2):
        PS[x1 + 1, 1, 32:64] = ends[2 * x1]
        PS[x1 + 1, 8, 32:64] = ends[2 * x1 + 1]

    halo_start(1, pooled_refs)

    load_w2.wait()
    for yo in range(2):
        MAPS[yo] = expand_map(yo, 128, 4)
    eye = pick(64, 64, lambda r, c: r == c)
    for a in range(3):
        taps_a = w2r[9 * a : 9 * a + 9].reshape(288, 64)
        W2A[64 * (2 - a) : 64 * (2 - a) + 64] = (0.5 * dot_lanes(eye, taps_a)).astype(BF16)
        W2B[32 * (2 - a) : 32 * (2 - a) + 32] = jnp.concatenate(
            [w2r[26 - 9 * a - j] for j in range(9)], axis=1
        )
    spread_2 = pick(64, 128, lambda r, c: r == (c >> 1))
    load_cot.wait()
    to_y2 = pick(256, 512, lambda r, c: c == ((r & 63) << 3) + (r >> 6))
    seeds = dot(to_y2, eight_rows(cot[...])).astype(BF16)
    SEED[...] = (0.125 * dot(seeds, spread_2)).reshape(4, 64, 128)

    def spread_edges(xs, ys):
        cells = PS[xs, ys, 32:64]
        shape = cells.shape
        sides = dot(cells.reshape(-1, 128), shift_2[...]).astype(BF16)
        PS[xs, ys, 0:32] = sides[:, :128].reshape(shape)
        PS[xs, ys, 64:96] = sides[:, 128:].reshape(shape)

    def taps(field, x, y2, skip=0, count=3):
        depth = count * field.shape[2]
        one = field[x, pl.ds(2 * y2 + skip, count)].reshape(depth, 128)
        two = field[x, pl.ds(2 * y2 + 1 + skip, count)].reshape(depth, 128)
        return jnp.concatenate([one, two], axis=1)

    for x1 in range(2):
        spread_edges(x1 + 1, slice(1, 9))

    def local_conv(y2):
        return dot(W2A[64:192], taps(PS, 1, y2)) + dot(W2A[0:128], taps(PS, 2, y2))

    def second_conv(y2, local):
        first = dot(W2A[128:192], taps(PS, 0, y2))
        last = dot(W2A[0:64], taps(PS, 3, y2))
        return local + jnp.concatenate([first, last], axis=0)

    for y2 in (1, 2):
        LOCAL[y2 - 1] = local_conv(y2)

    def second_block(rows):
        for y2 in rows:
            local = LOCAL[y2 - 1] if y2 in (1, 2) else local_conv(y2)
            total, slope = act_slope(second_conv(y2, local))
            TOT[y2] = total[:, :128] + total[:, 128:]
            seed = jnp.concatenate([SEED[y2]] * 2, axis=0)
            grad = (slope * jnp.concatenate([seed, seed], axis=1)).astype(BF16)
            G2[y2] = grad
            for yo in range(2):
                cells = grad[:, 128 * yo : 128 * yo + 128]
                sides = dot(cells, shift_2[...]).astype(BF16)
                y = 2 * y2 + yo + 2
                for x1 in range(2):
                    lo, hi = 64 * x1, 64 * x1 + 64
                    GS[x1, y, 64:128] = cells[lo:hi]
                    GS[x1, y, 0:64] = sides[lo:hi, :128]
                    GS[x1, y, 128:192] = sides[lo:hi, 128:]

    def gradient_halo(p):
        skip, count = (1, 2) if p == 0 else (0, 2) if p == 4 else (0, 3)
        weights = W2B[:, 192 * skip : 192 * (skip + count)]
        one = dot(weights, taps(GS, 0, p, skip, count))
        two = dot(weights, taps(GS, 1, p, skip, count))
        rows = (one[:32], one[32:64] + two[:32], one[64:] + two[32:64], two[64:])
        for yo in range(2):
            y = 2 * p + yo
            for x in range(4):
                cells = rows[x][:, 128 * yo : 128 * yo + 128]
                if 0 < x < 3 and 0 < y < 9:
                    BACK[x - 1, y - 1] = cells
                else:
                    OUTER[x, y] = cells.astype(BF16)

    halo_wait(1, pooled_refs, X_FACES)
    for x in (0, 3):
        spread_edges(x, slice(1, 9))
    second_block((1, 2))
    gradient_halo(2)
    halo_wait(1, pooled_refs, OTHERS)
    for y in (0, 9):
        spread_edges(slice(0, 4), y)
    second_block((0, 3))

    for p in (0, 1, 3, 4):
        gradient_halo(p)
    halo_start(2, grad_refs)

    share = 64 // pencils
    dw2[...] = jnp.zeros_like(dw2)

    def second_grad(y2, carry):
        terms = [None] * 3
        for x in range(4):
            lo, hi = (0 if x < 3 else 64), (128 if x > 0 else 64)
            part = dot_lanes(G2[y2, lo:hi], taps(PS, x, y2))
            for x1 in range(2):
                if 0 <= x - x1 < 3:
                    piece = part[64 * x1 - lo : 64 * x1 - lo + 64]
                    old = terms[x - x1]
                    terms[x - x1] = piece if old is None else old + piece
        for a in range(3):
            dw2[a] += terms[a]
        return carry

    lax.fori_loop(0, 4, second_grad, 0)
    columns = [dw2[a] for a in range(3)] + [jnp.zeros((64, 256 * LOW - 864), F32)]
    columns = jnp.concatenate(columns, axis=1).astype(BF16)
    for g in range(pencils):
        for part in range(LOW):
            rows = columns[share * g : share * g + share]
            part2[g, part] = rows[:, 256 * part : 256 * part + 256]

    def wait_slots(slots, count, sem):
        taken = slots.at[pl.ds(0, count)]
        pltpu.make_async_copy(taken, taken, sem).wait()

    def group_copies(group, slots, sems, src_of=None):
        size, me, device = group

        def start():
            for d in range(1, size):
                peer = wrap(me + d, size)
                pltpu.make_async_remote_copy(
                    src_ref=slots.at[me] if src_of is None else src_of(peer),
                    dst_ref=slots.at[me],
                    send_sem=sems.at[0],
                    recv_sem=sems.at[1],
                    device_id=device(peer),
                    device_id_type=MESH,
                ).start()

        def wait():
            for sem in (sems.at[0], sems.at[1]):
                wait_slots(slots, size - 1, sem)

        return start, wait

    def part_of(i):
        return part2.at[wrap(i, pencils), over(i, pencils)]

    start_a, wait_a = group_copies(group_z, sum_a, sem_a, part_of)
    start_b, wait_b = group_copies(group_xy, sum_b, sem_b)
    start_c, wait_c = group_copies(group_low, sum_c, sem_c)
    start_z, wait_z = group_copies(group_z, sum_1.at[0], sem_1.at[0])
    start_xy, wait_xy = group_copies(group_xy, sum_1.at[1], sem_1.at[1])

    def total_of(slots, size):
        total = slots[0].astype(F32)
        for i in range(1, size):
            total = total + slots[i].astype(F32)
        return total

    start_a()

    pool_2 = pick(128, 64, lambda r, c: (r >> 1) == c)
    pooled = 0.125 * joined(dot(split(TOT[...].reshape(256, 128), 2), pool_2), 2) + 0.7 * LOG_2
    from_y2 = pick(512, 256, lambda r, c: r == ((c & 63) << 3) + (c >> 6))
    pooled = dot(from_y2, pooled.astype(BF16)).reshape(64, 8, 64)
    p2_out[...] = pooled[:, :4].astype(BF16)

    def spread_back(back):
        cells = split(back.reshape(-1, 128), 2)
        return (0.125 * joined(dot(cells, spread_1[...]), 2)).reshape(-1, 32, 256)

    def first_grad(y1, seeds):
        total = None
        for x in range(4):
            seed = jnp.concatenate([seeds[x // 2]] * 2, axis=0)
            term = dot_lanes((SL[x, y1] * seed).astype(BF16), window(x, y1))
            total = term if total is None else total + term
        return total

    halo_wait(2, grad_refs, X_FACES)
    for x1 in range(2):
        CELLS[x1] = spread_back(BACK[x1] + face_x[x1].astype(F32))
    dw1[...] = jnp.zeros_like(dw1)

    def middle(i, carry):
        total = None
        for j in range(3):
            y1 = 1 + 3 * i + j
            term = first_grad(y1, (CELLS[0, y1], CELLS[1, y1]))
            total = term if total is None else total + term
        dw1[...] += total
        return carry

    lax.fori_loop(0, 2, middle, 0)

    halo_wait(2, grad_refs, OTHERS)
    for side, y1 in ((0, 0), (1, 7)):
        back = []
        for x1 in range(2):
            own = BACK[x1, y1] + face_x[x1, y1].astype(F32)
            back.append(own + face_y[side, x1].astype(F32) + corner[2 * x1 + side].astype(F32))
        seeds = spread_back(jnp.concatenate(back, axis=0))
        dw1[...] += first_grad(y1, (seeds[0], seeds[1]))

    folded = None
    for yo in range(2):
        term = joined(dot_lanes(split(dw1[32 * yo : 32 * yo + 32], 3), MAPS[yo]), 3)
        folded = term if folded is None else folded + term

    sum_1[0, group_z[1]] = folded.astype(BF16)
    start_z()
    wait_a()
    sum_a[group_z[1]] = part2[pencil, low]
    sum_b[group_xy[1]] = total_of(sum_a, group_z[0]).astype(BF16)
    start_b()
    wait_z()
    sum_1[1, group_xy[1]] = total_of(sum_1.at[0], group_z[0]).astype(BF16)
    start_xy()
    wait_b()
    sum_c[low] = total_of(sum_b, group_xy[0])
    start_c()
    wait_c()
    for tap in range(27):
        at = 32 * (tap % 8)
        g2_out[tap] = sum_c[tap // 8, :, at : at + 32]
    wait_xy()
    total = total_of(sum_1.at[1], group_xy[0]).T
    for tap in range(27):
        g1_out[tap] = total[4 * tap : 4 * tap + 4]


def write_out(*refs):
    count = len(refs) // 2
    sems = refs[-1]
    copies = [pltpu.make_async_copy(refs[i], refs[count + i], sems.at[i]) for i in range(count)]
    for copy in copies:
        copy.start()
    for copy in copies:
        copy.wait()


def solution(mesh):
    pencils = mesh.shape["pencil"]
    share = 64 // pencils
    size_z = LOW * pencils
    size_xy = mesh.shape["slab"] // LOW
    most = max(size_z, size_xy)

    def per_device(volume, weight_one, weight_two, cotangent):
        w1 = weight_one.transpose(1, 2, 0)
        w2 = weight_two.transpose(1, 2, 0)
        cot = cotangent.reshape(64, 4, 64)
        vmem = pl.BlockSpec(memory_space=pltpu.VMEM)
        hbm = pl.BlockSpec(memory_space=pltpu.HBM)
        shapes = (
            pltpu.VMEM((64, 4, 64), BF16),
            pltpu.VMEM((27, 4, 32), F32),
            pltpu.VMEM((27, share, 32), F32),
        )
        results = pl.pallas_call(
            kernel,
            out_shape=shapes,
            in_specs=[hbm] * 4,
            out_specs=(vmem,) * 3,
            scratch_shapes=[
                pltpu.VMEM((4, 4, 16, 256), BF16),
                pltpu.VMEM((27, 4, 32), BF16),
                pltpu.VMEM((27, 32, 64), BF16),
                pltpu.VMEM((64, 4, 64), BF16),
                pltpu.VMEM((6, 18, 16, 256), BF16),
                pltpu.VMEM((4, 10, 96, 128), BF16),
                pltpu.VMEM((2, 12, 192, 128), BF16),
                pltpu.VMEM((4, 8, 64, 256), F32),
                pltpu.VMEM((2, 8, 32, 256), F32),
                pltpu.VMEM((4, 64, 128), F32),
                pltpu.VMEM((4, 64, 128), F32),
                pltpu.VMEM((4, 128, 256), BF16),
                pltpu.VMEM((2, 128, 256), F32),
                pltpu.VMEM((2, 8, 32, 128), F32),
                pltpu.VMEM((4, 10, 32, 128), BF16),
                pltpu.VMEM((2, 8, 32, 128), BF16),
                pltpu.VMEM((2, 2, 32, 128), BF16),
                pltpu.VMEM((4, 32, 128), BF16),
                pltpu.VMEM((192, 288), BF16),
                pltpu.VMEM((96, 576), BF16),
                pltpu.VMEM((2, 128, 192), BF16),
                pltpu.VMEM((256, 128), BF16),
                pltpu.VMEM((128, 256), BF16),
                pltpu.VMEM((128, 256), BF16),
                pltpu.VMEM((2, 16, 256), BF16),
                pltpu.VMEM((2, 4, 16, 256), BF16),
                pltpu.VMEM((2, 16, 256), BF16),
                pltpu.VMEM((4, 16, 256), BF16),
                pltpu.VMEM((64, 192), F32),
                pltpu.VMEM((3, 64, 288), F32),
                pltpu.VMEM((pencils, LOW, share, 256), BF16),
                pltpu.VMEM((size_z, share, 256), BF16),
                pltpu.VMEM((size_xy, share, 256), BF16),
                pltpu.VMEM((LOW, share, 256), F32),
                pltpu.VMEM((2, most, 32, 128), BF16),
                pltpu.SemaphoreType.DMA((4,)),
                pltpu.SemaphoreType.DMA((8,)),
                pltpu.SemaphoreType.DMA((3, 8)),
                pltpu.SemaphoreType.DMA((2,)),
                pltpu.SemaphoreType.DMA((2,)),
                pltpu.SemaphoreType.DMA((2,)),
                pltpu.SemaphoreType.DMA((2, 2)),
            ],
            compiler_params=pltpu.CompilerParams(
                collective_id=0, has_side_effects=True, vmem_limit_bytes=56 * 2**20
            ),
        )(volume, w1, w2, cot)
        pooled, grad_one, grad_two = pl.pallas_call(
            write_out,
            out_shape=tuple(jax.ShapeDtypeStruct(s.shape, s.dtype) for s in shapes),
            in_specs=[vmem] * 3,
            out_specs=(hbm,) * 3,
            scratch_shapes=[pltpu.SemaphoreType.DMA((3,))],
            compiler_params=pltpu.CompilerParams(vmem_limit_bytes=4 * 2**20),
        )(*results)
        return (
            pooled.reshape(64, 1, 4, 64),
            grad_one.transpose(2, 0, 1),
            grad_two.transpose(1, 0, 2),
        )

    in_specs = (P(None, "slab", "pencil", None), P(), P(), P(None, "slab", "pencil", None))
    out_specs = (P(None, "slab", "pencil", None), P(), P("pencil", None, None))
    return jax.shard_map(
        per_device, mesh=mesh, in_specs=in_specs, out_specs=out_specs, check_vma=False
    )
```

```python
import functools

import jax
import jax.numpy as jnp
from jax import lax
from jax.experimental import pallas as pl
from jax.experimental.pallas import tpu as pltpu
from jax.sharding import PartitionSpec as P

MESH = pl.DeviceIdType.MESH
LOW = 4
F32 = jnp.float32
BF16 = jnp.bfloat16
SIDES = ((1, 1), (1, -1), (-1, 1), (-1, -1), (1, 0), (-1, 0), (0, 1), (0, -1))
X_FACES = (4, 5)
OTHERS = (6, 7, 0, 1, 2, 3)
ALL = tuple(range(8))
LOG_2 = 0.6931471805599453


def pick(rows, cols, hit):
    r = lax.broadcasted_iota(jnp.int32, (rows, cols), 0)
    c = lax.broadcasted_iota(jnp.int32, (rows, cols), 1)
    return jnp.where(hit(r, c), 1.0, 0.0).astype(BF16)


def dot(a, b):
    return jnp.dot(a, b, preferred_element_type=F32)


def dot_lanes(a, b):
    return lax.dot_general(a, b, (((1,), (1,)), ((), ())), preferred_element_type=F32)


def split(value, count):
    parts = []
    for _ in range(count):
        part = value.astype(BF16)
        parts.append(part)
        value = value - part.astype(F32)
    return jnp.concatenate(parts, axis=0)


def joined(value, count):
    rows = value.shape[0] // count
    total = value[:rows]
    for i in range(1, count):
        total = total + value[rows * i : rows * i + rows]
    return total


def act_slope(half):
    rows = half.shape[0] // 2
    t = jnp.tanh(half)
    size = jnp.abs(half)
    grown = 1.0 + jnp.abs(t)
    size = size[:rows] + size[rows:] - jnp.log(grown[:rows] * grown[rows:])
    return 1.3 * (half[:rows] + half[rows:]) + 0.7 * size, 0.65 + 0.35 * t


def wrap(index, size):
    return index & (size - 1) if size & (size - 1) == 0 else lax.rem(index, size)


def over(index, size):
    return index >> (size.bit_length() - 1) if size & (size - 1) == 0 else index // size


def expand_map(yo, rows, slots):
    def hit(r, j):
        b = ((j >> 4) & 3) - yo
        slot = j & 15
        row = slots * (9 * (j >> 6) + 3 * b + (slot >> 2)) + (slot & 3)
        return (b >= 0) & (b < 3) & (slot < 12) & (r == row)

    return pick(rows, 192, hit)


def eight_rows(value):
    value = value.astype(F32)
    value = jnp.concatenate([value, value], axis=1)
    return value.reshape(-1, value.shape[2]).astype(BF16)


def kernel(
    vol_hbm,
    w1_hbm,
    w2_hbm,
    cot_hbm,
    p2_out,
    g1_out,
    g2_out,
    vol,
    w1r,
    w2r,
    cot,
    V,
    PS,
    GS,
    SL,
    CELLS,
    TOT,
    SEED,
    G2,
    LOCAL,
    BACK,
    OUTER,
    face_x,
    face_y,
    corner,
    W2A,
    W2B,
    MAPS,
    pool_1,
    shift_2,
    spread_1,
    ypack,
    xrecv,
    yrecv,
    crecv,
    dw1,
    dw2,
    part2,
    sum_a,
    sum_b,
    sum_c,
    sum_1,
    sem_in,
    halo_send,
    halo_recv,
    sem_a,
    sem_b,
    sem_c,
    sem_1,
):
    slab = lax.axis_index("slab")
    pencil = lax.axis_index("pencil")
    slabs = lax.axis_size("slab")
    pencils = lax.axis_size("pencil")

    load_vol = pltpu.make_async_copy(vol_hbm, vol, sem_in.at[0])
    load_w1 = pltpu.make_async_copy(w1_hbm, w1r, sem_in.at[1])
    load_w2 = pltpu.make_async_copy(w2_hbm, w2r, sem_in.at[2])
    load_cot = pltpu.make_async_copy(cot_hbm, cot, sem_in.at[3])
    for load in (load_vol, load_w1, load_w2, load_cot):
        load.start()

    def exists(dx, dy):
        x = slab + dx
        y = pencil + dy
        ok = None
        if dx:
            ok = (x >= 0) & (x < slabs)
        if dy:
            oky = (y >= 0) & (y < pencils)
            ok = oky if ok is None else ok & oky
        return ok

    low = wrap(slab, LOW)
    group_z = (
        LOW * pencils,
        low * pencils + pencil,
        lambda i: (slab - low + over(i, pencils), wrap(i, pencils)),
    )
    group_xy = (slabs // LOW, over(slab, LOW), lambda i: (i * LOW + low, pencil))
    group_low = (LOW, low, lambda i: (slab - low + i, pencil))

    barrier = pltpu.get_barrier_semaphore()
    arrivals = 0
    for dx, dy in SIDES:
        ok = exists(dx, dy)
        arrivals = arrivals + ok.astype(jnp.int32)

        @pl.when(ok)
        def _():
            pl.semaphore_signal(
                barrier, inc=1, device_id=(slab + dx, pencil + dy), device_id_type=MESH
            )

    for size, me, device in (group_z, group_xy):
        arrivals = arrivals + (size - 1)
        for d in range(1, size):
            pl.semaphore_signal(
                barrier, inc=1, device_id=device(wrap(me + d, size)), device_id_type=MESH
            )

    def volume_refs(dx, dy):
        if dy == 0:
            return vol.at[:, 3 if dx == 1 else 0], xrecv.at[0 if dx == 1 else 1]
        src = ypack.at[1 if dy == 1 else 0]
        side = 0 if dy == 1 else 1
        if dx == 0:
            return src, yrecv.at[side]
        return src, crecv.at[2 * (0 if dx == 1 else 1) + side]

    def pooled_refs(dx, dy, ys=pl.ds(1, 8)):
        sx = {1: 2, -1: 1, 0: pl.ds(1, 2)}[dx]
        tx = {1: 0, -1: 3, 0: pl.ds(1, 2)}[dx]
        sy = {1: 8, -1: 1, 0: ys}[dy]
        ty = {1: 0, -1: 9, 0: ys}[dy]
        rows = pl.ds(32, 32)
        return PS.at[sx, sy, rows], PS.at[tx, ty, rows]

    middle_refs = functools.partial(pooled_refs, ys=pl.ds(2, 6))
    low_refs = functools.partial(pooled_refs, ys=1)
    high_refs = functools.partial(pooled_refs, ys=8)

    def grad_refs(dx, dy):
        src = OUTER.at[
            {1: 3, -1: 0, 0: pl.ds(1, 2)}[dx], {1: 9, -1: 0, 0: pl.ds(1, 8)}[dy]
        ]
        side_x = 0 if dx == 1 else 1
        side_y = 0 if dy == 1 else 1
        if dy == 0:
            return src, face_x.at[side_x]
        if dx == 0:
            return src, face_y.at[side_y]
        return src, corner.at[2 * side_x + side_y]

    def halo_copy(phase, k, refs):
        dx, dy = SIDES[k]
        src, dst = refs(dx, dy)
        extra = 2 * (phase - 3) + k - 4
        return pltpu.make_async_remote_copy(
            src_ref=src,
            dst_ref=dst,
            send_sem=halo_send.at[k if phase < 3 else 8 + extra],
            recv_sem=halo_recv.at[8 * phase + k if phase < 3 else 24 + extra],
            device_id=(slab + dx, pencil + dy),
            device_id_type=MESH,
        )

    def halo_start(phase, refs, sides):
        for k in sides:

            @pl.when(exists(*SIDES[k]))
            def _():
                halo_copy(phase, k, refs).start()

    def halo_wait(phase, refs, sides):
        for k in sides:
            dx, dy = SIDES[k]

            @pl.when(exists(dx, dy))
            def _():
                halo_copy(phase, k, refs).wait_send()

            @pl.when(exists(-dx, -dy))
            def _():
                halo_copy(phase, k, refs).wait_recv()

    load_vol.wait()
    edges = pick(32, 256, lambda r, c: c == ((r & 15) << 4) + 15 * (r >> 4))
    packed = dot(edges, vol[...].reshape(256, 256)).astype(BF16)
    ypack[0] = packed[:16]
    ypack[1] = packed[16:]
    pl.semaphore_wait(barrier, arrivals)
    halo_start(0, volume_refs, ALL)

    for dx, dy in SIDES:

        @pl.when(jnp.logical_not(exists(-dx, -dy)))
        def _():
            for refs in (volume_refs, pooled_refs, grad_refs):
                target = refs(dx, dy)[1]
                target[...] = jnp.zeros(target.shape, BF16)

    shift_1 = pick(256, 512, lambda r, c: r == jnp.where(c < 256, c - 1, c - 255))

    def shifted(block):
        sides = dot(block, shift_1).astype(BF16)
        return sides[:, :256], block, sides[:, 256:]

    def order(r, c):
        slot = r & 15
        return (slot < 12) & (c == ((slot >> 2) << 6) + ((slot & 3) << 4) + (r >> 4))

    def order_edge(r, c):
        slot = r & 15
        return (slot < 12) & (c == ((slot >> 2) << 4) + ((slot & 3) << 2) + (r >> 4))

    to_rows = pick(256, 192, order)
    to_edge = pick(64, 48, order_edge)

    def rows_of(parts, lo, hi):
        return jnp.concatenate([part[lo:hi] for part in parts], axis=0)

    local = shifted(jnp.concatenate([vol[:, x].reshape(64, 256) for x in range(4)], axis=0))
    for x in range(4):
        rows = dot(to_rows, rows_of(local, 64 * x, 64 * x + 64)).astype(BF16)
        V[x + 1, 1:17] = rows.reshape(16, 16, 256)

    load_w1.wait()
    eye = pick(32, 32, lambda r, c: r == c)
    w1f = dot_lanes(eye, eight_rows(w1r[...])).astype(BF16)
    w1p = jnp.concatenate(
        [(0.5 * dot(w1f, expand_map(yo, 216, 8))).astype(BF16) for yo in range(2)], axis=0
    )

    def window(x, y1):
        return V[pl.ds(x, 3), pl.ds(2 * y1, 4)].reshape(192, 256)

    def first_cells(x, y1):
        act, slope = act_slope(dot(w1p, window(x, y1)))
        SL[x, y1] = slope
        return act

    def inner(i, carry):
        for x in (1, 2):
            for j in range(2):
                CELLS[x - 1, 1 + 2 * i + j] = first_cells(x, 1 + 2 * i + j)
        return carry

    lax.fori_loop(0, 3, inner, 0)

    pool_1[...] = pick(256, 128, lambda r, c: (r >> 1) == c)
    shift_2[...] = pick(128, 256, lambda r, c: r == jnp.where(c < 128, c - 1, c - 127))
    spread_1[...] = pick(128, 256, lambda r, c: r == (c >> 1))

    def pool_cells(cells):
        parts = split(cells.reshape(-1, 256), 2)
        pooled = 0.125 * joined(dot(parts, pool_1[...]), 2) + 0.7 * LOG_2
        return pooled.astype(BF16).reshape(-1, 32, 128)

    halo_wait(0, volume_refs, X_FACES)
    arrived = shifted(jnp.concatenate([xrecv[s].reshape(64, 256) for s in range(2)], axis=0))
    for side, x in ((0, 0), (1, 5)):
        rows = dot(to_rows, rows_of(arrived, 64 * side, 64 * side + 64)).astype(BF16)
        V[x, 1:17] = rows.reshape(16, 16, 256)

    def outer(i, carry):
        for x in (0, 3):
            for j in range(3):
                CELLS[x // 2, 1 + 3 * i + j] += first_cells(x, 1 + 3 * i + j)
        return carry

    lax.fori_loop(0, 2, outer, 0)
    for x1 in range(2):
        PS[x1 + 1, 2:8, 32:64] = pool_cells(CELLS[x1, 1:7])
    halo_start(3, middle_refs, X_FACES)

    halo_wait(0, volume_refs, OTHERS)
    arrived = shifted(
        jnp.concatenate([yrecv[s] for s in range(2)] + [crecv[s] for s in range(4)], axis=0)
    )
    for side, y in ((0, 0), (1, 17)):
        at = 16 * side
        V[1:5, y] = dot(to_edge, rows_of(arrived, at, at + 16)).astype(BF16).reshape(4, 16, 256)
        at = 32 + 16 * side
        V[0, y] = dot(to_edge[48:], rows_of(arrived, at, at + 16)).astype(BF16)
        at = 64 + 16 * side
        V[5, y] = dot(to_edge[:16], rows_of(arrived, at, at + 16)).astype(BF16)
    ends = []
    for x1 in range(2):
        for y1 in (0, 7):
            ends.append(first_cells(2 * x1, y1) + first_cells(2 * x1 + 1, y1))
    ends = pool_cells(jnp.concatenate(ends, axis=0))
    for x1 in range(2):
        PS[x1 + 1, 1, 32:64] = ends[2 * x1]
        PS[x1 + 1, 8, 32:64] = ends[2 * x1 + 1]

    halo_start(1, pooled_refs, OTHERS)
    halo_start(1, low_refs, X_FACES)
    halo_start(4, high_refs, X_FACES)

    load_w2.wait()
    for yo in range(2):
        MAPS[yo] = expand_map(yo, 128, 4)
    eye = pick(64, 64, lambda r, c: r == c)
    for a in range(3):
        taps_a = w2r[9 * a : 9 * a + 9].reshape(288, 64)
        W2A[64 * (2 - a) : 64 * (2 - a) + 64] = (0.5 * dot_lanes(eye, taps_a)).astype(BF16)
        for b in range(3):
            at = 32 * (3 * b + a)
            taps_b = [w2r[26 - 9 * a - 3 * b - c] for c in range(3)]
            W2B[at : at + 32] = jnp.concatenate(taps_b, axis=1)
    spread_2 = pick(64, 128, lambda r, c: r == (c >> 1))
    load_cot.wait()
    to_y2 = pick(256, 512, lambda r, c: c == ((r & 63) << 3) + (r >> 6))
    seeds = dot(to_y2, eight_rows(cot[...])).astype(BF16)
    SEED[...] = (0.125 * dot(seeds, spread_2)).reshape(4, 64, 128)

    def spread_edges(xs, ys):
        cells = PS[xs, ys, 32:64]
        shape = cells.shape
        sides = dot(cells.reshape(-1, 128), shift_2[...]).astype(BF16)
        PS[xs, ys, 0:32] = sides[:, :128].reshape(shape)
        PS[xs, ys, 64:96] = sides[:, 128:].reshape(shape)

    def taps(x, y2):
        one = PS[x, pl.ds(2 * y2, 3)].reshape(288, 128)
        two = PS[x, pl.ds(2 * y2 + 1, 3)].reshape(288, 128)
        return jnp.concatenate([one, two], axis=1)

    for x1 in range(2):
        spread_edges(x1 + 1, slice(1, 9))

    def local_conv(y2):
        return dot(W2A[64:192], taps(1, y2)) + dot(W2A[0:128], taps(2, y2))

    def second_conv(y2, local):
        first = dot(W2A[128:192], taps(0, y2))
        last = dot(W2A[0:64], taps(3, y2))
        return local + jnp.concatenate([first, last], axis=0)

    for y2 in (1, 2):
        LOCAL[y2 - 1] = local_conv(y2)

    def second_block(rows):
        for y2 in rows:
            local = LOCAL[y2 - 1] if y2 in (1, 2) else local_conv(y2)
            total, slope = act_slope(second_conv(y2, local))
            TOT[y2] = total[:, :128] + total[:, 128:]
            seed = jnp.concatenate([SEED[y2]] * 2, axis=0)
            grad = (slope * jnp.concatenate([seed, seed], axis=1)).astype(BF16)
            G2[y2] = grad
            for yo in range(2):
                cells = grad[:, 128 * yo : 128 * yo + 128]
                sides = dot(cells, shift_2[...]).astype(BF16)
                y = 2 * y2 + yo
                for x1 in range(2):
                    lo, hi = 64 * x1, 64 * x1 + 64
                    GS[x1, y, 64:128] = cells[lo:hi]
                    GS[x1, y, 0:64] = sides[lo:hi, :128]
                    GS[x1, y, 128:192] = sides[lo:hi, 128:]

    def back_terms(y2):
        given = {}
        for x1 in range(2):
            cells = jnp.concatenate([GS[x1, 2 * y2], GS[x1, 2 * y2 + 1]], axis=1)
            terms = dot(W2B[...], cells)
            for b in range(3):
                for a in range(3):
                    at = 32 * (3 * b + a)
                    for yo in range(2):
                        term = terms[at : at + 32, 128 * yo : 128 * yo + 128]
                        place = (x1 + 2 - a, 2 * y2 + yo + 2 - b)
                        given[place] = given[place] + term if place in given else term
        for (x, y), term in given.items():
            met = {1: (), 2: (4, 5), 0: (2, 3), 3: (6, 7)}[y2]
            BACK[x, y] = BACK[x, y] + term if y in met else term

    halo_wait(3, middle_refs, X_FACES)
    for x in (0, 3):
        spread_edges(x, slice(2, 8))
    second_block((1, 2))
    back_terms(1)
    back_terms(2)
    halo_wait(1, pooled_refs, OTHERS)
    halo_wait(1, low_refs, X_FACES)
    halo_wait(4, high_refs, X_FACES)
    for y in (0, 9):
        spread_edges(slice(0, 4), y)
    for x in (0, 3):
        for y in (1, 8):
            spread_edges(x, y)
    second_block((0, 3))
    back_terms(0)
    back_terms(3)
    for x in (0, 3):
        OUTER[x] = BACK[x].astype(BF16)
    for y in (0, 9):
        OUTER[1:3, y] = BACK[1:3, y].astype(BF16)

    halo_start(2, grad_refs, ALL)

    share = 64 // pencils
    dw2[...] = jnp.zeros_like(dw2)

    def second_grad(i, carry):
        terms = [None] * 3
        for y2 in (2 * i, 2 * i + 1):
            for x in range(4):
                lo, hi = (0 if x < 3 else 64), (128 if x > 0 else 64)
                part = dot_lanes(G2[y2, lo:hi], taps(x, y2))
                for x1 in range(2):
                    if 0 <= x - x1 < 3:
                        piece = part[64 * x1 - lo : 64 * x1 - lo + 64]
                        old = terms[x - x1]
                        terms[x - x1] = piece if old is None else old + piece
        for a in range(3):
            dw2[a] += terms[a]
        return carry

    lax.fori_loop(0, 2, second_grad, 0)
    columns = [dw2[a] for a in range(3)] + [jnp.zeros((64, 256 * LOW - 864), F32)]
    columns = jnp.concatenate(columns, axis=1).astype(BF16)
    for g in range(pencils):
        for part in range(LOW):
            rows = columns[share * g : share * g + share]
            part2[g, part] = rows[:, 256 * part : 256 * part + 256]

    def wait_slots(slots, count, sem):
        taken = slots.at[pl.ds(0, count)]
        pltpu.make_async_copy(taken, taken, sem).wait()

    def group_copies(group, slots, sems, src_of=None):
        size, me, device = group

        def start():
            for d in range(1, size):
                peer = wrap(me + d, size)
                pltpu.make_async_remote_copy(
                    src_ref=slots.at[me] if src_of is None else src_of(peer),
                    dst_ref=slots.at[me],
                    send_sem=sems.at[0],
                    recv_sem=sems.at[1],
                    device_id=device(peer),
                    device_id_type=MESH,
                ).start()

        def wait():
            for sem in (sems.at[0], sems.at[1]):
                wait_slots(slots, size - 1, sem)

        return start, wait

    def part_of(i):
        return part2.at[wrap(i, pencils), over(i, pencils)]

    start_a, wait_a = group_copies(group_z, sum_a, sem_a, part_of)
    start_b, wait_b = group_copies(group_xy, sum_b, sem_b)
    start_c, wait_c = group_copies(group_low, sum_c, sem_c)
    start_z, wait_z = group_copies(group_z, sum_1.at[0], sem_1.at[0])
    start_xy, wait_xy = group_copies(group_xy, sum_1.at[1], sem_1.at[1])

    def total_of(slots, size):
        total = slots[0].astype(F32)
        for i in range(1, size):
            total = total + slots[i].astype(F32)
        return total

    start_a()

    pool_2 = pick(128, 64, lambda r, c: (r >> 1) == c)
    pooled = 0.125 * joined(dot(split(TOT[...].reshape(256, 128), 2), pool_2), 2) + 0.7 * LOG_2
    from_y2 = pick(512, 256, lambda r, c: r == ((c & 63) << 3) + (c >> 6))
    pooled = dot(from_y2, pooled.astype(BF16)).reshape(64, 8, 64)
    p2_out[...] = pooled[:, :4].astype(BF16)

    def spread_back(back):
        cells = split(back.reshape(-1, 128), 2)
        return (0.125 * joined(dot(cells, spread_1[...]), 2)).reshape(-1, 32, 256)

    def first_grad(y1, seeds):
        total = None
        for x in range(4):
            seed = jnp.concatenate([seeds[x // 2]] * 2, axis=0)
            term = dot_lanes((SL[x, y1] * seed).astype(BF16), window(x, y1))
            total = term if total is None else total + term
        return total

    halo_wait(2, grad_refs, X_FACES)
    for x1 in range(2):
        CELLS[x1] = spread_back(BACK[x1 + 1, 1:9] + face_x[x1].astype(F32))
    dw1[...] = jnp.zeros_like(dw1)

    def middle(i, carry):
        total = None
        for j in range(3):
            y1 = 1 + 3 * i + j
            term = first_grad(y1, (CELLS[0, y1], CELLS[1, y1]))
            total = term if total is None else total + term
        dw1[...] += total
        return carry

    lax.fori_loop(0, 2, middle, 0)

    halo_wait(2, grad_refs, OTHERS)
    for side, y1 in ((0, 0), (1, 7)):
        back = []
        for x1 in range(2):
            own = BACK[x1 + 1, y1 + 1] + face_x[x1, y1].astype(F32)
            back.append(own + face_y[side, x1].astype(F32) + corner[2 * x1 + side].astype(F32))
        seeds = spread_back(jnp.concatenate(back, axis=0))
        dw1[...] += first_grad(y1, (seeds[0], seeds[1]))

    folded = None
    for yo in range(2):
        term = joined(dot_lanes(split(dw1[32 * yo : 32 * yo + 32], 3), MAPS[yo]), 3)
        folded = term if folded is None else folded + term

    sum_1[0, group_z[1]] = folded.astype(BF16)
    start_z()
    wait_a()
    sum_a[group_z[1]] = part2[pencil, low]
    sum_b[group_xy[1]] = total_of(sum_a, group_z[0]).astype(BF16)
    start_b()
    wait_z()
    sum_1[1, group_xy[1]] = total_of(sum_1.at[0], group_z[0]).astype(BF16)
    start_xy()
    wait_b()
    sum_c[low] = total_of(sum_b, group_xy[0])
    start_c()
    wait_c()
    for tap in range(27):
        at = 32 * (tap % 8)
        g2_out[tap] = sum_c[tap // 8, :, at : at + 32]
    wait_xy()
    total = total_of(sum_1.at[1], group_xy[0]).T
    for tap in range(27):
        g1_out[tap] = total[4 * tap : 4 * tap + 4]


def write_out(*refs):
    count = len(refs) // 2
    sems = refs[-1]
    copies = [pltpu.make_async_copy(refs[i], refs[count + i], sems.at[i]) for i in range(count)]
    for copy in copies:
        copy.start()
    for copy in copies:
        copy.wait()


def solution(mesh):
    pencils = mesh.shape["pencil"]
    share = 64 // pencils
    size_z = LOW * pencils
    size_xy = mesh.shape["slab"] // LOW
    most = max(size_z, size_xy)

    def per_device(volume, weight_one, weight_two, cotangent):
        w1 = weight_one.transpose(1, 2, 0)
        w2 = weight_two.transpose(1, 2, 0)
        cot = cotangent.reshape(64, 4, 64)
        vmem = pl.BlockSpec(memory_space=pltpu.VMEM)
        hbm = pl.BlockSpec(memory_space=pltpu.HBM)
        shapes = (
            pltpu.VMEM((64, 4, 64), BF16),
            pltpu.VMEM((27, 4, 32), F32),
            pltpu.VMEM((27, share, 32), F32),
        )
        results = pl.pallas_call(
            kernel,
            out_shape=shapes,
            in_specs=[hbm] * 4,
            out_specs=(vmem,) * 3,
            scratch_shapes=[
                pltpu.VMEM((4, 4, 16, 256), BF16),
                pltpu.VMEM((27, 4, 32), BF16),
                pltpu.VMEM((27, 32, 64), BF16),
                pltpu.VMEM((64, 4, 64), BF16),
                pltpu.VMEM((6, 18, 16, 256), BF16),
                pltpu.VMEM((4, 10, 96, 128), BF16),
                pltpu.VMEM((2, 8, 192, 128), BF16),
                pltpu.VMEM((4, 8, 64, 256), F32),
                pltpu.VMEM((2, 8, 32, 256), F32),
                pltpu.VMEM((4, 64, 128), F32),
                pltpu.VMEM((4, 64, 128), F32),
                pltpu.VMEM((4, 128, 256), BF16),
                pltpu.VMEM((2, 128, 256), F32),
                pltpu.VMEM((4, 10, 32, 128), F32),
                pltpu.VMEM((4, 10, 32, 128), BF16),
                pltpu.VMEM((2, 8, 32, 128), BF16),
                pltpu.VMEM((2, 2, 32, 128), BF16),
                pltpu.VMEM((4, 32, 128), BF16),
                pltpu.VMEM((192, 288), BF16),
                pltpu.VMEM((288, 192), BF16),
                pltpu.VMEM((2, 128, 192), BF16),
                pltpu.VMEM((256, 128), BF16),
                pltpu.VMEM((128, 256), BF16),
                pltpu.VMEM((128, 256), BF16),
                pltpu.VMEM((2, 16, 256), BF16),
                pltpu.VMEM((2, 4, 16, 256), BF16),
                pltpu.VMEM((2, 16, 256), BF16),
                pltpu.VMEM((4, 16, 256), BF16),
                pltpu.VMEM((64, 192), F32),
                pltpu.VMEM((3, 64, 288), F32),
                pltpu.VMEM((pencils, LOW, share, 256), BF16),
                pltpu.VMEM((size_z, share, 256), BF16),
                pltpu.VMEM((size_xy, share, 256), BF16),
                pltpu.VMEM((LOW, share, 256), F32),
                pltpu.VMEM((2, most, 32, 128), BF16),
                pltpu.SemaphoreType.DMA((4,)),
                pltpu.SemaphoreType.DMA((12,)),
                pltpu.SemaphoreType.DMA((28,)),
                pltpu.SemaphoreType.DMA((2,)),
                pltpu.SemaphoreType.DMA((2,)),
                pltpu.SemaphoreType.DMA((2,)),
                pltpu.SemaphoreType.DMA((2, 2)),
            ],
            compiler_params=pltpu.CompilerParams(
                collective_id=0, has_side_effects=True, vmem_limit_bytes=56 * 2**20
            ),
        )(volume, w1, w2, cot)
        pooled, grad_one, grad_two = pl.pallas_call(
            write_out,
            out_shape=tuple(jax.ShapeDtypeStruct(s.shape, s.dtype) for s in shapes),
            in_specs=[vmem] * 3,
            out_specs=(hbm,) * 3,
            scratch_shapes=[pltpu.SemaphoreType.DMA((3,))],
            compiler_params=pltpu.CompilerParams(vmem_limit_bytes=4 * 2**20),
        )(*results)
        return (
            pooled.reshape(64, 1, 4, 64),
            grad_one.transpose(2, 0, 1),
            grad_two.transpose(1, 0, 2),
        )

    in_specs = (P(None, "slab", "pencil", None), P(), P(), P(None, "slab", "pencil", None))
    out_specs = (P(None, "slab", "pencil", None), P(), P("pencil", None, None))
    return jax.shard_map(
        per_device, mesh=mesh, in_specs=in_specs, out_specs=out_specs, check_vma=False
    )
```

```python
import functools

import jax
import jax.numpy as jnp
from jax import lax
from jax.experimental import pallas as pl
from jax.experimental.pallas import tpu as pltpu
from jax.sharding import PartitionSpec as P

MESH = pl.DeviceIdType.MESH
LOW = 4
F32 = jnp.float32
BF16 = jnp.bfloat16
SIDES = ((1, 1), (1, -1), (-1, 1), (-1, -1), (1, 0), (-1, 0), (0, 1), (0, -1))
X_FACES = (4, 5)
OTHERS = (0, 1, 2, 3, 6, 7)
ALL = tuple(range(8))
LOG_2 = 0.6931471805599453


def pick(rows, cols, hit):
    r = lax.broadcasted_iota(jnp.int32, (rows, cols), 0)
    c = lax.broadcasted_iota(jnp.int32, (rows, cols), 1)
    return jnp.where(hit(r, c), 1.0, 0.0).astype(BF16)


def dot(a, b):
    return jnp.dot(a, b, preferred_element_type=F32)


def dot_lanes(a, b):
    return lax.dot_general(a, b, (((1,), (1,)), ((), ())), preferred_element_type=F32)


def split(value, count):
    parts = []
    for _ in range(count):
        part = value.astype(BF16)
        parts.append(part)
        value = value - part.astype(F32)
    return jnp.concatenate(parts, axis=0)


def joined(value, count):
    rows = value.shape[0] // count
    total = value[:rows]
    for i in range(1, count):
        total = total + value[rows * i : rows * i + rows]
    return total


def act_slope(half):
    rows = half.shape[0] // 2
    t = jnp.tanh(half)
    size = jnp.abs(half)
    grown = 1.0 + jnp.abs(t)
    size = size[:rows] + size[rows:] - jnp.log(grown[:rows] * grown[rows:])
    return 1.3 * (half[:rows] + half[rows:]) + 0.7 * size, 0.65 + 0.35 * t


def wrap(index, size):
    return index & (size - 1) if size & (size - 1) == 0 else lax.rem(index, size)


def over(index, size):
    return index >> (size.bit_length() - 1) if size & (size - 1) == 0 else index // size


def expand_map(yo, rows, slots):
    def hit(r, j):
        b = ((j >> 4) & 3) - yo
        slot = j & 15
        row = slots * (9 * (j >> 6) + 3 * b + (slot >> 2)) + (slot & 3)
        return (b >= 0) & (b < 3) & (slot < 12) & (r == row)

    return pick(rows, 192, hit)


def eight_rows(value):
    value = value.astype(F32)
    value = jnp.concatenate([value, value], axis=1)
    return value.reshape(-1, value.shape[2]).astype(BF16)


def kernel(
    vol_hbm,
    w1_hbm,
    w2_hbm,
    cot_hbm,
    p2_out,
    g1_out,
    g2_out,
    vol,
    w1r,
    w2r,
    cot,
    V,
    PS,
    GS,
    SL,
    CELLS,
    TOT,
    SEED,
    G2,
    LOCAL,
    BACK,
    OUTER,
    face_x,
    face_y,
    corner,
    W2A,
    W2B,
    MAPS,
    pool_1,
    shift_2,
    spread_1,
    ypack,
    xrecv,
    yrecv,
    crecv,
    dw1,
    dw2,
    part2,
    sum_a,
    sum_b,
    sum_c,
    sum_1,
    sem_in,
    halo_send,
    halo_recv,
    sem_a,
    sem_b,
    sem_c,
    sem_1,
):
    slab = lax.axis_index("slab")
    pencil = lax.axis_index("pencil")
    slabs = lax.axis_size("slab")
    pencils = lax.axis_size("pencil")

    load_vol = pltpu.make_async_copy(vol_hbm, vol, sem_in.at[0])
    load_w1 = pltpu.make_async_copy(w1_hbm, w1r, sem_in.at[1])
    load_w2 = pltpu.make_async_copy(w2_hbm, w2r, sem_in.at[2])
    load_cot = pltpu.make_async_copy(cot_hbm, cot, sem_in.at[3])
    for load in (load_vol, load_w1, load_w2, load_cot):
        load.start()

    def exists(dx, dy):
        x = slab + dx
        y = pencil + dy
        ok = None
        if dx:
            ok = (x >= 0) & (x < slabs)
        if dy:
            oky = (y >= 0) & (y < pencils)
            ok = oky if ok is None else ok & oky
        return ok

    low = wrap(slab, LOW)
    group_z = (
        LOW * pencils,
        low * pencils + pencil,
        lambda i: (slab - low + over(i, pencils), wrap(i, pencils)),
    )
    group_xy = (slabs // LOW, over(slab, LOW), lambda i: (i * LOW + low, pencil))
    group_low = (LOW, low, lambda i: (slab - low + i, pencil))

    def others(group):
        size, me, _ = group
        if group is group_xy and size == 16:
            steps = [(dx, dy) for dx in range(4) for dy in range(4) if dx or dy]
            steps.sort(key=lambda step: -sum(min(d, 4 - d) for d in step))
            return [((me + 4 * dx) & 12) + ((me + dy) & 3) for dx, dy in steps]
        if group is group_z and size == 16:
            z = 2 * pencil + (low >> 1)
            steps = [(dz, core) for dz in range(8) for core in range(2) if dz or core]
            steps.sort(key=lambda step: -min(step[0], 8 - step[0]))
            found = []
            for dz, core in steps:
                there = (z + dz) & 7
                found.append(8 * (there & 1) + 4 * ((low + core) & 1) + (there >> 1))
            return found
        return [wrap(me + d, size) for d in range(1, size)]

    barrier = pltpu.get_barrier_semaphore()
    arrivals = 0
    for dx, dy in SIDES:
        ok = exists(dx, dy)
        arrivals = arrivals + ok.astype(jnp.int32)

        @pl.when(ok)
        def _():
            pl.semaphore_signal(
                barrier, inc=1, device_id=(slab + dx, pencil + dy), device_id_type=MESH
            )

    for group in (group_z, group_xy):
        arrivals = arrivals + (group[0] - 1)
        for peer in others(group):
            pl.semaphore_signal(
                barrier, inc=1, device_id=group[2](peer), device_id_type=MESH
            )

    def volume_refs(dx, dy):
        if dy == 0:
            return vol.at[:, 3 if dx == 1 else 0], xrecv.at[0 if dx == 1 else 1]
        src = ypack.at[1 if dy == 1 else 0]
        side = 0 if dy == 1 else 1
        if dx == 0:
            return src, yrecv.at[side]
        return src, crecv.at[2 * (0 if dx == 1 else 1) + side]

    def pooled_refs(dx, dy, ys=pl.ds(1, 8)):
        sx = {1: 2, -1: 1, 0: pl.ds(1, 2)}[dx]
        tx = {1: 0, -1: 3, 0: pl.ds(1, 2)}[dx]
        sy = {1: 8, -1: 1, 0: ys}[dy]
        ty = {1: 0, -1: 9, 0: ys}[dy]
        rows = pl.ds(32, 32)
        return PS.at[sx, sy, rows], PS.at[tx, ty, rows]

    middle_refs = functools.partial(pooled_refs, ys=pl.ds(2, 6))
    low_refs = functools.partial(pooled_refs, ys=1)
    high_refs = functools.partial(pooled_refs, ys=8)

    def grad_refs(dx, dy):
        src = OUTER.at[
            {1: 3, -1: 0, 0: pl.ds(1, 2)}[dx], {1: 9, -1: 0, 0: pl.ds(1, 8)}[dy]
        ]
        side_x = 0 if dx == 1 else 1
        side_y = 0 if dy == 1 else 1
        if dy == 0:
            return src, face_x.at[side_x]
        if dx == 0:
            return src, face_y.at[side_y]
        return src, corner.at[2 * side_x + side_y]

    def halo_copy(phase, k, refs):
        dx, dy = SIDES[k]
        src, dst = refs(dx, dy)
        extra = 2 * (phase - 3) + k - 4
        return pltpu.make_async_remote_copy(
            src_ref=src,
            dst_ref=dst,
            send_sem=halo_send.at[k if phase < 3 else 8 + extra],
            recv_sem=halo_recv.at[8 * phase + k if phase < 3 else 24 + extra],
            device_id=(slab + dx, pencil + dy),
            device_id_type=MESH,
        )

    def halo_start(phase, refs, sides):
        for k in sides:

            @pl.when(exists(*SIDES[k]))
            def _():
                halo_copy(phase, k, refs).start()

    def halo_wait(phase, refs, sides):
        for k in sides:
            dx, dy = SIDES[k]

            @pl.when(exists(dx, dy))
            def _():
                halo_copy(phase, k, refs).wait_send()

            @pl.when(exists(-dx, -dy))
            def _():
                halo_copy(phase, k, refs).wait_recv()

    load_vol.wait()
    edges = pick(32, 256, lambda r, c: c == ((r & 15) << 4) + 15 * (r >> 4))
    packed = dot(edges, vol[...].reshape(256, 256)).astype(BF16)
    ypack[0] = packed[:16]
    ypack[1] = packed[16:]
    pl.semaphore_wait(barrier, arrivals)
    halo_start(0, volume_refs, ALL)

    for dx, dy in SIDES:

        @pl.when(jnp.logical_not(exists(-dx, -dy)))
        def _():
            for refs in (volume_refs, pooled_refs, grad_refs):
                target = refs(dx, dy)[1]
                target[...] = jnp.zeros(target.shape, BF16)

    shift_1 = pick(256, 512, lambda r, c: r == jnp.where(c < 256, c - 1, c - 255))

    def shifted(block):
        sides = dot(block, shift_1).astype(BF16)
        return sides[:, :256], block, sides[:, 256:]

    def order(r, c):
        slot = r & 15
        return (slot < 12) & (c == ((slot >> 2) << 6) + ((slot & 3) << 4) + (r >> 4))

    def order_edge(r, c):
        slot = r & 15
        return (slot < 12) & (c == ((slot >> 2) << 4) + ((slot & 3) << 2) + (r >> 4))

    to_rows = pick(256, 192, order)
    to_edge = pick(64, 48, order_edge)

    def rows_of(parts, lo, hi):
        return jnp.concatenate([part[lo:hi] for part in parts], axis=0)

    local = shifted(jnp.concatenate([vol[:, x].reshape(64, 256) for x in range(4)], axis=0))
    for x in range(4):
        rows = dot(to_rows, rows_of(local, 64 * x, 64 * x + 64)).astype(BF16)
        V[x + 1, 1:17] = rows.reshape(16, 16, 256)

    load_w1.wait()
    eye = pick(32, 32, lambda r, c: r == c)
    w1f = dot_lanes(eye, eight_rows(w1r[...])).astype(BF16)
    w1p = jnp.concatenate(
        [(0.5 * dot(w1f, expand_map(yo, 216, 8))).astype(BF16) for yo in range(2)], axis=0
    )

    def window(x, y1):
        return V[pl.ds(x, 3), pl.ds(2 * y1, 4)].reshape(192, 256)

    def first_cells(x, y1):
        act, slope = act_slope(dot(w1p, window(x, y1)))
        SL[x, y1] = slope
        return act

    def inner(i, carry):
        for x in (1, 2):
            for j in range(2):
                CELLS[x - 1, 1 + 2 * i + j] = first_cells(x, 1 + 2 * i + j)
        return carry

    lax.fori_loop(0, 3, inner, 0)

    pool_1[...] = pick(256, 128, lambda r, c: (r >> 1) == c)
    shift_2[...] = pick(128, 256, lambda r, c: r == jnp.where(c < 128, c - 1, c - 127))
    spread_1[...] = pick(128, 256, lambda r, c: r == (c >> 1))

    def pool_cells(cells):
        parts = split(cells.reshape(-1, 256), 2)
        pooled = 0.125 * joined(dot(parts, pool_1[...]), 2) + 0.7 * LOG_2
        return pooled.astype(BF16).reshape(-1, 32, 128)

    halo_wait(0, volume_refs, X_FACES)
    arrived = shifted(jnp.concatenate([xrecv[s].reshape(64, 256) for s in range(2)], axis=0))
    for side, x in ((0, 0), (1, 5)):
        rows = dot(to_rows, rows_of(arrived, 64 * side, 64 * side + 64)).astype(BF16)
        V[x, 1:17] = rows.reshape(16, 16, 256)

    def outer(i, carry):
        for x in (0, 3):
            for j in range(3):
                CELLS[x // 2, 1 + 3 * i + j] += first_cells(x, 1 + 3 * i + j)
        return carry

    lax.fori_loop(0, 2, outer, 0)
    for x1 in range(2):
        PS[x1 + 1, 2:8, 32:64] = pool_cells(CELLS[x1, 1:7])
    halo_start(3, middle_refs, X_FACES)

    halo_wait(0, volume_refs, OTHERS)
    arrived = shifted(
        jnp.concatenate([yrecv[s] for s in range(2)] + [crecv[s] for s in range(4)], axis=0)
    )
    for side, y in ((0, 0), (1, 17)):
        at = 16 * side
        V[1:5, y] = dot(to_edge, rows_of(arrived, at, at + 16)).astype(BF16).reshape(4, 16, 256)
        at = 32 + 16 * side
        V[0, y] = dot(to_edge[48:], rows_of(arrived, at, at + 16)).astype(BF16)
        at = 64 + 16 * side
        V[5, y] = dot(to_edge[:16], rows_of(arrived, at, at + 16)).astype(BF16)
    ends = []
    for x1 in range(2):
        for y1 in (0, 7):
            ends.append(first_cells(2 * x1, y1) + first_cells(2 * x1 + 1, y1))
    ends = pool_cells(jnp.concatenate(ends, axis=0))
    for x1 in range(2):
        PS[x1 + 1, 1, 32:64] = ends[2 * x1]
        PS[x1 + 1, 8, 32:64] = ends[2 * x1 + 1]

    halo_start(1, pooled_refs, OTHERS)
    halo_start(1, low_refs, X_FACES)
    halo_start(4, high_refs, X_FACES)

    load_w2.wait()
    for yo in range(2):
        MAPS[yo] = expand_map(yo, 128, 4)
    eye = pick(64, 64, lambda r, c: r == c)
    for a in range(3):
        taps_a = w2r[9 * a : 9 * a + 9].reshape(288, 64)
        W2A[64 * (2 - a) : 64 * (2 - a) + 64] = (0.5 * dot_lanes(eye, taps_a)).astype(BF16)
        for b in range(3):
            at = 32 * (3 * b + a)
            taps_b = [w2r[26 - 9 * a - 3 * b - c] for c in range(3)]
            W2B[at : at + 32] = jnp.concatenate(taps_b, axis=1)
    spread_2 = pick(64, 128, lambda r, c: r == (c >> 1))
    load_cot.wait()
    to_y2 = pick(256, 512, lambda r, c: c == ((r & 63) << 3) + (r >> 6))
    seeds = dot(to_y2, eight_rows(cot[...])).astype(BF16)
    SEED[...] = (0.125 * dot(seeds, spread_2)).reshape(4, 64, 128)

    def spread_edges(xs, ys):
        cells = PS[xs, ys, 32:64]
        shape = cells.shape
        sides = dot(cells.reshape(-1, 128), shift_2[...]).astype(BF16)
        PS[xs, ys, 0:32] = sides[:, :128].reshape(shape)
        PS[xs, ys, 64:96] = sides[:, 128:].reshape(shape)

    def taps(x, y2):
        one = PS[x, pl.ds(2 * y2, 3)].reshape(288, 128)
        two = PS[x, pl.ds(2 * y2 + 1, 3)].reshape(288, 128)
        return jnp.concatenate([one, two], axis=1)

    for x1 in range(2):
        spread_edges(x1 + 1, slice(1, 9))

    def local_conv(y2):
        return dot(W2A[64:192], taps(1, y2)) + dot(W2A[0:128], taps(2, y2))

    def second_conv(y2, local):
        first = dot(W2A[128:192], taps(0, y2))
        last = dot(W2A[0:64], taps(3, y2))
        return local + jnp.concatenate([first, last], axis=0)

    for y2 in (1, 2):
        LOCAL[y2 - 1] = local_conv(y2)

    def second_block(rows):
        for y2 in rows:
            local = LOCAL[y2 - 1] if y2 in (1, 2) else local_conv(y2)
            total, slope = act_slope(second_conv(y2, local))
            TOT[y2] = total[:, :128] + total[:, 128:]
            seed = jnp.concatenate([SEED[y2]] * 2, axis=0)
            grad = (slope * jnp.concatenate([seed, seed], axis=1)).astype(BF16)
            G2[y2] = grad
            for yo in range(2):
                cells = grad[:, 128 * yo : 128 * yo + 128]
                sides = dot(cells, shift_2[...]).astype(BF16)
                y = 2 * y2 + yo
                for x1 in range(2):
                    lo, hi = 64 * x1, 64 * x1 + 64
                    GS[x1, y, 64:128] = cells[lo:hi]
                    GS[x1, y, 0:64] = sides[lo:hi, :128]
                    GS[x1, y, 128:192] = sides[lo:hi, 128:]

    def back_terms(y2):
        given = {}
        for x1 in range(2):
            cells = jnp.concatenate([GS[x1, 2 * y2], GS[x1, 2 * y2 + 1]], axis=1)
            terms = dot(W2B[...], cells)
            for b in range(3):
                for a in range(3):
                    at = 32 * (3 * b + a)
                    for yo in range(2):
                        term = terms[at : at + 32, 128 * yo : 128 * yo + 128]
                        place = (x1 + 2 - a, 2 * y2 + yo + 2 - b)
                        given[place] = given[place] + term if place in given else term
        for (x, y), term in given.items():
            met = {1: (), 2: (4, 5), 0: (2, 3), 3: (6, 7)}[y2]
            BACK[x, y] = BACK[x, y] + term if y in met else term

    def second_grad(rows):
        terms = [None] * 3
        for y2 in rows:
            for x in range(4):
                lo, hi = (0 if x < 3 else 64), (128 if x > 0 else 64)
                part = dot_lanes(G2[y2, lo:hi], taps(x, y2))
                for x1 in range(2):
                    if 0 <= x - x1 < 3:
                        piece = part[64 * x1 - lo : 64 * x1 - lo + 64]
                        old = terms[x - x1]
                        terms[x - x1] = piece if old is None else old + piece
        for a in range(3):
            dw2[rows[0], a] = terms[a]

    halo_wait(3, middle_refs, X_FACES)
    for x in (0, 3):
        spread_edges(x, slice(2, 8))
    second_block((1, 2))
    back_terms(1)
    back_terms(2)
    second_grad((1, 2))
    halo_wait(1, pooled_refs, OTHERS)
    halo_wait(1, low_refs, X_FACES)
    halo_wait(4, high_refs, X_FACES)
    for y in (0, 9):
        spread_edges(slice(0, 4), y)
    for x in (0, 3):
        for y in (1, 8):
            spread_edges(x, y)
    second_block((0, 3))
    back_terms(0)
    back_terms(3)
    for x in (0, 3):
        OUTER[x] = BACK[x].astype(BF16)
    for y in (0, 9):
        OUTER[1:3, y] = BACK[1:3, y].astype(BF16)

    halo_start(2, grad_refs, ALL)

    share = 64 // pencils
    second_grad((0, 3))
    columns = [dw2[0, a] + dw2[1, a] for a in range(3)] + [jnp.zeros((64, 256 * LOW - 864), F32)]
    columns = jnp.concatenate(columns, axis=1).astype(BF16)
    for g in range(pencils):
        for part in range(LOW):
            rows = columns[share * g : share * g + share]
            part2[g, part] = rows[:, 256 * part : 256 * part + 256]

    def wait_slots(slots, count, sem):
        taken = slots.at[pl.ds(0, count)]
        pltpu.make_async_copy(taken, taken, sem).wait()

    def group_copies(group, slots, sems, src_of=None):
        size, me, device = group

        def start():
            for peer in others(group):
                pltpu.make_async_remote_copy(
                    src_ref=slots.at[me] if src_of is None else src_of(peer),
                    dst_ref=slots.at[me],
                    send_sem=sems.at[0],
                    recv_sem=sems.at[1],
                    device_id=device(peer),
                    device_id_type=MESH,
                ).start()

        def wait():
            for sem in (sems.at[0], sems.at[1]):
                wait_slots(slots, size - 1, sem)

        return start, wait

    def part_of(i):
        return part2.at[wrap(i, pencils), over(i, pencils)]

    start_a, wait_a = group_copies(group_z, sum_a, sem_a, part_of)
    start_b, wait_b = group_copies(group_xy, sum_b, sem_b)
    start_c, wait_c = group_copies(group_low, sum_c, sem_c)
    start_z, wait_z = group_copies(group_z, sum_1.at[0], sem_1.at[0])
    start_xy, wait_xy = group_copies(group_xy, sum_1.at[1], sem_1.at[1])

    def total_of(slots, size):
        total = slots[0].astype(F32)
        for i in range(1, size):
            total = total + slots[i].astype(F32)
        return total

    start_a()

    pool_2 = pick(128, 64, lambda r, c: (r >> 1) == c)
    pooled = 0.125 * joined(dot(split(TOT[...].reshape(256, 128), 2), pool_2), 2) + 0.7 * LOG_2
    from_y2 = pick(512, 256, lambda r, c: r == ((c & 63) << 3) + (c >> 6))
    pooled = dot(from_y2, pooled.astype(BF16)).reshape(64, 8, 64)
    p2_out[...] = pooled[:, :4].astype(BF16)

    def spread_back(back):
        cells = split(back.reshape(-1, 128), 2)
        return (0.125 * joined(dot(cells, spread_1[...]), 2)).reshape(-1, 32, 256)

    def first_grad(y1, seeds):
        total = None
        for x in range(4):
            seed = jnp.concatenate([seeds[x // 2]] * 2, axis=0)
            term = dot_lanes((SL[x, y1] * seed).astype(BF16), window(x, y1))
            total = term if total is None else total + term
        return total

    halo_wait(2, grad_refs, X_FACES)
    for x1 in range(2):
        CELLS[x1] = spread_back(BACK[x1 + 1, 1:9] + face_x[x1].astype(F32))
    dw1[...] = jnp.zeros_like(dw1)

    def middle(i, carry):
        total = None
        for j in range(3):
            y1 = 1 + 3 * i + j
            term = first_grad(y1, (CELLS[0, y1], CELLS[1, y1]))
            total = term if total is None else total + term
        dw1[...] += total
        return carry

    lax.fori_loop(0, 2, middle, 0)

    halo_wait(2, grad_refs, OTHERS)
    for side, y1 in ((0, 0), (1, 7)):
        back = []
        for x1 in range(2):
            own = BACK[x1 + 1, y1 + 1] + face_x[x1, y1].astype(F32)
            back.append(own + face_y[side, x1].astype(F32) + corner[2 * x1 + side].astype(F32))
        seeds = spread_back(jnp.concatenate(back, axis=0))
        dw1[...] += first_grad(y1, (seeds[0], seeds[1]))

    folded = None
    for yo in range(2):
        term = joined(dot_lanes(split(dw1[32 * yo : 32 * yo + 32], 3), MAPS[yo]), 3)
        folded = term if folded is None else folded + term

    sum_1[0, group_z[1]] = folded.astype(BF16)
    start_z()
    wait_a()
    sum_a[group_z[1]] = part2[pencil, low]
    sum_b[group_xy[1]] = total_of(sum_a, group_z[0]).astype(BF16)
    start_b()
    wait_z()
    sum_1[1, group_xy[1]] = total_of(sum_1.at[0], group_z[0]).astype(BF16)
    start_xy()
    wait_b()
    sum_c[low] = total_of(sum_b, group_xy[0]).astype(BF16)
    start_c()
    wait_xy()
    total = total_of(sum_1.at[1], group_xy[0]).T
    for tap in range(27):
        g1_out[tap] = total[4 * tap : 4 * tap + 4]
    wait_c()
    totals = [sum_c[i].astype(F32) for i in range(LOW)]
    for tap in range(27):
        at = 32 * (tap % 8)
        g2_out[tap] = totals[tap // 8][:, at : at + 32]


def write_out(*refs):
    count = len(refs) // 2
    sems = refs[-1]
    copies = [pltpu.make_async_copy(refs[i], refs[count + i], sems.at[i]) for i in range(count)]
    for copy in copies:
        copy.start()
    for copy in copies:
        copy.wait()


def solution(mesh):
    pencils = mesh.shape["pencil"]
    share = 64 // pencils
    size_z = LOW * pencils
    size_xy = mesh.shape["slab"] // LOW
    most = max(size_z, size_xy)

    def per_device(volume, weight_one, weight_two, cotangent):
        w1 = weight_one.transpose(1, 2, 0)
        w2 = weight_two.transpose(1, 2, 0)
        cot = cotangent.reshape(64, 4, 64)
        vmem = pl.BlockSpec(memory_space=pltpu.VMEM)
        hbm = pl.BlockSpec(memory_space=pltpu.HBM)
        shapes = (
            pltpu.VMEM((64, 4, 64), BF16),
            pltpu.VMEM((27, 4, 32), F32),
            pltpu.VMEM((27, share, 32), F32),
        )
        results = pl.pallas_call(
            kernel,
            out_shape=shapes,
            in_specs=[hbm] * 4,
            out_specs=(vmem,) * 3,
            scratch_shapes=[
                pltpu.VMEM((4, 4, 16, 256), BF16),
                pltpu.VMEM((27, 4, 32), BF16),
                pltpu.VMEM((27, 32, 64), BF16),
                pltpu.VMEM((64, 4, 64), BF16),
                pltpu.VMEM((6, 18, 16, 256), BF16),
                pltpu.VMEM((4, 10, 96, 128), BF16),
                pltpu.VMEM((2, 8, 192, 128), BF16),
                pltpu.VMEM((4, 8, 64, 256), F32),
                pltpu.VMEM((2, 8, 32, 256), F32),
                pltpu.VMEM((4, 64, 128), F32),
                pltpu.VMEM((4, 64, 128), F32),
                pltpu.VMEM((4, 128, 256), BF16),
                pltpu.VMEM((2, 128, 256), F32),
                pltpu.VMEM((4, 10, 32, 128), F32),
                pltpu.VMEM((4, 10, 32, 128), BF16),
                pltpu.VMEM((2, 8, 32, 128), BF16),
                pltpu.VMEM((2, 2, 32, 128), BF16),
                pltpu.VMEM((4, 32, 128), BF16),
                pltpu.VMEM((192, 288), BF16),
                pltpu.VMEM((288, 192), BF16),
                pltpu.VMEM((2, 128, 192), BF16),
                pltpu.VMEM((256, 128), BF16),
                pltpu.VMEM((128, 256), BF16),
                pltpu.VMEM((128, 256), BF16),
                pltpu.VMEM((2, 16, 256), BF16),
                pltpu.VMEM((2, 4, 16, 256), BF16),
                pltpu.VMEM((2, 16, 256), BF16),
                pltpu.VMEM((4, 16, 256), BF16),
                pltpu.VMEM((64, 192), F32),
                pltpu.VMEM((2, 3, 64, 288), F32),
                pltpu.VMEM((pencils, LOW, share, 256), BF16),
                pltpu.VMEM((size_z, share, 256), BF16),
                pltpu.VMEM((size_xy, share, 256), BF16),
                pltpu.VMEM((LOW, share, 256), BF16),
                pltpu.VMEM((2, most, 32, 128), BF16),
                pltpu.SemaphoreType.DMA((4,)),
                pltpu.SemaphoreType.DMA((12,)),
                pltpu.SemaphoreType.DMA((28,)),
                pltpu.SemaphoreType.DMA((2,)),
                pltpu.SemaphoreType.DMA((2,)),
                pltpu.SemaphoreType.DMA((2,)),
                pltpu.SemaphoreType.DMA((2, 2)),
            ],
            compiler_params=pltpu.CompilerParams(
                collective_id=0, has_side_effects=True, vmem_limit_bytes=56 * 2**20
            ),
        )(volume, w1, w2, cot)
        pooled, grad_one, grad_two = pl.pallas_call(
            write_out,
            out_shape=tuple(jax.ShapeDtypeStruct(s.shape, s.dtype) for s in shapes),
            in_specs=[vmem] * 3,
            out_specs=(hbm,) * 3,
            scratch_shapes=[pltpu.SemaphoreType.DMA((3,))],
            compiler_params=pltpu.CompilerParams(vmem_limit_bytes=4 * 2**20),
        )(*results)
        return (
            pooled.reshape(64, 1, 4, 64),
            grad_one.transpose(2, 0, 1),
            grad_two.transpose(1, 0, 2),
        )

    in_specs = (P(None, "slab", "pencil", None), P(), P(), P(None, "slab", "pencil", None))
    out_specs = (P(None, "slab", "pencil", None), P(), P("pencil", None, None))
    return jax.shard_map(
        per_device, mesh=mesh, in_specs=in_specs, out_specs=out_specs, check_vma=False
    )
```

```python
import functools

import jax
import jax.numpy as jnp
from jax import lax
from jax.experimental import pallas as pl
from jax.experimental.pallas import tpu as pltpu
from jax.sharding import PartitionSpec as P

MESH = pl.DeviceIdType.MESH
LOW = 4
F32 = jnp.float32
BF16 = jnp.bfloat16
SIDES = ((1, 1), (1, -1), (-1, 1), (-1, -1), (1, 0), (-1, 0), (0, 1), (0, -1))
X_FACES = (4, 5)
OTHERS = (0, 1, 2, 3, 6, 7)
ALL = tuple(range(8))
LOG_2 = 0.6931471805599453


def pick(rows, cols, hit):
    r = lax.broadcasted_iota(jnp.int32, (rows, cols), 0)
    c = lax.broadcasted_iota(jnp.int32, (rows, cols), 1)
    return jnp.where(hit(r, c), 1.0, 0.0).astype(BF16)


def dot(a, b):
    return jnp.dot(a, b, preferred_element_type=F32)


def dot_lanes(a, b):
    return lax.dot_general(a, b, (((1,), (1,)), ((), ())), preferred_element_type=F32)


def split(value, count):
    parts = []
    for _ in range(count):
        part = value.astype(BF16)
        parts.append(part)
        value = value - part.astype(F32)
    return jnp.concatenate(parts, axis=0)


def joined(value, count):
    rows = value.shape[0] // count
    total = value[:rows]
    for i in range(1, count):
        total = total + value[rows * i : rows * i + rows]
    return total


def act_slope(half):
    rows = half.shape[0] // 2
    t = jnp.tanh(half)
    size = jnp.abs(half)
    grown = 1.0 + jnp.abs(t)
    size = size[:rows] + size[rows:] - jnp.log(grown[:rows] * grown[rows:])
    return 1.3 * (half[:rows] + half[rows:]) + 0.7 * size, 0.65 + 0.35 * t


def wrap(index, size):
    return index & (size - 1) if size & (size - 1) == 0 else lax.rem(index, size)


def over(index, size):
    return index >> (size.bit_length() - 1) if size & (size - 1) == 0 else index // size


def expand_map(yo, rows, slots):
    def hit(r, j):
        b = ((j >> 4) & 3) - yo
        slot = j & 15
        row = slots * (9 * (j >> 6) + 3 * b + (slot >> 2)) + (slot & 3)
        return (b >= 0) & (b < 3) & (slot < 12) & (r == row)

    return pick(rows, 192, hit)


def eight_rows(value):
    value = value.astype(F32)
    value = jnp.concatenate([value, value], axis=1)
    return value.reshape(-1, value.shape[2]).astype(BF16)


def kernel(
    vol_hbm,
    w1_hbm,
    w2_hbm,
    cot_hbm,
    p2_out,
    g1_out,
    g2_out,
    vol,
    w1r,
    w2r,
    cot,
    V,
    PS,
    GS,
    SL,
    CELLS,
    TOT,
    SEED,
    G2,
    LOCAL,
    BACK,
    OUTER,
    face_x,
    face_y,
    corner,
    W2A,
    W2B,
    MAPS,
    pool_1,
    shift_2,
    spread_1,
    ypack,
    xrecv,
    yrecv,
    crecv,
    dw1,
    dw2,
    part2,
    sum_a,
    sum_b,
    sum_c,
    sum_1,
    sem_in,
    halo_send,
    halo_recv,
    sem_a,
    sem_b,
    sem_c,
    sem_1,
):
    slab = lax.axis_index("slab")
    pencil = lax.axis_index("pencil")
    slabs = lax.axis_size("slab")
    pencils = lax.axis_size("pencil")

    load_vol = pltpu.make_async_copy(vol_hbm, vol, sem_in.at[0])
    load_w1 = pltpu.make_async_copy(w1_hbm, w1r, sem_in.at[1])
    load_w2 = pltpu.make_async_copy(w2_hbm, w2r, sem_in.at[2])
    load_cot = pltpu.make_async_copy(cot_hbm, cot, sem_in.at[3])
    for load in (load_vol, load_w1, load_w2, load_cot):
        load.start()

    def exists(dx, dy):
        x = slab + dx
        y = pencil + dy
        ok = None
        if dx:
            ok = (x >= 0) & (x < slabs)
        if dy:
            oky = (y >= 0) & (y < pencils)
            ok = oky if ok is None else ok & oky
        return ok

    low = wrap(slab, LOW)
    group_z = (
        LOW * pencils,
        low * pencils + pencil,
        lambda i: (slab - low + over(i, pencils), wrap(i, pencils)),
    )
    group_xy = (slabs // LOW, over(slab, LOW), lambda i: (i * LOW + low, pencil))
    group_low = (LOW, low, lambda i: (slab - low + i, pencil))

    def others(group):
        size, me, _ = group
        if group is group_xy and size == 16:
            steps = [(dx, dy) for dx in range(4) for dy in range(4) if dx or dy]
            steps.sort(key=lambda step: -sum(min(d, 4 - d) for d in step))
            return [((me + 4 * dx) & 12) + ((me + dy) & 3) for dx, dy in steps]
        if group is group_z and size == 16:
            z = 2 * pencil + (low >> 1)
            steps = [(dz, core) for dz in range(8) for core in range(2) if dz or core]
            steps.sort(key=lambda step: -min(step[0], 8 - step[0]))
            found = []
            for dz, core in steps:
                there = (z + dz) & 7
                found.append(8 * (there & 1) + 4 * ((low + core) & 1) + (there >> 1))
            return found
        return [wrap(me + d, size) for d in range(1, size)]

    barrier = pltpu.get_barrier_semaphore()
    arrivals = 0
    for dx, dy in SIDES:
        ok = exists(dx, dy)
        arrivals = arrivals + ok.astype(jnp.int32)

        @pl.when(ok)
        def _():
            pl.semaphore_signal(
                barrier, inc=1, device_id=(slab + dx, pencil + dy), device_id_type=MESH
            )

    for group in (group_z, group_xy):
        arrivals = arrivals + (group[0] - 1)
        for peer in others(group):
            pl.semaphore_signal(
                barrier, inc=1, device_id=group[2](peer), device_id_type=MESH
            )

    def volume_refs(dx, dy):
        if dy == 0:
            return vol.at[:, 3 if dx == 1 else 0], xrecv.at[0 if dx == 1 else 1]
        src = ypack.at[1 if dy == 1 else 0]
        side = 0 if dy == 1 else 1
        if dx == 0:
            return src, yrecv.at[side]
        return src, crecv.at[2 * (0 if dx == 1 else 1) + side]

    def pooled_refs(dx, dy, ys=pl.ds(1, 8)):
        sx = {1: 2, -1: 1, 0: pl.ds(1, 2)}[dx]
        tx = {1: 0, -1: 3, 0: pl.ds(1, 2)}[dx]
        sy = {1: 8, -1: 1, 0: ys}[dy]
        ty = {1: 0, -1: 9, 0: ys}[dy]
        rows = pl.ds(32, 32)
        return PS.at[sx, sy, rows], PS.at[tx, ty, rows]

    middle_refs = functools.partial(pooled_refs, ys=pl.ds(2, 6))
    low_refs = functools.partial(pooled_refs, ys=1)
    high_refs = functools.partial(pooled_refs, ys=8)

    def grad_refs(dx, dy):
        src = OUTER.at[
            {1: 3, -1: 0, 0: pl.ds(1, 2)}[dx], {1: 9, -1: 0, 0: pl.ds(1, 8)}[dy]
        ]
        side_x = 0 if dx == 1 else 1
        side_y = 0 if dy == 1 else 1
        if dy == 0:
            return src, face_x.at[side_x]
        if dx == 0:
            return src, face_y.at[side_y]
        return src, corner.at[2 * side_x + side_y]

    def halo_copy(phase, k, refs):
        dx, dy = SIDES[k]
        src, dst = refs(dx, dy)
        extra = 2 * (phase - 3) + k - 4
        return pltpu.make_async_remote_copy(
            src_ref=src,
            dst_ref=dst,
            send_sem=halo_send.at[k if phase < 3 else 8 + extra],
            recv_sem=halo_recv.at[8 * phase + k if phase < 3 else 24 + extra],
            device_id=(slab + dx, pencil + dy),
            device_id_type=MESH,
        )

    def halo_start(phase, refs, sides):
        for k in sides:

            @pl.when(exists(*SIDES[k]))
            def _():
                halo_copy(phase, k, refs).start()

    def halo_wait(phase, refs, sides):
        for k in sides:
            dx, dy = SIDES[k]

            @pl.when(exists(dx, dy))
            def _():
                halo_copy(phase, k, refs).wait_send()

            @pl.when(exists(-dx, -dy))
            def _():
                halo_copy(phase, k, refs).wait_recv()

    load_vol.wait()
    edges = pick(32, 256, lambda r, c: c == ((r & 15) << 4) + 15 * (r >> 4))
    packed = dot(edges, vol[...].reshape(256, 256)).astype(BF16)
    ypack[0] = packed[:16]
    ypack[1] = packed[16:]
    pl.semaphore_wait(barrier, arrivals)
    halo_start(0, volume_refs, ALL)

    for dx, dy in SIDES:

        @pl.when(jnp.logical_not(exists(-dx, -dy)))
        def _():
            for refs in (volume_refs, pooled_refs, grad_refs):
                target = refs(dx, dy)[1]
                target[...] = jnp.zeros(target.shape, BF16)

    shift_1 = pick(256, 512, lambda r, c: r == jnp.where(c < 256, c - 1, c - 255))

    def shifted(block):
        sides = dot(block, shift_1).astype(BF16)
        return sides[:, :256], block, sides[:, 256:]

    def order(r, c):
        slot = r & 15
        return (slot < 12) & (c == ((slot >> 2) << 6) + ((slot & 3) << 4) + (r >> 4))

    def order_edge(r, c):
        slot = r & 15
        return (slot < 12) & (c == ((slot >> 2) << 4) + ((slot & 3) << 2) + (r >> 4))

    to_rows = pick(256, 192, order)
    to_edge = pick(64, 48, order_edge)

    def rows_of(parts, lo, hi):
        return jnp.concatenate([part[lo:hi] for part in parts], axis=0)

    local = shifted(jnp.concatenate([vol[:, x].reshape(64, 256) for x in range(4)], axis=0))
    for x in range(4):
        rows = dot(to_rows, rows_of(local, 64 * x, 64 * x + 64)).astype(BF16)
        V[x + 1, 1:17] = rows.reshape(16, 16, 256)

    load_w1.wait()
    eye = pick(32, 32, lambda r, c: r == c)
    w1f = dot_lanes(eye, eight_rows(w1r[...])).astype(BF16)
    w1p = jnp.concatenate(
        [(0.5 * dot(w1f, expand_map(yo, 216, 8))).astype(BF16) for yo in range(2)], axis=0
    )

    def window(x, y1):
        return V[pl.ds(x, 3), pl.ds(2 * y1, 4)].reshape(192, 256)

    def first_cells(x, y1):
        act, slope = act_slope(dot(w1p, window(x, y1)))
        SL[x, y1] = slope
        return act

    def inner(i, carry):
        for x in (1, 2):
            for j in range(2):
                CELLS[x - 1, 1 + 2 * i + j] = first_cells(x, 1 + 2 * i + j)
        return carry

    lax.fori_loop(0, 3, inner, 0)

    pool_1[...] = pick(256, 128, lambda r, c: (r >> 1) == c)
    shift_2[...] = pick(128, 256, lambda r, c: r == jnp.where(c < 128, c - 1, c - 127))
    spread_1[...] = pick(128, 256, lambda r, c: r == (c >> 1))

    def pool_cells(cells):
        parts = split(cells.reshape(-1, 256), 2)
        pooled = 0.125 * joined(dot(parts, pool_1[...]), 2) + 0.7 * LOG_2
        return pooled.astype(BF16).reshape(-1, 32, 128)

    halo_wait(0, volume_refs, X_FACES)
    arrived = shifted(jnp.concatenate([xrecv[s].reshape(64, 256) for s in range(2)], axis=0))
    for side, x in ((0, 0), (1, 5)):
        rows = dot(to_rows, rows_of(arrived, 64 * side, 64 * side + 64)).astype(BF16)
        V[x, 1:17] = rows.reshape(16, 16, 256)

    def outer(i, carry):
        for x in (0, 3):
            for j in range(3):
                CELLS[x // 2, 1 + 3 * i + j] += first_cells(x, 1 + 3 * i + j)
        return carry

    for i in range(2):
        outer(i, 0)
    for x1 in range(2):
        PS[x1 + 1, 2:8, 32:64] = pool_cells(CELLS[x1, 1:7])
    halo_start(3, middle_refs, X_FACES)

    halo_wait(0, volume_refs, OTHERS)
    arrived = shifted(
        jnp.concatenate([yrecv[s] for s in range(2)] + [crecv[s] for s in range(4)], axis=0)
    )
    for side, y in ((0, 0), (1, 17)):
        at = 16 * side
        V[1:5, y] = dot(to_edge, rows_of(arrived, at, at + 16)).astype(BF16).reshape(4, 16, 256)
        at = 32 + 16 * side
        V[0, y] = dot(to_edge[48:], rows_of(arrived, at, at + 16)).astype(BF16)
        at = 64 + 16 * side
        V[5, y] = dot(to_edge[:16], rows_of(arrived, at, at + 16)).astype(BF16)
    ends = []
    for x1 in range(2):
        for y1 in (0, 7):
            ends.append(first_cells(2 * x1, y1) + first_cells(2 * x1 + 1, y1))
    ends = pool_cells(jnp.concatenate(ends, axis=0))
    for x1 in range(2):
        PS[x1 + 1, 1, 32:64] = ends[2 * x1]
        PS[x1 + 1, 8, 32:64] = ends[2 * x1 + 1]

    halo_start(1, pooled_refs, OTHERS)
    halo_start(1, low_refs, X_FACES)
    halo_start(4, high_refs, X_FACES)

    load_w2.wait()
    for yo in range(2):
        MAPS[yo] = expand_map(yo, 128, 4)
    eye = pick(64, 64, lambda r, c: r == c)
    for a in range(3):
        taps_a = w2r[9 * a : 9 * a + 9].reshape(288, 64)
        W2A[64 * (2 - a) : 64 * (2 - a) + 64] = (0.5 * dot_lanes(eye, taps_a)).astype(BF16)
        for b in range(3):
            at = 32 * (3 * b + a)
            taps_b = [w2r[26 - 9 * a - 3 * b - c] for c in range(3)]
            W2B[at : at + 32] = jnp.concatenate(taps_b, axis=1)
    spread_2 = pick(64, 128, lambda r, c: r == (c >> 1))
    load_cot.wait()
    to_y2 = pick(256, 512, lambda r, c: c == ((r & 63) << 3) + (r >> 6))
    seeds = dot(to_y2, eight_rows(cot[...])).astype(BF16)
    SEED[...] = (0.125 * dot(seeds, spread_2)).reshape(4, 64, 128)

    def spread_edges(xs, ys):
        cells = PS[xs, ys, 32:64]
        shape = cells.shape
        sides = dot(cells.reshape(-1, 128), shift_2[...]).astype(BF16)
        PS[xs, ys, 0:32] = sides[:, :128].reshape(shape)
        PS[xs, ys, 64:96] = sides[:, 128:].reshape(shape)

    def taps(x, y2):
        one = PS[x, pl.ds(2 * y2, 3)].reshape(288, 128)
        two = PS[x, pl.ds(2 * y2 + 1, 3)].reshape(288, 128)
        return jnp.concatenate([one, two], axis=1)

    for x1 in range(2):
        spread_edges(x1 + 1, slice(1, 9))

    def local_conv(y2):
        return dot(W2A[64:192], taps(1, y2)) + dot(W2A[0:128], taps(2, y2))

    def second_conv(y2, local):
        first = dot(W2A[128:192], taps(0, y2))
        last = dot(W2A[0:64], taps(3, y2))
        return local + jnp.concatenate([first, last], axis=0)

    for y2 in (1, 2):
        LOCAL[y2 - 1] = local_conv(y2)

    def second_block(rows):
        for y2 in rows:
            local = LOCAL[y2 - 1] if y2 in (1, 2) else local_conv(y2)
            total, slope = act_slope(second_conv(y2, local))
            TOT[y2] = total[:, :128] + total[:, 128:]
            seed = jnp.concatenate([SEED[y2]] * 2, axis=0)
            grad = (slope * jnp.concatenate([seed, seed], axis=1)).astype(BF16)
            G2[y2] = grad
            for yo in range(2):
                cells = grad[:, 128 * yo : 128 * yo + 128]
                sides = dot(cells, shift_2[...]).astype(BF16)
                y = 2 * y2 + yo
                for x1 in range(2):
                    lo, hi = 64 * x1, 64 * x1 + 64
                    GS[x1, y, 64:128] = cells[lo:hi]
                    GS[x1, y, 0:64] = sides[lo:hi, :128]
                    GS[x1, y, 128:192] = sides[lo:hi, 128:]

    def back_terms(y2):
        given = {}
        for x1 in range(2):
            cells = jnp.concatenate([GS[x1, 2 * y2], GS[x1, 2 * y2 + 1]], axis=1)
            terms = dot(W2B[...], cells)
            for b in range(3):
                for a in range(3):
                    at = 32 * (3 * b + a)
                    for yo in range(2):
                        term = terms[at : at + 32, 128 * yo : 128 * yo + 128]
                        place = (x1 + 2 - a, 2 * y2 + yo + 2 - b)
                        given[place] = given[place] + term if place in given else term
        for (x, y), term in given.items():
            met = {1: (), 2: (4, 5), 0: (2, 3), 3: (6, 7)}[y2]
            BACK[x, y] = BACK[x, y] + term if y in met else term

    def second_grad(rows):
        terms = [None] * 3
        for y2 in rows:
            for x in range(4):
                lo, hi = (0 if x < 3 else 64), (128 if x > 0 else 64)
                part = dot_lanes(G2[y2, lo:hi], taps(x, y2))
                for x1 in range(2):
                    if 0 <= x - x1 < 3:
                        piece = part[64 * x1 - lo : 64 * x1 - lo + 64]
                        old = terms[x - x1]
                        terms[x - x1] = piece if old is None else old + piece
        for a in range(3):
            dw2[rows[0], a] = terms[a]

    halo_wait(3, middle_refs, X_FACES)
    for x in (0, 3):
        spread_edges(x, slice(2, 8))
    second_block((1, 2))
    back_terms(1)
    back_terms(2)
    second_grad((1, 2))
    halo_wait(1, pooled_refs, OTHERS)
    halo_wait(1, low_refs, X_FACES)
    halo_wait(4, high_refs, X_FACES)
    for y in (0, 9):
        spread_edges(slice(0, 4), y)
    for x in (0, 3):
        for y in (1, 8):
            spread_edges(x, y)
    second_block((0, 3))
    back_terms(0)
    back_terms(3)
    for x in (0, 3):
        OUTER[x] = BACK[x].astype(BF16)
    for y in (0, 9):
        OUTER[1:3, y] = BACK[1:3, y].astype(BF16)

    halo_start(2, grad_refs, ALL)

    share = 64 // pencils
    second_grad((0, 3))
    columns = [dw2[0, a] + dw2[1, a] for a in range(3)] + [jnp.zeros((64, 256 * LOW - 864), F32)]
    columns = jnp.concatenate(columns, axis=1).astype(BF16)
    for g in range(pencils):
        for part in range(LOW):
            rows = columns[share * g : share * g + share]
            part2[g, part] = rows[:, 256 * part : 256 * part + 256]

    def wait_slots(slots, count, sem):
        taken = slots.at[pl.ds(0, count)]
        pltpu.make_async_copy(taken, taken, sem).wait()

    def group_copies(group, slots, sems, src_of=None):
        size, me, device = group

        def start():
            for peer in others(group):
                pltpu.make_async_remote_copy(
                    src_ref=slots.at[me] if src_of is None else src_of(peer),
                    dst_ref=slots.at[me],
                    send_sem=sems.at[0],
                    recv_sem=sems.at[1],
                    device_id=device(peer),
                    device_id_type=MESH,
                ).start()

        def wait():
            for sem in (sems.at[0], sems.at[1]):
                wait_slots(slots, size - 1, sem)

        return start, wait

    def part_of(i):
        return part2.at[wrap(i, pencils), over(i, pencils)]

    start_a, wait_a = group_copies(group_z, sum_a, sem_a, part_of)
    start_b, wait_b = group_copies(group_xy, sum_b, sem_b)
    start_c, wait_c = group_copies(group_low, sum_c, sem_c)
    start_z, wait_z = group_copies(group_z, sum_1.at[0], sem_1.at[0])
    start_xy, wait_xy = group_copies(group_xy, sum_1.at[1], sem_1.at[1])

    def total_of(slots, size):
        total = slots[0].astype(F32)
        for i in range(1, size):
            total = total + slots[i].astype(F32)
        return total

    start_a()

    pool_2 = pick(128, 64, lambda r, c: (r >> 1) == c)
    pooled = 0.125 * joined(dot(split(TOT[...].reshape(256, 128), 2), pool_2), 2) + 0.7 * LOG_2
    from_y2 = pick(512, 256, lambda r, c: r == ((c & 63) << 3) + (c >> 6))
    pooled = dot(from_y2, pooled.astype(BF16)).reshape(64, 8, 64)
    p2_out[...] = pooled[:, :4].astype(BF16)

    def spread_back(back):
        cells = split(back.reshape(-1, 128), 2)
        return (0.125 * joined(dot(cells, spread_1[...]), 2)).reshape(-1, 32, 256)

    def first_grad(y1, seeds):
        total = None
        for x in range(4):
            seed = jnp.concatenate([seeds[x // 2]] * 2, axis=0)
            term = dot_lanes((SL[x, y1] * seed).astype(BF16), window(x, y1))
            total = term if total is None else total + term
        return total

    halo_wait(2, grad_refs, X_FACES)
    for x1 in range(2):
        CELLS[x1] = spread_back(BACK[x1 + 1, 1:9] + face_x[x1].astype(F32))
    dw1[...] = jnp.zeros_like(dw1)

    def middle(i, carry):
        total = None
        for j in range(3):
            y1 = 1 + 3 * i + j
            term = first_grad(y1, (CELLS[0, y1], CELLS[1, y1]))
            total = term if total is None else total + term
        dw1[...] += total
        return carry

    for i in range(2):
        middle(i, 0)

    halo_wait(2, grad_refs, OTHERS)
    for side, y1 in ((0, 0), (1, 7)):
        back = []
        for x1 in range(2):
            own = BACK[x1 + 1, y1 + 1] + face_x[x1, y1].astype(F32)
            back.append(own + face_y[side, x1].astype(F32) + corner[2 * x1 + side].astype(F32))
        seeds = spread_back(jnp.concatenate(back, axis=0))
        dw1[...] += first_grad(y1, (seeds[0], seeds[1]))

    folded = None
    for yo in range(2):
        term = joined(dot_lanes(split(dw1[32 * yo : 32 * yo + 32], 3), MAPS[yo]), 3)
        folded = term if folded is None else folded + term

    sum_1[0, group_z[1]] = folded.astype(BF16)
    start_z()
    wait_a()
    sum_a[group_z[1]] = part2[pencil, low]
    sum_b[group_xy[1]] = total_of(sum_a, group_z[0]).astype(BF16)
    start_b()
    wait_z()
    sum_1[1, group_xy[1]] = total_of(sum_1.at[0], group_z[0]).astype(BF16)
    start_xy()
    wait_b()
    sum_c[low] = total_of(sum_b, group_xy[0]).astype(BF16)
    start_c()
    wait_xy()
    total = total_of(sum_1.at[1], group_xy[0]).T
    for tap in range(27):
        g1_out[tap] = total[4 * tap : 4 * tap + 4]
    wait_c()
    totals = [sum_c[i].astype(F32) for i in range(LOW)]
    for tap in range(27):
        at = 32 * (tap % 8)
        g2_out[tap] = totals[tap // 8][:, at : at + 32]


def write_out(*refs):
    count = len(refs) // 2
    sems = refs[-1]
    copies = [pltpu.make_async_copy(refs[i], refs[count + i], sems.at[i]) for i in range(count)]
    for copy in copies:
        copy.start()
    for copy in copies:
        copy.wait()


def solution(mesh):
    pencils = mesh.shape["pencil"]
    share = 64 // pencils
    size_z = LOW * pencils
    size_xy = mesh.shape["slab"] // LOW
    most = max(size_z, size_xy)

    def per_device(volume, weight_one, weight_two, cotangent):
        w1 = weight_one.transpose(1, 2, 0)
        w2 = weight_two.transpose(1, 2, 0)
        cot = cotangent.reshape(64, 4, 64)
        vmem = pl.BlockSpec(memory_space=pltpu.VMEM)
        hbm = pl.BlockSpec(memory_space=pltpu.HBM)
        shapes = (
            pltpu.VMEM((64, 4, 64), BF16),
            pltpu.VMEM((27, 4, 32), F32),
            pltpu.VMEM((27, share, 32), F32),
        )
        results = pl.pallas_call(
            kernel,
            out_shape=shapes,
            in_specs=[hbm] * 4,
            out_specs=(vmem,) * 3,
            scratch_shapes=[
                pltpu.VMEM((4, 4, 16, 256), BF16),
                pltpu.VMEM((27, 4, 32), BF16),
                pltpu.VMEM((27, 32, 64), BF16),
                pltpu.VMEM((64, 4, 64), BF16),
                pltpu.VMEM((6, 18, 16, 256), BF16),
                pltpu.VMEM((4, 10, 96, 128), BF16),
                pltpu.VMEM((2, 8, 192, 128), BF16),
                pltpu.VMEM((4, 8, 64, 256), F32),
                pltpu.VMEM((2, 8, 32, 256), F32),
                pltpu.VMEM((4, 64, 128), F32),
                pltpu.VMEM((4, 64, 128), F32),
                pltpu.VMEM((4, 128, 256), BF16),
                pltpu.VMEM((2, 128, 256), F32),
                pltpu.VMEM((4, 10, 32, 128), F32),
                pltpu.VMEM((4, 10, 32, 128), BF16),
                pltpu.VMEM((2, 8, 32, 128), BF16),
                pltpu.VMEM((2, 2, 32, 128), BF16),
                pltpu.VMEM((4, 32, 128), BF16),
                pltpu.VMEM((192, 288), BF16),
                pltpu.VMEM((288, 192), BF16),
                pltpu.VMEM((2, 128, 192), BF16),
                pltpu.VMEM((256, 128), BF16),
                pltpu.VMEM((128, 256), BF16),
                pltpu.VMEM((128, 256), BF16),
                pltpu.VMEM((2, 16, 256), BF16),
                pltpu.VMEM((2, 4, 16, 256), BF16),
                pltpu.VMEM((2, 16, 256), BF16),
                pltpu.VMEM((4, 16, 256), BF16),
                pltpu.VMEM((64, 192), F32),
                pltpu.VMEM((2, 3, 64, 288), F32),
                pltpu.VMEM((pencils, LOW, share, 256), BF16),
                pltpu.VMEM((size_z, share, 256), BF16),
                pltpu.VMEM((size_xy, share, 256), BF16),
                pltpu.VMEM((LOW, share, 256), BF16),
                pltpu.VMEM((2, most, 32, 128), BF16),
                pltpu.SemaphoreType.DMA((4,)),
                pltpu.SemaphoreType.DMA((12,)),
                pltpu.SemaphoreType.DMA((28,)),
                pltpu.SemaphoreType.DMA((2,)),
                pltpu.SemaphoreType.DMA((2,)),
                pltpu.SemaphoreType.DMA((2,)),
                pltpu.SemaphoreType.DMA((2, 2)),
            ],
            compiler_params=pltpu.CompilerParams(
                collective_id=0, has_side_effects=True, vmem_limit_bytes=56 * 2**20
            ),
        )(volume, w1, w2, cot)
        pooled, grad_one, grad_two = pl.pallas_call(
            write_out,
            out_shape=tuple(jax.ShapeDtypeStruct(s.shape, s.dtype) for s in shapes),
            in_specs=[vmem] * 3,
            out_specs=(hbm,) * 3,
            scratch_shapes=[pltpu.SemaphoreType.DMA((3,))],
            compiler_params=pltpu.CompilerParams(vmem_limit_bytes=4 * 2**20),
        )(*results)
        return (
            pooled.reshape(64, 1, 4, 64),
            grad_one.transpose(2, 0, 1),
            grad_two.transpose(1, 0, 2),
        )

    in_specs = (P(None, "slab", "pencil", None), P(), P(), P(None, "slab", "pencil", None))
    out_specs = (P(None, "slab", "pencil", None), P(), P("pencil", None, None))
    return jax.shard_map(
        per_device, mesh=mesh, in_specs=in_specs, out_specs=out_specs, check_vma=False
    )
```

```python
import functools

import jax
import jax.numpy as jnp
from jax import lax
from jax.experimental import pallas as pl
from jax.experimental.pallas import tpu as pltpu
from jax.sharding import PartitionSpec as P

MESH = pl.DeviceIdType.MESH
LOW = 4
F32 = jnp.float32
BF16 = jnp.bfloat16
SIDES = ((1, 1), (1, -1), (-1, 1), (-1, -1), (1, 0), (-1, 0), (0, 1), (0, -1))
X_FACES = (4, 5)
OTHERS = (0, 1, 2, 3, 6, 7)
ALL = tuple(range(8))
LOG_2 = 0.6931471805599453


def pick(rows, cols, hit):
    r = lax.broadcasted_iota(jnp.int32, (rows, cols), 0)
    c = lax.broadcasted_iota(jnp.int32, (rows, cols), 1)
    return jnp.where(hit(r, c), 1.0, 0.0).astype(BF16)


def dot(a, b):
    return jnp.dot(a, b, preferred_element_type=F32)


def dot_lanes(a, b):
    return lax.dot_general(a, b, (((1,), (1,)), ((), ())), preferred_element_type=F32)


def split(value, count):
    parts = []
    for _ in range(count):
        part = value.astype(BF16)
        parts.append(part)
        value = value - part.astype(F32)
    return jnp.concatenate(parts, axis=0)


def joined(value, count):
    rows = value.shape[0] // count
    total = value[:rows]
    for i in range(1, count):
        total = total + value[rows * i : rows * i + rows]
    return total


def act_slope(half):
    rows = half.shape[0] // 2
    t = jnp.tanh(half)
    size = jnp.abs(half)
    grown = 1.0 + jnp.abs(t)
    size = size[:rows] + size[rows:] - jnp.log(grown[:rows] * grown[rows:])
    return 1.3 * (half[:rows] + half[rows:]) + 0.7 * size, 0.65 + 0.35 * t


def wrap(index, size):
    return index & (size - 1) if size & (size - 1) == 0 else lax.rem(index, size)


def over(index, size):
    return index >> (size.bit_length() - 1) if size & (size - 1) == 0 else index // size


def expand_map(yo, rows, slots):
    def hit(r, j):
        b = ((j >> 4) & 3) - yo
        slot = j & 15
        row = slots * (9 * (j >> 6) + 3 * b + (slot >> 2)) + (slot & 3)
        return (b >= 0) & (b < 3) & (slot < 12) & (r == row)

    return pick(rows, 192, hit)


def eight_rows(value):
    value = value.astype(F32)
    value = jnp.concatenate([value, value], axis=1)
    return value.reshape(-1, value.shape[2]).astype(BF16)


def kernel(
    vol_hbm,
    w1_hbm,
    w2_hbm,
    cot_hbm,
    p2_out,
    g1_out,
    g2_out,
    vol,
    w1r,
    w2r,
    cot,
    V,
    PS,
    GS,
    SL,
    CELLS,
    TOT,
    SEED,
    G2,
    LOCAL,
    BACK,
    OUTER,
    face_x,
    face_y,
    corner,
    W2A,
    W2B,
    MAPS,
    pool_1,
    shift_2,
    spread_1,
    ypack,
    xrecv,
    yrecv,
    crecv,
    dw1,
    dw2,
    part2,
    sum_a,
    sum_b,
    sum_c,
    sum_1,
    sem_in,
    halo_send,
    halo_recv,
    sem_a,
    sem_b,
    sem_c,
    sem_1,
):
    slab = lax.axis_index("slab")
    pencil = lax.axis_index("pencil")
    slabs = lax.axis_size("slab")
    pencils = lax.axis_size("pencil")

    load_vol = pltpu.make_async_copy(vol_hbm, vol, sem_in.at[0])
    load_w1 = pltpu.make_async_copy(w1_hbm, w1r, sem_in.at[1])
    load_w2 = pltpu.make_async_copy(w2_hbm, w2r, sem_in.at[2])
    load_cot = pltpu.make_async_copy(cot_hbm, cot, sem_in.at[3])
    for load in (load_vol, load_w1, load_w2, load_cot):
        load.start()

    def exists(dx, dy):
        x = slab + dx
        y = pencil + dy
        ok = None
        if dx:
            ok = (x >= 0) & (x < slabs)
        if dy:
            oky = (y >= 0) & (y < pencils)
            ok = oky if ok is None else ok & oky
        return ok

    low = wrap(slab, LOW)
    group_z = (
        LOW * pencils,
        low * pencils + pencil,
        lambda i: (slab - low + over(i, pencils), wrap(i, pencils)),
    )
    group_xy = (slabs // LOW, over(slab, LOW), lambda i: (i * LOW + low, pencil))
    group_low = (LOW, low, lambda i: (slab - low + i, pencil))

    def others(group):
        size, me, _ = group
        if group is group_xy and size == 16:
            steps = [(dx, dy) for dx in range(4) for dy in range(4) if dx or dy]
            steps.sort(key=lambda step: -sum(min(d, 4 - d) for d in step))
            return [((me + 4 * dx) & 12) + ((me + dy) & 3) for dx, dy in steps]
        if group is group_z and size == 16:
            z = 2 * pencil + (low >> 1)
            steps = [(dz, core) for dz in range(8) for core in range(2) if dz or core]
            steps.sort(key=lambda step: -min(step[0], 8 - step[0]))
            found = []
            for dz, core in steps:
                there = (z + dz) & 7
                found.append(8 * (there & 1) + 4 * ((low + core) & 1) + (there >> 1))
            return found
        return [wrap(me + d, size) for d in range(1, size)]

    barrier = pltpu.get_barrier_semaphore()
    arrivals = 0
    for dx, dy in SIDES:
        ok = exists(dx, dy)
        arrivals = arrivals + ok.astype(jnp.int32)

        @pl.when(ok)
        def _():
            pl.semaphore_signal(
                barrier, inc=1, device_id=(slab + dx, pencil + dy), device_id_type=MESH
            )

    for group in (group_z, group_xy):
        arrivals = arrivals + (group[0] - 1)
        for peer in others(group):
            pl.semaphore_signal(
                barrier, inc=1, device_id=group[2](peer), device_id_type=MESH
            )

    def volume_refs(dx, dy):
        if dy == 0:
            return vol.at[:, 3 if dx == 1 else 0], xrecv.at[0 if dx == 1 else 1]
        src = ypack.at[1 if dy == 1 else 0]
        side = 0 if dy == 1 else 1
        if dx == 0:
            return src, yrecv.at[side]
        return src, crecv.at[2 * (0 if dx == 1 else 1) + side]

    def pooled_refs(dx, dy, ys=pl.ds(1, 8)):
        sx = {1: 2, -1: 1, 0: pl.ds(1, 2)}[dx]
        tx = {1: 0, -1: 3, 0: pl.ds(1, 2)}[dx]
        sy = {1: 8, -1: 1, 0: ys}[dy]
        ty = {1: 0, -1: 9, 0: ys}[dy]
        rows = pl.ds(32, 32)
        return PS.at[sx, sy, rows], PS.at[tx, ty, rows]

    middle_refs = functools.partial(pooled_refs, ys=pl.ds(2, 6))
    low_refs = functools.partial(pooled_refs, ys=1)
    high_refs = functools.partial(pooled_refs, ys=8)

    def grad_refs(dx, dy):
        src = OUTER.at[
            {1: 3, -1: 0, 0: pl.ds(1, 2)}[dx], {1: 9, -1: 0, 0: pl.ds(1, 8)}[dy]
        ]
        side_x = 0 if dx == 1 else 1
        side_y = 0 if dy == 1 else 1
        if dy == 0:
            return src, face_x.at[side_x]
        if dx == 0:
            return src, face_y.at[side_y]
        return src, corner.at[2 * side_x + side_y]

    def halo_copy(phase, k, refs):
        dx, dy = SIDES[k]
        src, dst = refs(dx, dy)
        extra = 2 * (phase - 3) + k - 4
        return pltpu.make_async_remote_copy(
            src_ref=src,
            dst_ref=dst,
            send_sem=halo_send.at[k if phase < 3 else 8 + extra],
            recv_sem=halo_recv.at[8 * (phase % 2) + k if phase < 3 else 16 + extra],
            device_id=(slab + dx, pencil + dy),
            device_id_type=MESH,
        )

    def halo_start(phase, refs, sides):
        for k in sides:

            @pl.when(exists(*SIDES[k]))
            def _():
                halo_copy(phase, k, refs).start()

    def halo_wait(phase, refs, sides):
        for k in sides:
            dx, dy = SIDES[k]

            @pl.when(exists(dx, dy))
            def _():
                halo_copy(phase, k, refs).wait_send()

            @pl.when(exists(-dx, -dy))
            def _():
                halo_copy(phase, k, refs).wait_recv()

    load_vol.wait()
    edges = pick(32, 256, lambda r, c: c == ((r & 15) << 4) + 15 * (r >> 4))
    packed = dot(edges, vol[...].reshape(256, 256)).astype(BF16)
    ypack[0] = packed[:16]
    ypack[1] = packed[16:]
    pl.semaphore_wait(barrier, arrivals)
    halo_start(0, volume_refs, ALL)

    for dx, dy in SIDES:

        @pl.when(jnp.logical_not(exists(-dx, -dy)))
        def _():
            for refs in (volume_refs, pooled_refs, grad_refs):
                target = refs(dx, dy)[1]
                target[...] = jnp.zeros(target.shape, BF16)

    shift_1 = pick(256, 512, lambda r, c: r == jnp.where(c < 256, c - 1, c - 255))

    def shifted(block):
        sides = dot(block, shift_1).astype(BF16)
        return sides[:, :256], block, sides[:, 256:]

    def order(r, c):
        slot = r & 15
        return (slot < 12) & (c == ((slot >> 2) << 6) + ((slot & 3) << 4) + (r >> 4))

    def order_edge(r, c):
        slot = r & 15
        return (slot < 12) & (c == ((slot >> 2) << 4) + ((slot & 3) << 2) + (r >> 4))

    to_rows = pick(256, 192, order)
    to_edge = pick(64, 48, order_edge)

    def rows_of(parts, lo, hi):
        return jnp.concatenate([part[lo:hi] for part in parts], axis=0)

    local = shifted(jnp.concatenate([vol[:, x].reshape(64, 256) for x in range(4)], axis=0))
    for x in range(4):
        rows = dot(to_rows, rows_of(local, 64 * x, 64 * x + 64)).astype(BF16)
        V[x + 1, 1:17] = rows.reshape(16, 16, 256)

    load_w1.wait()
    eye = pick(32, 32, lambda r, c: r == c)
    w1f = dot_lanes(eye, eight_rows(w1r[...])).astype(BF16)
    w1p = jnp.concatenate(
        [(0.5 * dot(w1f, expand_map(yo, 216, 8))).astype(BF16) for yo in range(2)], axis=0
    )

    def window(x, y1):
        return V[pl.ds(x, 3), pl.ds(2 * y1, 4)].reshape(192, 256)

    def first_cells(x, y1):
        act, slope = act_slope(dot(w1p, window(x, y1)))
        SL[x, y1] = slope
        return act

    def inner(i, carry):
        for x in (1, 2):
            for j in range(2):
                CELLS[x - 1, 1 + 2 * i + j] = first_cells(x, 1 + 2 * i + j)
        return carry

    lax.fori_loop(0, 3, inner, 0)

    pool_1[...] = pick(256, 128, lambda r, c: (r >> 1) == c)
    shift_2[...] = pick(128, 256, lambda r, c: r == jnp.where(c < 128, c - 1, c - 127))
    spread_1[...] = pick(128, 256, lambda r, c: r == (c >> 1))

    def pool_cells(cells):
        parts = split(cells.reshape(-1, 256), 2)
        pooled = 0.125 * joined(dot(parts, pool_1[...]), 2) + 0.7 * LOG_2
        return pooled.astype(BF16).reshape(-1, 32, 128)

    halo_wait(0, volume_refs, X_FACES)
    arrived = shifted(jnp.concatenate([xrecv[s].reshape(64, 256) for s in range(2)], axis=0))
    for side, x in ((0, 0), (1, 5)):
        rows = dot(to_rows, rows_of(arrived, 64 * side, 64 * side + 64)).astype(BF16)
        V[x, 1:17] = rows.reshape(16, 16, 256)

    def outer(i, carry):
        for x in (0, 3):
            for j in range(3):
                CELLS[x // 2, 1 + 3 * i + j] += first_cells(x, 1 + 3 * i + j)
        return carry

    for i in range(2):
        outer(i, 0)
    for x1 in range(2):
        PS[x1 + 1, 2:8, 32:64] = pool_cells(CELLS[x1, 1:7])
    halo_start(3, middle_refs, X_FACES)

    halo_wait(0, volume_refs, OTHERS)
    arrived = shifted(
        jnp.concatenate([yrecv[s] for s in range(2)] + [crecv[s] for s in range(4)], axis=0)
    )
    for side, y in ((0, 0), (1, 17)):
        at = 16 * side
        V[1:5, y] = dot(to_edge, rows_of(arrived, at, at + 16)).astype(BF16).reshape(4, 16, 256)
        at = 32 + 16 * side
        V[0, y] = dot(to_edge[48:], rows_of(arrived, at, at + 16)).astype(BF16)
        at = 64 + 16 * side
        V[5, y] = dot(to_edge[:16], rows_of(arrived, at, at + 16)).astype(BF16)
    ends = []
    for x1 in range(2):
        for y1 in (0, 7):
            ends.append(first_cells(2 * x1, y1) + first_cells(2 * x1 + 1, y1))
    ends = pool_cells(jnp.concatenate(ends, axis=0))
    for x1 in range(2):
        PS[x1 + 1, 1, 32:64] = ends[2 * x1]
        PS[x1 + 1, 8, 32:64] = ends[2 * x1 + 1]

    halo_start(1, pooled_refs, OTHERS)
    halo_start(1, low_refs, X_FACES)
    halo_start(4, high_refs, X_FACES)

    load_w2.wait()
    for yo in range(2):
        MAPS[yo] = expand_map(yo, 128, 4)
    eye = pick(64, 64, lambda r, c: r == c)
    for a in range(3):
        taps_a = w2r[9 * a : 9 * a + 9].reshape(288, 64)
        W2A[64 * (2 - a) : 64 * (2 - a) + 64] = (0.5 * dot_lanes(eye, taps_a)).astype(BF16)
        for b in range(3):
            at = 32 * (3 * b + a)
            taps_b = [w2r[26 - 9 * a - 3 * b - c] for c in range(3)]
            W2B[at : at + 32] = jnp.concatenate(taps_b, axis=1)
    spread_2 = pick(64, 128, lambda r, c: r == (c >> 1))
    load_cot.wait()
    to_y2 = pick(256, 512, lambda r, c: c == ((r & 63) << 3) + (r >> 6))
    seeds = dot(to_y2, eight_rows(cot[...])).astype(BF16)
    SEED[...] = (0.125 * dot(seeds, spread_2)).reshape(4, 64, 128)

    def spread_edges(xs, ys):
        cells = PS[xs, ys, 32:64]
        shape = cells.shape
        sides = dot(cells.reshape(-1, 128), shift_2[...]).astype(BF16)
        PS[xs, ys, 0:32] = sides[:, :128].reshape(shape)
        PS[xs, ys, 64:96] = sides[:, 128:].reshape(shape)

    def taps(x, y2):
        one = PS[x, pl.ds(2 * y2, 3)].reshape(288, 128)
        two = PS[x, pl.ds(2 * y2 + 1, 3)].reshape(288, 128)
        return jnp.concatenate([one, two], axis=1)

    for x1 in range(2):
        spread_edges(x1 + 1, slice(1, 9))

    def local_conv(y2):
        return dot(W2A[64:192], taps(1, y2)) + dot(W2A[0:128], taps(2, y2))

    def second_conv(y2, local):
        first = dot(W2A[128:192], taps(0, y2))
        last = dot(W2A[0:64], taps(3, y2))
        return local + jnp.concatenate([first, last], axis=0)

    for y2 in (1, 2):
        LOCAL[y2 - 1] = local_conv(y2)

    def second_block(rows):
        for y2 in rows:
            local = LOCAL[y2 - 1] if y2 in (1, 2) else local_conv(y2)
            total, slope = act_slope(second_conv(y2, local))
            TOT[y2] = total[:, :128] + total[:, 128:]
            seed = jnp.concatenate([SEED[y2]] * 2, axis=0)
            grad = (slope * jnp.concatenate([seed, seed], axis=1)).astype(BF16)
            G2[y2] = grad
            for yo in range(2):
                cells = grad[:, 128 * yo : 128 * yo + 128]
                sides = dot(cells, shift_2[...]).astype(BF16)
                y = 2 * y2 + yo
                for x1 in range(2):
                    lo, hi = 64 * x1, 64 * x1 + 64
                    GS[x1, y, 64:128] = cells[lo:hi]
                    GS[x1, y, 0:64] = sides[lo:hi, :128]
                    GS[x1, y, 128:192] = sides[lo:hi, 128:]

    def back_terms(y2):
        given = {}
        for x1 in range(2):
            cells = jnp.concatenate([GS[x1, 2 * y2], GS[x1, 2 * y2 + 1]], axis=1)
            terms = dot(W2B[...], cells)
            for b in range(3):
                for a in range(3):
                    at = 32 * (3 * b + a)
                    for yo in range(2):
                        term = terms[at : at + 32, 128 * yo : 128 * yo + 128]
                        place = (x1 + 2 - a, 2 * y2 + yo + 2 - b)
                        given[place] = given[place] + term if place in given else term
        for (x, y), term in given.items():
            met = {1: (), 2: (4, 5), 0: (2, 3), 3: (6, 7)}[y2]
            BACK[x, y] = BACK[x, y] + term if y in met else term

    def second_grad(rows):
        terms = [None] * 3
        for y2 in rows:
            for x in range(4):
                lo, hi = (0 if x < 3 else 64), (128 if x > 0 else 64)
                part = dot_lanes(G2[y2, lo:hi], taps(x, y2))
                for x1 in range(2):
                    if 0 <= x - x1 < 3:
                        piece = part[64 * x1 - lo : 64 * x1 - lo + 64]
                        old = terms[x - x1]
                        terms[x - x1] = piece if old is None else old + piece
        for a in range(3):
            dw2[rows[0], a] = terms[a]

    halo_wait(3, middle_refs, X_FACES)
    for x in (0, 3):
        spread_edges(x, slice(2, 8))
    second_block((1, 2))
    back_terms(1)
    back_terms(2)
    second_grad((1, 2))
    halo_wait(1, pooled_refs, OTHERS)
    halo_wait(1, low_refs, X_FACES)
    halo_wait(4, high_refs, X_FACES)
    for y in (0, 9):
        spread_edges(slice(0, 4), y)
    for x in (0, 3):
        for y in (1, 8):
            spread_edges(x, y)
    second_block((0, 3))
    back_terms(0)
    back_terms(3)
    for x in (0, 3):
        OUTER[x] = BACK[x].astype(BF16)
    for y in (0, 9):
        OUTER[1:3, y] = BACK[1:3, y].astype(BF16)

    halo_start(2, grad_refs, ALL)

    share = 64 // pencils
    second_grad((0, 3))
    columns = [dw2[0, a] + dw2[1, a] for a in range(3)] + [jnp.zeros((64, 256 * LOW - 864), F32)]
    columns = jnp.concatenate(columns, axis=1).astype(BF16)
    for g in range(pencils):
        for part in range(LOW):
            rows = columns[share * g : share * g + share]
            part2[g, part] = rows[:, 256 * part : 256 * part + 256]

    def wait_slots(slots, count, sem):
        taken = slots.at[pl.ds(0, count)]
        pltpu.make_async_copy(taken, taken, sem).wait()

    def group_copies(group, slots, sems, src_of=None):
        size, me, device = group

        def start():
            for peer in others(group):
                pltpu.make_async_remote_copy(
                    src_ref=slots.at[me] if src_of is None else src_of(peer),
                    dst_ref=slots.at[me],
                    send_sem=sems.at[0],
                    recv_sem=sems.at[1],
                    device_id=device(peer),
                    device_id_type=MESH,
                ).start()

        def wait():
            for sem in (sems.at[0], sems.at[1]):
                wait_slots(slots, size - 1, sem)

        return start, wait

    def part_of(i):
        return part2.at[wrap(i, pencils), over(i, pencils)]

    start_a, wait_a = group_copies(group_z, sum_a, sem_a, part_of)
    start_b, wait_b = group_copies(group_xy, sum_b, sem_b)
    start_c, wait_c = group_copies(group_low, sum_c, sem_c)
    start_z, wait_z = group_copies(group_z, sum_1.at[0], sem_1.at[0])
    start_xy, wait_xy = group_copies(group_xy, sum_1.at[1], sem_1.at[1])

    def total_of(slots, size):
        total = slots[0].astype(F32)
        for i in range(1, size):
            total = total + slots[i].astype(F32)
        return total

    start_a()

    pool_2 = pick(128, 64, lambda r, c: (r >> 1) == c)
    pooled = 0.125 * joined(dot(split(TOT[...].reshape(256, 128), 2), pool_2), 2) + 0.7 * LOG_2
    from_y2 = pick(512, 256, lambda r, c: r == ((c & 63) << 3) + (c >> 6))
    pooled = dot(from_y2, pooled.astype(BF16)).reshape(64, 8, 64)
    p2_out[...] = pooled[:, :4].astype(BF16)

    def spread_back(back):
        cells = split(back.reshape(-1, 128), 2)
        return (0.125 * joined(dot(cells, spread_1[...]), 2)).reshape(-1, 32, 256)

    def first_grad(y1, seeds):
        total = None
        for x in range(4):
            seed = jnp.concatenate([seeds[x // 2]] * 2, axis=0)
            term = dot_lanes((SL[x, y1] * seed).astype(BF16), window(x, y1))
            total = term if total is None else total + term
        return total

    halo_wait(2, grad_refs, X_FACES)
    for x1 in range(2):
        CELLS[x1] = spread_back(BACK[x1 + 1, 1:9] + face_x[x1].astype(F32))
    dw1[...] = jnp.zeros_like(dw1)

    def middle(i, carry):
        total = None
        for j in range(3):
            y1 = 1 + 3 * i + j
            term = first_grad(y1, (CELLS[0, y1], CELLS[1, y1]))
            total = term if total is None else total + term
        dw1[...] += total
        return carry

    for i in range(2):
        middle(i, 0)

    halo_wait(2, grad_refs, OTHERS)
    for side, y1 in ((0, 0), (1, 7)):
        back = []
        for x1 in range(2):
            own = BACK[x1 + 1, y1 + 1] + face_x[x1, y1].astype(F32)
            back.append(own + face_y[side, x1].astype(F32) + corner[2 * x1 + side].astype(F32))
        seeds = spread_back(jnp.concatenate(back, axis=0))
        dw1[...] += first_grad(y1, (seeds[0], seeds[1]))

    folded = None
    for yo in range(2):
        term = joined(dot_lanes(split(dw1[32 * yo : 32 * yo + 32], 3), MAPS[yo]), 3)
        folded = term if folded is None else folded + term

    sum_1[0, group_z[1]] = folded.astype(BF16)
    start_z()
    wait_a()
    sum_a[group_z[1]] = part2[pencil, low]
    sum_b[group_xy[1]] = total_of(sum_a, group_z[0]).astype(BF16)
    start_b()
    wait_z()
    sum_1[1, group_xy[1]] = total_of(sum_1.at[0], group_z[0]).astype(BF16)
    start_xy()
    wait_b()
    sum_c[low] = total_of(sum_b, group_xy[0]).astype(BF16)
    start_c()
    wait_xy()
    total = total_of(sum_1.at[1], group_xy[0]).T
    for tap in range(27):
        g1_out[tap] = total[4 * tap : 4 * tap + 4]
    wait_c()
    totals = [sum_c[i].astype(F32) for i in range(LOW)]
    for tap in range(27):
        at = 32 * (tap % 8)
        g2_out[tap] = totals[tap // 8][:, at : at + 32]


def write_out(*refs):
    count = len(refs) // 2
    sems = refs[-1]
    copies = [pltpu.make_async_copy(refs[i], refs[count + i], sems.at[i]) for i in range(count)]
    for copy in copies:
        copy.start()
    for copy in copies:
        copy.wait()


def solution(mesh):
    pencils = mesh.shape["pencil"]
    share = 64 // pencils
    size_z = LOW * pencils
    size_xy = mesh.shape["slab"] // LOW
    most = max(size_z, size_xy)

    def per_device(volume, weight_one, weight_two, cotangent):
        w1 = weight_one.transpose(1, 2, 0)
        w2 = weight_two.transpose(1, 2, 0)
        cot = cotangent.reshape(64, 4, 64)
        vmem = pl.BlockSpec(memory_space=pltpu.VMEM)
        hbm = pl.BlockSpec(memory_space=pltpu.HBM)
        shapes = (
            pltpu.VMEM((64, 4, 64), BF16),
            pltpu.VMEM((27, 4, 32), F32),
            pltpu.VMEM((27, share, 32), F32),
        )
        results = pl.pallas_call(
            kernel,
            out_shape=shapes,
            in_specs=[hbm] * 4,
            out_specs=(vmem,) * 3,
            scratch_shapes=[
                pltpu.VMEM((4, 4, 16, 256), BF16),
                pltpu.VMEM((27, 4, 32), BF16),
                pltpu.VMEM((27, 32, 64), BF16),
                pltpu.VMEM((64, 4, 64), BF16),
                pltpu.VMEM((6, 18, 16, 256), BF16),
                pltpu.VMEM((4, 10, 96, 128), BF16),
                pltpu.VMEM((2, 8, 192, 128), BF16),
                pltpu.VMEM((4, 8, 64, 256), F32),
                pltpu.VMEM((2, 8, 32, 256), F32),
                pltpu.VMEM((4, 64, 128), F32),
                pltpu.VMEM((4, 64, 128), F32),
                pltpu.VMEM((4, 128, 256), BF16),
                pltpu.VMEM((2, 128, 256), F32),
                pltpu.VMEM((4, 10, 32, 128), F32),
                pltpu.VMEM((4, 10, 32, 128), BF16),
                pltpu.VMEM((2, 8, 32, 128), BF16),
                pltpu.VMEM((2, 2, 32, 128), BF16),
                pltpu.VMEM((4, 32, 128), BF16),
                pltpu.VMEM((192, 288), BF16),
                pltpu.VMEM((288, 192), BF16),
                pltpu.VMEM((2, 128, 192), BF16),
                pltpu.VMEM((256, 128), BF16),
                pltpu.VMEM((128, 256), BF16),
                pltpu.VMEM((128, 256), BF16),
                pltpu.VMEM((2, 16, 256), BF16),
                pltpu.VMEM((2, 4, 16, 256), BF16),
                pltpu.VMEM((2, 16, 256), BF16),
                pltpu.VMEM((4, 16, 256), BF16),
                pltpu.VMEM((64, 192), F32),
                pltpu.VMEM((2, 3, 64, 288), F32),
                pltpu.VMEM((pencils, LOW, share, 256), BF16),
                pltpu.VMEM((size_z, share, 256), BF16),
                pltpu.VMEM((size_xy, share, 256), BF16),
                pltpu.VMEM((LOW, share, 256), BF16),
                pltpu.VMEM((2, most, 32, 128), BF16),
                pltpu.SemaphoreType.DMA((4,)),
                pltpu.SemaphoreType.DMA((12,)),
                pltpu.SemaphoreType.DMA((20,)),
                pltpu.SemaphoreType.DMA((2,)),
                pltpu.SemaphoreType.DMA((2,)),
                pltpu.SemaphoreType.DMA((2,)),
                pltpu.SemaphoreType.DMA((2, 2)),
            ],
            compiler_params=pltpu.CompilerParams(
                collective_id=0, has_side_effects=True, vmem_limit_bytes=56 * 2**20
            ),
        )(volume, w1, w2, cot)
        pooled, grad_one, grad_two = pl.pallas_call(
            write_out,
            out_shape=tuple(jax.ShapeDtypeStruct(s.shape, s.dtype) for s in shapes),
            in_specs=[vmem] * 3,
            out_specs=(hbm,) * 3,
            scratch_shapes=[pltpu.SemaphoreType.DMA((3,))],
            compiler_params=pltpu.CompilerParams(vmem_limit_bytes=4 * 2**20),
        )(*results)
        return (
            pooled.reshape(64, 1, 4, 64),
            grad_one.transpose(2, 0, 1),
            grad_two.transpose(1, 0, 2),
        )

    in_specs = (P(None, "slab", "pencil", None), P(), P(), P(None, "slab", "pencil", None))
    out_specs = (P(None, "slab", "pencil", None), P(), P("pencil", None, None))
    return jax.shard_map(
        per_device, mesh=mesh, in_specs=in_specs, out_specs=out_specs, check_vma=False
    )
```

```python
import functools

import jax
import jax.numpy as jnp
from jax import lax
from jax.experimental import pallas as pl
from jax.experimental.pallas import tpu as pltpu
from jax.sharding import PartitionSpec as P

MESH = pl.DeviceIdType.MESH
LOW = 4
F32 = jnp.float32
BF16 = jnp.bfloat16
SIDES = ((1, 1), (1, -1), (-1, 1), (-1, -1), (1, 0), (-1, 0), (0, 1), (0, -1))
X_FACES = (4, 5)
OTHERS = (0, 1, 2, 3, 6, 7)
ALL = tuple(range(8))
LOG_2 = 0.6931471805599453


def pick(rows, cols, hit):
    r = lax.broadcasted_iota(jnp.int32, (rows, cols), 0)
    c = lax.broadcasted_iota(jnp.int32, (rows, cols), 1)
    return jnp.where(hit(r, c), 1.0, 0.0).astype(BF16)


def dot(a, b):
    return jnp.dot(a, b, preferred_element_type=F32)


def dot_lanes(a, b):
    return lax.dot_general(a, b, (((1,), (1,)), ((), ())), preferred_element_type=F32)


def split(value, count):
    parts = []
    for _ in range(count):
        part = value.astype(BF16)
        parts.append(part)
        value = value - part.astype(F32)
    return jnp.concatenate(parts, axis=0)


def joined(value, count):
    rows = value.shape[0] // count
    total = value[:rows]
    for i in range(1, count):
        total = total + value[rows * i : rows * i + rows]
    return total


def act_slope(half):
    rows = half.shape[0] // 2
    t = jnp.tanh(half)
    size = jnp.abs(half)
    grown = 1.0 + jnp.abs(t)
    size = size[:rows] + size[rows:] - jnp.log(grown[:rows] * grown[rows:])
    return 1.3 * (half[:rows] + half[rows:]) + 0.7 * size, 0.65 + 0.35 * t


def wrap(index, size):
    return index & (size - 1) if size & (size - 1) == 0 else lax.rem(index, size)


def over(index, size):
    return index >> (size.bit_length() - 1) if size & (size - 1) == 0 else index // size


def expand_map(yo, rows, slots):
    def hit(r, j):
        b = ((j >> 4) & 3) - yo
        slot = j & 15
        row = slots * (9 * (j >> 6) + 3 * b + (slot >> 2)) + (slot & 3)
        return (b >= 0) & (b < 3) & (slot < 12) & (r == row)

    return pick(rows, 192, hit)


def eight_rows(value):
    value = value.astype(F32)
    value = jnp.concatenate([value, value], axis=1)
    return value.reshape(-1, value.shape[2]).astype(BF16)


def kernel(
    vol_hbm,
    w1_hbm,
    w2_hbm,
    cot_hbm,
    p2_out,
    g1_out,
    g2_out,
    vol,
    w1r,
    w2r,
    cot,
    V,
    PS,
    GS,
    SL,
    CELLS,
    TOT,
    SEED,
    G2,
    LOCAL,
    BACK,
    OUTER,
    face_x,
    face_y,
    corner,
    W2A,
    W2B,
    MAPS,
    pool_1,
    shift_2,
    spread_1,
    ypack,
    xrecv,
    yrecv,
    crecv,
    dw1,
    dw2,
    part2,
    sum_a,
    sum_b,
    sum_c,
    sum_1,
    sem_in,
    halo_send,
    halo_recv,
    sem_a,
    sem_b,
    sem_c,
    sem_1,
):
    slab = lax.axis_index("slab")
    pencil = lax.axis_index("pencil")
    slabs = lax.axis_size("slab")
    pencils = lax.axis_size("pencil")

    load_vol = pltpu.make_async_copy(vol_hbm, vol, sem_in.at[0])
    load_w1 = pltpu.make_async_copy(w1_hbm, w1r, sem_in.at[1])
    load_w2 = pltpu.make_async_copy(w2_hbm, w2r, sem_in.at[2])
    load_cot = pltpu.make_async_copy(cot_hbm, cot, sem_in.at[3])
    for load in (load_vol, load_w1, load_w2, load_cot):
        load.start()

    def exists(dx, dy):
        x = slab + dx
        y = pencil + dy
        ok = None
        if dx:
            ok = (x >= 0) & (x < slabs)
        if dy:
            oky = (y >= 0) & (y < pencils)
            ok = oky if ok is None else ok & oky
        return ok

    low = wrap(slab, LOW)
    group_z = (
        LOW * pencils,
        low * pencils + pencil,
        lambda i: (slab - low + over(i, pencils), wrap(i, pencils)),
    )
    group_xy = (slabs // LOW, over(slab, LOW), lambda i: (i * LOW + low, pencil))
    group_low = (LOW, low, lambda i: (slab - low + i, pencil))

    def others(group):
        size, me, _ = group
        if group is group_xy and size == 16:
            steps = [(dx, dy) for dx in range(4) for dy in range(4) if dx or dy]
            steps.sort(key=lambda step: -sum(min(d, 4 - d) for d in step))
            return [((me + 4 * dx) & 12) + ((me + dy) & 3) for dx, dy in steps]
        if group is group_z and size == 16:
            z = 2 * pencil + (low >> 1)
            steps = [(dz, core) for dz in range(8) for core in range(2) if dz or core]
            steps.sort(key=lambda step: -min(step[0], 8 - step[0]))
            found = []
            for dz, core in steps:
                there = (z + dz) & 7
                found.append(8 * (there & 1) + 4 * ((low + core) & 1) + (there >> 1))
            return found
        return [wrap(me + d, size) for d in range(1, size)]

    barrier = pltpu.get_barrier_semaphore()
    arrivals = 0
    for dx, dy in SIDES:
        ok = exists(dx, dy)
        arrivals = arrivals + ok.astype(jnp.int32)

        @pl.when(ok)
        def _():
            pl.semaphore_signal(
                barrier, inc=1, device_id=(slab + dx, pencil + dy), device_id_type=MESH
            )

    for group in (group_z, group_xy):
        arrivals = arrivals + (group[0] - 1)
        for peer in others(group):
            pl.semaphore_signal(
                barrier, inc=1, device_id=group[2](peer), device_id_type=MESH
            )

    def volume_refs(dx, dy):
        if dy == 0:
            return vol.at[:, 3 if dx == 1 else 0], xrecv.at[0 if dx == 1 else 1]
        src = ypack.at[1 if dy == 1 else 0]
        side = 0 if dy == 1 else 1
        if dx == 0:
            return src, yrecv.at[side]
        return src, crecv.at[2 * (0 if dx == 1 else 1) + side]

    def pooled_refs(dx, dy, ys=pl.ds(1, 8)):
        sx = {1: 2, -1: 1, 0: pl.ds(1, 2)}[dx]
        tx = {1: 0, -1: 3, 0: pl.ds(1, 2)}[dx]
        sy = {1: 8, -1: 1, 0: ys}[dy]
        ty = {1: 0, -1: 9, 0: ys}[dy]
        rows = pl.ds(32, 32)
        return PS.at[sx, sy, rows], PS.at[tx, ty, rows]

    middle_refs = functools.partial(pooled_refs, ys=pl.ds(2, 6))
    low_refs = functools.partial(pooled_refs, ys=1)
    high_refs = functools.partial(pooled_refs, ys=8)

    def grad_refs(dx, dy):
        src = OUTER.at[
            {1: 3, -1: 0, 0: pl.ds(1, 2)}[dx], {1: 9, -1: 0, 0: pl.ds(1, 8)}[dy]
        ]
        side_x = 0 if dx == 1 else 1
        side_y = 0 if dy == 1 else 1
        if dy == 0:
            return src, face_x.at[side_x]
        if dx == 0:
            return src, face_y.at[side_y]
        return src, corner.at[2 * side_x + side_y]

    def halo_copy(phase, k, refs):
        dx, dy = SIDES[k]
        src, dst = refs(dx, dy)
        extra = 2 * (phase - 3) + k - 4
        return pltpu.make_async_remote_copy(
            src_ref=src,
            dst_ref=dst,
            send_sem=halo_send.at[k if phase < 3 else 8 + extra],
            recv_sem=halo_recv.at[8 * (phase % 2) + k if phase < 3 else 16 + extra],
            device_id=(slab + dx, pencil + dy),
            device_id_type=MESH,
        )

    def halo_start(phase, refs, sides):
        for k in sides:

            @pl.when(exists(*SIDES[k]))
            def _():
                halo_copy(phase, k, refs).start()

    def halo_wait(phase, refs, sides):
        for k in sides:
            dx, dy = SIDES[k]

            @pl.when(exists(dx, dy))
            def _():
                halo_copy(phase, k, refs).wait_send()

            @pl.when(exists(-dx, -dy))
            def _():
                halo_copy(phase, k, refs).wait_recv()

    load_vol.wait()
    edges = pick(32, 256, lambda r, c: c == ((r & 15) << 4) + 15 * (r >> 4))
    packed = dot(edges, vol[...].reshape(256, 256)).astype(BF16)
    ypack[0] = packed[:16]
    ypack[1] = packed[16:]
    pl.semaphore_wait(barrier, arrivals)
    halo_start(0, volume_refs, ALL)

    for dx, dy in SIDES:

        @pl.when(jnp.logical_not(exists(-dx, -dy)))
        def _():
            for refs in (volume_refs, pooled_refs, grad_refs):
                target = refs(dx, dy)[1]
                target[...] = jnp.zeros(target.shape, BF16)

    shift_1 = pick(256, 512, lambda r, c: r == jnp.where(c < 256, c - 1, c - 255))

    def shifted(block):
        sides = dot(block, shift_1).astype(BF16)
        return sides[:, :256], block, sides[:, 256:]

    def order(r, c):
        slot = r & 15
        return (slot < 12) & (c == ((slot >> 2) << 6) + ((slot & 3) << 4) + (r >> 4))

    def order_edge(r, c):
        slot = r & 15
        return (slot < 12) & (c == ((slot >> 2) << 4) + ((slot & 3) << 2) + (r >> 4))

    to_rows = pick(256, 192, order)
    to_edge = pick(64, 48, order_edge)

    def rows_of(parts, lo, hi):
        return jnp.concatenate([part[lo:hi] for part in parts], axis=0)

    local = shifted(jnp.concatenate([vol[:, x].reshape(64, 256) for x in range(4)], axis=0))
    for x in range(4):
        rows = dot(to_rows, rows_of(local, 64 * x, 64 * x + 64)).astype(BF16)
        V[x + 1, 1:17] = rows.reshape(16, 16, 256)

    load_w1.wait()
    eye = pick(32, 32, lambda r, c: r == c)
    w1f = dot_lanes(eye, eight_rows(w1r[...])).astype(BF16)
    w1p = jnp.concatenate(
        [(0.5 * dot(w1f, expand_map(yo, 216, 8))).astype(BF16) for yo in range(2)], axis=0
    )

    def window(x, y1):
        return V[pl.ds(x, 3), pl.ds(2 * y1, 4)].reshape(192, 256)

    def first_cells(x, y1):
        act, slope = act_slope(dot(w1p, window(x, y1)))
        SL[x, y1] = slope
        return act

    def inner(i, carry):
        for x in (1, 2):
            for j in range(2):
                CELLS[x - 1, 1 + 2 * i + j] = first_cells(x, 1 + 2 * i + j)
        return carry

    lax.fori_loop(0, 3, inner, 0)

    pool_1[...] = pick(256, 128, lambda r, c: (r >> 1) == c)
    shift_2[...] = pick(128, 256, lambda r, c: r == jnp.where(c < 128, c - 1, c - 127))
    spread_1[...] = pick(128, 256, lambda r, c: r == (c >> 1))

    def pool_cells(cells):
        parts = split(cells.reshape(-1, 256), 2)
        pooled = 0.125 * joined(dot(parts, pool_1[...]), 2) + 0.7 * LOG_2
        return pooled.astype(BF16).reshape(-1, 32, 128)

    halo_wait(0, volume_refs, X_FACES)
    arrived = shifted(jnp.concatenate([xrecv[s].reshape(64, 256) for s in range(2)], axis=0))
    for side, x in ((0, 0), (1, 5)):
        rows = dot(to_rows, rows_of(arrived, 64 * side, 64 * side + 64)).astype(BF16)
        V[x, 1:17] = rows.reshape(16, 16, 256)

    def outer(i, carry):
        for x in (0, 3):
            for j in range(3):
                CELLS[x // 2, 1 + 3 * i + j] += first_cells(x, 1 + 3 * i + j)
        return carry

    for i in range(2):
        outer(i, 0)
    for x1 in range(2):
        PS[x1 + 1, 2:8, 32:64] = pool_cells(CELLS[x1, 1:7])
    halo_start(3, middle_refs, X_FACES)

    halo_wait(0, volume_refs, OTHERS)
    arrived = shifted(
        jnp.concatenate([yrecv[s] for s in range(2)] + [crecv[s] for s in range(4)], axis=0)
    )
    for side, y in ((0, 0), (1, 17)):
        at = 16 * side
        V[1:5, y] = dot(to_edge, rows_of(arrived, at, at + 16)).astype(BF16).reshape(4, 16, 256)
        at = 32 + 16 * side
        V[0, y] = dot(to_edge[48:], rows_of(arrived, at, at + 16)).astype(BF16)
        at = 64 + 16 * side
        V[5, y] = dot(to_edge[:16], rows_of(arrived, at, at + 16)).astype(BF16)
    ends = []
    for x1 in range(2):
        for y1 in (0, 7):
            ends.append(first_cells(2 * x1, y1) + first_cells(2 * x1 + 1, y1))
    ends = pool_cells(jnp.concatenate(ends, axis=0))
    for x1 in range(2):
        PS[x1 + 1, 1, 32:64] = ends[2 * x1]
        PS[x1 + 1, 8, 32:64] = ends[2 * x1 + 1]

    halo_start(1, pooled_refs, OTHERS)
    halo_start(1, low_refs, X_FACES)
    halo_start(4, high_refs, X_FACES)

    load_w2.wait()
    for yo in range(2):
        MAPS[yo] = expand_map(yo, 128, 4)
    eye = pick(64, 64, lambda r, c: r == c)
    for a in range(3):
        taps_a = w2r[9 * a : 9 * a + 9].reshape(288, 64)
        W2A[64 * (2 - a) : 64 * (2 - a) + 64] = (0.5 * dot_lanes(eye, taps_a)).astype(BF16)
        for b in range(3):
            at = 32 * (3 * b + a)
            taps_b = [w2r[26 - 9 * a - 3 * b - c] for c in range(3)]
            W2B[at : at + 32] = jnp.concatenate(taps_b, axis=1)
    spread_2 = pick(64, 128, lambda r, c: r == (c >> 1))
    load_cot.wait()
    to_y2 = pick(256, 512, lambda r, c: c == ((r & 63) << 3) + (r >> 6))
    seeds = dot(to_y2, eight_rows(cot[...])).astype(BF16)
    SEED[...] = (0.125 * dot(seeds, spread_2)).reshape(4, 64, 128)

    def spread_edges(xs, ys):
        cells = PS[xs, ys, 32:64]
        shape = cells.shape
        sides = dot(cells.reshape(-1, 128), shift_2[...]).astype(BF16)
        PS[xs, ys, 0:32] = sides[:, :128].reshape(shape)
        PS[xs, ys, 64:96] = sides[:, 128:].reshape(shape)

    def taps(x, y2):
        one = PS[x, pl.ds(2 * y2, 3)].reshape(288, 128)
        two = PS[x, pl.ds(2 * y2 + 1, 3)].reshape(288, 128)
        return jnp.concatenate([one, two], axis=1)

    for x1 in range(2):
        spread_edges(x1 + 1, slice(1, 9))

    def local_conv(y2):
        return dot(W2A[64:192], taps(1, y2)) + dot(W2A[0:128], taps(2, y2))

    def second_conv(y2, local):
        first = dot(W2A[128:192], taps(0, y2))
        last = dot(W2A[0:64], taps(3, y2))
        return local + jnp.concatenate([first, last], axis=0)

    for y2 in (1, 2):
        LOCAL[y2 - 1] = local_conv(y2)

    def second_block(rows):
        for y2 in rows:
            local = LOCAL[y2 - 1] if y2 in (1, 2) else local_conv(y2)
            total, slope = act_slope(second_conv(y2, local))
            TOT[y2] = total[:, :128] + total[:, 128:]
            seed = jnp.concatenate([SEED[y2]] * 2, axis=0)
            grad = (slope * jnp.concatenate([seed, seed], axis=1)).astype(BF16)
            G2[y2] = grad
            for yo in range(2):
                cells = grad[:, 128 * yo : 128 * yo + 128]
                sides = dot(cells, shift_2[...]).astype(BF16)
                y = 2 * y2 + yo
                for x1 in range(2):
                    lo, hi = 64 * x1, 64 * x1 + 64
                    GS[x1, y, 64:128] = cells[lo:hi]
                    GS[x1, y, 0:64] = sides[lo:hi, :128]
                    GS[x1, y, 128:192] = sides[lo:hi, 128:]

    def back_terms(y2):
        given = {}
        for x1 in range(2):
            cells = jnp.concatenate([GS[x1, 2 * y2], GS[x1, 2 * y2 + 1]], axis=1)
            terms = dot(W2B[...], cells)
            for b in range(3):
                for a in range(3):
                    at = 32 * (3 * b + a)
                    for yo in range(2):
                        term = terms[at : at + 32, 128 * yo : 128 * yo + 128]
                        place = (x1 + 2 - a, 2 * y2 + yo + 2 - b)
                        given[place] = given[place] + term if place in given else term
        for (x, y), term in given.items():
            met = {1: (), 2: (4, 5), 0: (2, 3), 3: (6, 7)}[y2]
            BACK[x, y] = BACK[x, y] + term if y in met else term

    def second_grad(rows):
        terms = [None] * 3
        for y2 in rows:
            for x in range(4):
                lo, hi = (0 if x < 3 else 64), (128 if x > 0 else 64)
                part = dot_lanes(G2[y2, lo:hi], taps(x, y2))
                for x1 in range(2):
                    if 0 <= x - x1 < 3:
                        piece = part[64 * x1 - lo : 64 * x1 - lo + 64]
                        old = terms[x - x1]
                        terms[x - x1] = piece if old is None else old + piece
        for a in range(3):
            dw2[rows[0], a] = terms[a]

    halo_wait(3, middle_refs, X_FACES)
    for x in (0, 3):
        spread_edges(x, slice(2, 8))
    second_block((1, 2))
    back_terms(1)
    back_terms(2)
    second_grad((1, 2))
    halo_wait(1, pooled_refs, OTHERS)
    halo_wait(1, low_refs, X_FACES)
    halo_wait(4, high_refs, X_FACES)
    for y in (0, 9):
        spread_edges(slice(0, 4), y)
    for x in (0, 3):
        for y in (1, 8):
            spread_edges(x, y)
    second_block((0, 3))
    back_terms(0)
    back_terms(3)
    for x in (0, 3):
        OUTER[x] = BACK[x].astype(BF16)
    for y in (0, 9):
        OUTER[1:3, y] = BACK[1:3, y].astype(BF16)

    halo_start(2, grad_refs, ALL)

    share = 64 // pencils
    second_grad((0, 3))
    columns = [dw2[0, a] + dw2[1, a] for a in range(3)] + [jnp.zeros((64, 256 * LOW - 864), F32)]
    columns = jnp.concatenate(columns, axis=1).astype(BF16)
    for g in range(pencils):
        for part in range(LOW):
            rows = columns[share * g : share * g + share]
            part2[g, part] = rows[:, 256 * part : 256 * part + 256]

    def wait_slots(slots, count, sem):
        taken = slots.at[pl.ds(0, count)]
        pltpu.make_async_copy(taken, taken, sem).wait()

    def group_copies(group, slots, send, recv, src_of=None):
        size, me, device = group

        def start():
            for peer in others(group):
                pltpu.make_async_remote_copy(
                    src_ref=slots.at[me] if src_of is None else src_of(peer),
                    dst_ref=slots.at[me],
                    send_sem=send,
                    recv_sem=recv,
                    device_id=device(peer),
                    device_id_type=MESH,
                ).start()

        def wait():
            for sem in (send, recv):
                wait_slots(slots, size - 1, sem)

        return start, wait

    def part_of(i):
        return part2.at[wrap(i, pencils), over(i, pencils)]

    start_a, wait_a = group_copies(group_z, sum_a, sem_a.at[0], sem_a.at[1], part_of)
    start_b, wait_b = group_copies(group_xy, sum_b, sem_a.at[0], sem_b.at[0])
    start_c, wait_c = group_copies(group_low, sum_c, sem_a.at[0], sem_c.at[0])
    start_z, wait_z = group_copies(group_z, sum_1.at[0], sem_1.at[0], sem_1.at[1])
    start_xy, wait_xy = group_copies(group_xy, sum_1.at[1], sem_1.at[0], sem_1.at[2])

    def total_of(slots, size):
        total = slots[0].astype(F32)
        for i in range(1, size):
            total = total + slots[i].astype(F32)
        return total

    start_a()

    pool_2 = pick(128, 64, lambda r, c: (r >> 1) == c)
    pooled = 0.125 * joined(dot(split(TOT[...].reshape(256, 128), 2), pool_2), 2) + 0.7 * LOG_2
    from_y2 = pick(512, 256, lambda r, c: r == ((c & 63) << 3) + (c >> 6))
    pooled = dot(from_y2, pooled.astype(BF16)).reshape(64, 8, 64)
    p2_out[...] = pooled[:, :4].astype(BF16)

    def spread_back(back):
        cells = split(back.reshape(-1, 128), 2)
        return (0.125 * joined(dot(cells, spread_1[...]), 2)).reshape(-1, 32, 256)

    def first_grad(y1, seeds):
        total = None
        for x in range(4):
            seed = jnp.concatenate([seeds[x // 2]] * 2, axis=0)
            term = dot_lanes((SL[x, y1] * seed).astype(BF16), window(x, y1))
            total = term if total is None else total + term
        return total

    halo_wait(2, grad_refs, X_FACES)
    for x1 in range(2):
        CELLS[x1] = spread_back(BACK[x1 + 1, 1:9] + face_x[x1].astype(F32))
    dw1[...] = jnp.zeros_like(dw1)

    def middle(i, carry):
        total = None
        for j in range(3):
            y1 = 1 + 3 * i + j
            term = first_grad(y1, (CELLS[0, y1], CELLS[1, y1]))
            total = term if total is None else total + term
        dw1[...] += total
        return carry

    for i in range(2):
        middle(i, 0)

    halo_wait(2, grad_refs, OTHERS)
    for side, y1 in ((0, 0), (1, 7)):
        back = []
        for x1 in range(2):
            own = BACK[x1 + 1, y1 + 1] + face_x[x1, y1].astype(F32)
            back.append(own + face_y[side, x1].astype(F32) + corner[2 * x1 + side].astype(F32))
        seeds = spread_back(jnp.concatenate(back, axis=0))
        dw1[...] += first_grad(y1, (seeds[0], seeds[1]))

    folded = None
    for yo in range(2):
        term = joined(dot_lanes(split(dw1[32 * yo : 32 * yo + 32], 3), MAPS[yo]), 3)
        folded = term if folded is None else folded + term

    sum_1[0, group_z[1]] = folded.astype(BF16)
    start_z()
    wait_a()
    sum_a[group_z[1]] = part2[pencil, low]
    sum_b[group_xy[1]] = total_of(sum_a, group_z[0]).astype(BF16)
    start_b()
    wait_z()
    sum_1[1, group_xy[1]] = total_of(sum_1.at[0], group_z[0]).astype(BF16)
    start_xy()
    wait_b()
    sum_c[low] = total_of(sum_b, group_xy[0]).astype(BF16)
    start_c()
    wait_xy()
    total = total_of(sum_1.at[1], group_xy[0]).T
    for tap in range(27):
        g1_out[tap] = total[4 * tap : 4 * tap + 4]
    wait_c()
    totals = [sum_c[i].astype(F32) for i in range(LOW)]
    for tap in range(27):
        at = 32 * (tap % 8)
        g2_out[tap] = totals[tap // 8][:, at : at + 32]


def write_out(*refs):
    count = len(refs) // 2
    sems = refs[-1]
    copies = [pltpu.make_async_copy(refs[i], refs[count + i], sems.at[i]) for i in range(count)]
    for copy in copies:
        copy.start()
    for copy in copies:
        copy.wait()


def solution(mesh):
    pencils = mesh.shape["pencil"]
    share = 64 // pencils
    size_z = LOW * pencils
    size_xy = mesh.shape["slab"] // LOW
    most = max(size_z, size_xy)

    def per_device(volume, weight_one, weight_two, cotangent):
        w1 = weight_one.transpose(1, 2, 0)
        w2 = weight_two.transpose(1, 2, 0)
        cot = cotangent.reshape(64, 4, 64)
        vmem = pl.BlockSpec(memory_space=pltpu.VMEM)
        hbm = pl.BlockSpec(memory_space=pltpu.HBM)
        shapes = (
            pltpu.VMEM((64, 4, 64), BF16),
            pltpu.VMEM((27, 4, 32), F32),
            pltpu.VMEM((27, share, 32), F32),
        )
        results = pl.pallas_call(
            kernel,
            out_shape=shapes,
            in_specs=[hbm] * 4,
            out_specs=(vmem,) * 3,
            scratch_shapes=[
                pltpu.VMEM((4, 4, 16, 256), BF16),
                pltpu.VMEM((27, 4, 32), BF16),
                pltpu.VMEM((27, 32, 64), BF16),
                pltpu.VMEM((64, 4, 64), BF16),
                pltpu.VMEM((6, 18, 16, 256), BF16),
                pltpu.VMEM((4, 10, 96, 128), BF16),
                pltpu.VMEM((2, 8, 192, 128), BF16),
                pltpu.VMEM((4, 8, 64, 256), F32),
                pltpu.VMEM((2, 8, 32, 256), F32),
                pltpu.VMEM((4, 64, 128), F32),
                pltpu.VMEM((4, 64, 128), F32),
                pltpu.VMEM((4, 128, 256), BF16),
                pltpu.VMEM((2, 128, 256), F32),
                pltpu.VMEM((4, 10, 32, 128), F32),
                pltpu.VMEM((4, 10, 32, 128), BF16),
                pltpu.VMEM((2, 8, 32, 128), BF16),
                pltpu.VMEM((2, 2, 32, 128), BF16),
                pltpu.VMEM((4, 32, 128), BF16),
                pltpu.VMEM((192, 288), BF16),
                pltpu.VMEM((288, 192), BF16),
                pltpu.VMEM((2, 128, 192), BF16),
                pltpu.VMEM((256, 128), BF16),
                pltpu.VMEM((128, 256), BF16),
                pltpu.VMEM((128, 256), BF16),
                pltpu.VMEM((2, 16, 256), BF16),
                pltpu.VMEM((2, 4, 16, 256), BF16),
                pltpu.VMEM((2, 16, 256), BF16),
                pltpu.VMEM((4, 16, 256), BF16),
                pltpu.VMEM((64, 192), F32),
                pltpu.VMEM((2, 3, 64, 288), F32),
                pltpu.VMEM((pencils, LOW, share, 256), BF16),
                pltpu.VMEM((size_z, share, 256), BF16),
                pltpu.VMEM((size_xy, share, 256), BF16),
                pltpu.VMEM((LOW, share, 256), BF16),
                pltpu.VMEM((2, most, 32, 128), BF16),
                pltpu.SemaphoreType.DMA((4,)),
                pltpu.SemaphoreType.DMA((12,)),
                pltpu.SemaphoreType.DMA((20,)),
                pltpu.SemaphoreType.DMA((2,)),
                pltpu.SemaphoreType.DMA((1,)),
                pltpu.SemaphoreType.DMA((1,)),
                pltpu.SemaphoreType.DMA((3,)),
            ],
            compiler_params=pltpu.CompilerParams(
                collective_id=0, has_side_effects=True, vmem_limit_bytes=56 * 2**20
            ),
        )(volume, w1, w2, cot)
        pooled, grad_one, grad_two = pl.pallas_call(
            write_out,
            out_shape=tuple(jax.ShapeDtypeStruct(s.shape, s.dtype) for s in shapes),
            in_specs=[vmem] * 3,
            out_specs=(hbm,) * 3,
            scratch_shapes=[pltpu.SemaphoreType.DMA((3,))],
            compiler_params=pltpu.CompilerParams(vmem_limit_bytes=4 * 2**20),
        )(*results)
        return (
            pooled.reshape(64, 1, 4, 64),
            grad_one.transpose(2, 0, 1),
            grad_two.transpose(1, 0, 2),
        )

    in_specs = (P(None, "slab", "pencil", None), P(), P(), P(None, "slab", "pencil", None))
    out_specs = (P(None, "slab", "pencil", None), P(), P("pencil", None, None))
    return jax.shard_map(
        per_device, mesh=mesh, in_specs=in_specs, out_specs=out_specs, check_vma=False
    )
```
